32 devices in a mesh: rep: 4 (over x, core), shard: 8 (over z, y).
Axes of the slice: x: 2, y: 2, z: 4, core: 2. Of those that a mesh axis runs over, the one named last changes fastest.
Arguments:
- tokens: bfloat16 [16384, 768], P(('rep', 'shard')), may hold values from -6 to 6
- w_qkv: bfloat16 [768, 2304], P('shard'), may hold values from -0.21875 to 0.21875
- w_out: bfloat16 [768, 768], P('shard'), may hold values from -1.75 to 1.75
- w_up: bfloat16 [768, 3072], P('shard'), may hold values from -0.21875 to 0.21875
- w_down: bfloat16 [3072, 768], P('shard'), may hold values from -0.109375 to 0.109375
- gain_attn: bfloat16 [768], P('shard'), may hold values from 0.099609375 to 1.8984375
- gain_mlp: bfloat16 [768], P('shard'), may hold values from 0.099609375 to 1.8984375
- d_out: bfloat16 [16384, 768], P(('rep', 'shard')), may hold values from -6 to 6
Outputs:
- block_out: bfloat16 [16384, 768], P(('rep', 'shard'))
- d_tokens: float32 [16384, 768], P(('rep', 'shard'))
- d_w_qkv: float32 [768, 2304], P('shard')
- d_w_out: float32 [768, 768], P('shard')
- d_w_up: float32 [768, 3072], P('shard')
- d_w_down: float32 [3072, 768], P('shard')
- d_gain_attn: float32 [768], P('shard')
- d_gain_mlp: float32 [768], P('shard')
The draws below stay inside these ranges and needn't reach their ends.
All inputs are finite; a program needn't handle non-finite values.
Results may differ from the reference program's by a relative error of at most 0.015.
Values may be sent and summed in bfloat16 or wider, within the bound.
No kernel may reach another device: no remote copies, remote signals or barrier semaphores. Data moves between devices by JAX's collectives and lax.ppermute only.
A program may use at most 256 MiB of HBM per device.

```python
import jax
import jax.numpy as jnp
from jax import lax

D = 768
HEADS = 12
HDIM = 64
FF = 3072
GROUPS_DEV = 2
PLEN = 1024
CLEN = 128
CONTS = 8
PR_DEV = 128
TOK_DEV = 512
TOKENS = 16384


def block_levels(key, dims, split, least, top_value):
    gain, own = 1.0, jax.random.fold_in(key, 6)
    for axis_at, parts in split:
        steps = jnp.exp(jax.random.uniform(jax.random.fold_in(own, axis_at), (parts,), jnp.float32, least / len(split), top_value / len(split)))
        gain = gain * jnp.repeat(steps, dims[axis_at] // parts).reshape([-1 if axis == axis_at else 1 for axis in range(len(dims))])
    return gain


def centred(own_key, dims, scale, bound, shards=(), held_as=jnp.bfloat16):
    entries = jax.random.normal(own_key, dims, jnp.float32) * scale
    if len(shards) > 0:
        entries = block_levels(own_key, dims, shards, -0.22, 0.18) * entries
    return jnp.clip(entries, min=-bound, max=bound).astype(held_as)


def setup_inputs(seed: int = 0) -> dict:
    keys = jax.random.split(jax.random.key(seed), 9)
    tokens = centred(keys[0], (TOKENS, D), 1.0, 6.0, ((0, 32),))
    w_qkv = centred(keys[1], (D, 3 * D), D ** -0.5, 0.21875, ((0, 8),))
    w_out = centred(keys[2], (D, D), (max(D // 64, 1)) ** -0.5, 1.75, ((0, 8),))
    w_up = centred(keys[3], (D, FF), D ** -0.5, 0.21875, ((0, 8),))
    w_down = centred(keys[4], (FF, D), FF ** -0.5, 0.109375, ((0, 8),))
    gain_attn = jnp.clip(1.0 + 0.18 * jax.random.normal(keys[5], (D,), jnp.float32), 0.099609375, 1.8984375).astype(jnp.bfloat16)
    gain_mlp = jnp.clip(1.0 + 0.18 * jax.random.normal(keys[6], (D,), jnp.float32), 0.099609375, 1.8984375).astype(jnp.bfloat16)
    d_out = centred(keys[7], (TOKENS, D), 1.0, 6.0, ((0, 32),))
    return {"tokens": tokens, "w_qkv": w_qkv, "w_out": w_out, "w_up": w_up, "w_down": w_down, "gain_attn": gain_attn, "gain_mlp": gain_mlp, "d_out": d_out}


@jax.custom_vjp
def low(v):
    return lax.optimization_barrier(v.astype(jnp.bfloat16)).astype(jnp.float32)

@jax.custom_vjp
def low_back(v):
    return v

def low_keep(v):
    return (low(v), None)

def low_pass(kept, grad):
    return (grad,)

def back_keep(v):
    return (v, None)

def back_low(kept, grad):
    return (low(grad),)
low.defvjp(low_keep, low_pass)
low_back.defvjp(back_keep, back_low)
norm_eps = 1e-05
neg_fill = -1e+30

def matmul_hi(left_mat, right_mat):
    return jnp.dot(left_mat, right_mat, precision=lax.Precision.HIGHEST)

def rms_scale(values, gain_vec):
    return values * lax.rsqrt(lax.optimization_barrier(jnp.mean(values * values, axis=-1, keepdims=True)) + norm_eps) * gain_vec

def group_attention(pieces):
    q_prompt, k_prompt, v_prompt, q_cont, k_cont, v_cont = pieces
    score_scale = HDIM ** (-0.5)
    highest = lax.Precision.HIGHEST
    scores = low_back(jnp.einsum('qhd,khd->hqk', q_prompt, k_prompt, precision=highest) * score_scale)
    row_ids = lax.broadcasted_iota(jnp.int32, (PLEN, PLEN), 0)
    col_ids = lax.broadcasted_iota(jnp.int32, (PLEN, PLEN), 1)
    scores = jnp.where(col_ids <= row_ids, scores, neg_fill)
    weights = low(jax.nn.softmax(scores, axis=-1))
    out_prompt = jnp.einsum('hqk,khd->qhd', weights, v_prompt, precision=highest)
    from_prompt = jnp.einsum('cqhd,khd->chqk', q_cont, k_prompt, precision=highest)
    from_own = jnp.einsum('cqhd,ckhd->chqk', q_cont, k_cont, precision=highest)
    scores_c = low_back(jnp.concatenate([from_prompt, from_own], axis=-1) * score_scale)
    row_c = lax.broadcasted_iota(jnp.int32, (CLEN, PLEN + CLEN), 0)
    col_c = lax.broadcasted_iota(jnp.int32, (CLEN, PLEN + CLEN), 1)
    scores_c = jnp.where((col_c < PLEN) | (col_c - PLEN <= row_c), scores_c, neg_fill)
    weights_c = low(jax.nn.softmax(scores_c, axis=-1))
    out_cont = jnp.einsum('chqk,khd->cqhd', weights_c[..., :PLEN], v_prompt, precision=highest)
    out_cont = out_cont + jnp.einsum('chqk,ckhd->cqhd', weights_c[..., PLEN:], v_cont, precision=highest)
    return (out_prompt, out_cont)

def block_forward(token_rows, w_qkv, w_out, w_up, w_down, gain_attn, gain_mlp):
    prompt_rows = GROUPS_DEV * PR_DEV
    normed = low(rms_scale(token_rows, gain_attn))
    qkv_all = low(low_back(matmul_hi(normed, w_qkv)))
    per_device = qkv_all.reshape(CONTS, TOK_DEV, 3, HEADS, HDIM)
    prompt = per_device[:, :prompt_rows].reshape(CONTS, GROUPS_DEV, PR_DEV, 3, HEADS, HDIM)
    prompt = prompt.transpose(1, 0, 2, 3, 4, 5).reshape(GROUPS_DEV, PLEN, 3, HEADS, HDIM)
    cont_part = per_device[:, prompt_rows:].reshape(CONTS, GROUPS_DEV, CLEN, 3, HEADS, HDIM)
    cont_part = cont_part.transpose(1, 0, 2, 3, 4, 5)
    pieces = (prompt[:, :, 0], prompt[:, :, 1], prompt[:, :, 2], cont_part[:, :, :, 0], cont_part[:, :, :, 1], cont_part[:, :, :, 2])
    out_prompt, out_cont = lax.map(jax.checkpoint(group_attention), pieces)
    out_prompt = out_prompt.reshape(GROUPS_DEV, CONTS, PR_DEV, D).transpose(1, 0, 2, 3)
    out_prompt = out_prompt.reshape(CONTS, prompt_rows, D)
    out_cont = out_cont.reshape(GROUPS_DEV, CONTS, CLEN, D).transpose(1, 0, 2, 3)
    out_cont = out_cont.reshape(CONTS, GROUPS_DEV * CLEN, D)
    attended = jnp.concatenate([out_prompt, out_cont], axis=1).reshape(CONTS * TOK_DEV, D)
    attended = low(low_back(attended))
    middle = token_rows + low_back(matmul_hi(attended, w_out))
    normed_mlp = low(rms_scale(middle, gain_mlp))
    hidden = low_back(matmul_hi(normed_mlp, w_up))
    active = low(jax.nn.gelu(hidden, approximate=True))
    return middle + matmul_hi(active, w_down)

def reference(tokens, w_qkv, w_out, w_up, w_down, gain_attn, gain_mlp, d_out):

    def forward(token_rows, wq_full, wo_full, wu_full, wd_full, ga_full, gm_full):

        def one_block(block_rows):
            return block_forward(block_rows, wq_full, wo_full, wu_full, wd_full, ga_full, gm_full)
        blocks = token_rows.reshape(TOKENS // (CONTS * TOK_DEV), CONTS * TOK_DEV, D)
        return lax.map(jax.checkpoint(one_block), blocks).reshape(TOKENS, D)
    primals = tuple((array_in.astype(jnp.float32) for array_in in (tokens, w_qkv, w_out, w_up, w_down, gain_attn, gain_mlp)))
    block_out, pullback = jax.vjp(forward, *primals)
    gradients = pullback(d_out.astype(jnp.float32))
    return (block_out.astype(jnp.bfloat16), gradients[0], gradients[1], gradients[2], gradients[3], gradients[4], gradients[5], gradients[6])
```

```python
import functools

import jax
import jax.numpy as jnp
from jax import lax
from jax.experimental import pallas as pl
from jax.experimental.pallas import tpu as pltpu
from jax.sharding import PartitionSpec as P

D = 768
HEADS = 12
HDIM = 64
FF = 3072
PR = 128
PLEN = 1024
KEYS = PLEN + 2 * PR
ROWS = 4 * PR
PAIRS = HEADS // 2
FCHUNK = 512
norm_eps = 1e-05
neg_fill = -1e30
SCALE = HDIM ** (-0.5)
GELU_C = 0.7978845608028654
GELU_A = 0.044715
BF = jnp.bfloat16
F32 = jnp.float32
VMEM_LIMIT = 60 * 1024 * 1024


def dot_nt(a, b):
    return lax.dot_general(a, b, (((1,), (1,)), ((), ())), preferred_element_type=F32)


def dot_tn(a, b):
    return lax.dot_general(a, b, (((0,), (0,)), ((), ())), preferred_element_type=F32)


def dot_nn(a, b):
    return jnp.dot(a, b, preferred_element_type=F32)


def rms_inv(values):
    return lax.rsqrt(jnp.mean(values * values, axis=-1, keepdims=True) + norm_eps)


def fill_normed(x_ref, gain_ref, normed_ref):
    gain = gain_ref[...]

    @pl.loop(0, KEYS, step=PR)
    def _(row):
        rows = pl.ds(pl.multiple_of(row, PR), PR)
        part = x_ref[rows, :].astype(F32)
        normed_ref[rows, :] = (part * rms_inv(part) * gain).astype(BF)


def lane_half(head):
    lanes = lax.broadcasted_iota(jnp.int32, (1, 2 * HDIM), 1)
    return (lanes >= HDIM) if head else (lanes < HDIM)


def attn_fwd_kernel(
    pos_ref, x_ref, gain_ref, wq_ref, wk_ref, wv_ref,
    q_ref, k_ref, v_ref, e_ref, ec_ref, o_ref, r_ref,
    normed_ref, bias_ref,
):
    @pl.when(pl.program_id(0) == 0)
    def _():
        fill_normed(x_ref, gain_ref, normed_ref)
        pos = pos_ref[0]
        row = lax.broadcasted_iota(jnp.int32, (PR, PR), 0)
        col = lax.broadcasted_iota(jnp.int32, (PR, PR), 1)
        tri = jnp.where(col <= row, 0.0, neg_fill)
        for part in range(2):
            mine = jnp.bitwise_xor(pos, part)
            for block in range(8):
                at = (pl.ds(part * PR, PR), pl.ds(block * PR, PR))
                if block == part:
                    bias_ref[at] = tri
                else:
                    seen = jnp.bitwise_xor(pos, block) < mine
                    bias_ref[at] = jnp.full((PR, PR), jnp.where(seen, 0.0, neg_fill), F32)

    keys = dot_nn(normed_ref[...], wk_ref[...]).astype(BF)
    values = dot_nn(normed_ref[...], wv_ref[...]).astype(BF)
    k_ref[...] = keys
    v_ref[...] = values
    wq = wq_ref[...]
    q_ref[0 : 2 * PR, :] = (dot_nn(normed_ref[0 : 2 * PR, :], wq) * SCALE).astype(BF)
    q_ref[2 * PR :, :] = (dot_nn(normed_ref[PLEN:, :], wq) * SCALE).astype(BF)
    row = lax.broadcasted_iota(jnp.int32, (PR, PR), 0)
    col = lax.broadcasted_iota(jnp.int32, (PR, PR), 1)
    tri = jnp.where(col <= row, 0.0, neg_fill)
    for chunk in range(4):
        rows = slice(chunk * PR, (chunk + 1) * PR)
        query = q_ref[rows, :]
        outs, invs = [], []
        for head in range(2):
            masked = jnp.where(lane_half(head), query, jnp.zeros_like(query))
            scores = dot_nt(masked, k_ref[0:PLEN, :])
            if chunk < 2:
                scores = scores + bias_ref[rows, :]
                top = jnp.max(scores, axis=-1, keepdims=True)
                terms = jnp.exp(scores - top)
                total = jnp.sum(terms, axis=-1, keepdims=True)
                low_terms = terms.astype(BF)
                e_ref[head, rows, :] = low_terms
                out = dot_nn(low_terms, v_ref[0:PLEN, :])
            else:
                own = slice(PLEN + (chunk - 2) * PR, PLEN + (chunk - 1) * PR)
                near = dot_nt(masked, k_ref[own, :]) + tri
                top = jnp.maximum(
                    jnp.max(scores, axis=-1, keepdims=True), jnp.max(near, axis=-1, keepdims=True)
                )
                terms = jnp.exp(scores - top)
                near_terms = jnp.exp(near - top)
                total = jnp.sum(terms, axis=-1, keepdims=True) + jnp.sum(
                    near_terms, axis=-1, keepdims=True
                )
                low_terms = terms.astype(BF)
                low_near = near_terms.astype(BF)
                e_ref[head, rows, :] = low_terms
                ec_ref[head, (chunk - 2) * PR : (chunk - 1) * PR, :] = low_near
                out = dot_nn(low_terms, v_ref[0:PLEN, :]) + dot_nn(low_near, v_ref[own, :])
            inv = 1.0 / total
            outs.append(out * inv)
            invs.append(jnp.broadcast_to(inv, (PR, 2 * HDIM)))
        low_half = lane_half(0)
        o_ref[rows, :] = jnp.where(low_half, outs[0], outs[1]).astype(BF)
        r_ref[rows, :] = jnp.where(low_half, invs[0], invs[1])


def attn_fwd(pos, x_all, gain, w_qkv):
    pair = lambda n: (lambda i: (0, n * PAIRS + i))
    whole = lambda i: (0, 0)
    heads = lambda i: (i, 0, 0)
    width = 2 * HDIM
    return pl.pallas_call(
        attn_fwd_kernel,
        grid=(PAIRS,),
        in_specs=[
            pl.BlockSpec(memory_space=pltpu.SMEM),
            pl.BlockSpec((KEYS, D), whole),
            pl.BlockSpec((1, D), whole),
            pl.BlockSpec((D, width), pair(0)),
            pl.BlockSpec((D, width), pair(1)),
            pl.BlockSpec((D, width), pair(2)),
        ],
        out_specs=[
            pl.BlockSpec((ROWS, width), pair(0)),
            pl.BlockSpec((KEYS, width), pair(0)),
            pl.BlockSpec((KEYS, width), pair(0)),
            pl.BlockSpec((2, ROWS, PLEN), heads),
            pl.BlockSpec((2, 2 * PR, PR), heads),
            pl.BlockSpec((ROWS, width), pair(0)),
            pl.BlockSpec((ROWS, width), pair(0)),
        ],
        out_shape=[
            jax.ShapeDtypeStruct((ROWS, D), BF),
            jax.ShapeDtypeStruct((KEYS, D), BF),
            jax.ShapeDtypeStruct((KEYS, D), BF),
            jax.ShapeDtypeStruct((HEADS, ROWS, PLEN), BF),
            jax.ShapeDtypeStruct((HEADS, 2 * PR, PR), BF),
            jax.ShapeDtypeStruct((ROWS, D), BF),
            jax.ShapeDtypeStruct((ROWS, D), F32),
        ],
        scratch_shapes=[pltpu.VMEM((KEYS, D), BF), pltpu.VMEM((2 * PR, PLEN), F32)],
        compiler_params=pltpu.CompilerParams(vmem_limit_bytes=VMEM_LIMIT),
        cost_estimate=pl.CostEstimate(
            flops=20_000_000_000, bytes_accessed=25_000_000, transcendentals=6_300_000
        ),
    )(pos, x_all, gain, w_qkv, w_qkv, w_qkv)


def mlp_kernel(
    x_ref, att_ref, dout_ref, gain_ref, wout_ref, wup_ref, wdown_ref,
    out_ref, dmid_ref, datt_ref, dwout_ref, dwup_ref, dwdown_ref, dgain_ref,
    mid_ref, nm_ref, acc_ref, e_ref,
):
    step = pl.program_id(0)

    @pl.when(step == 0)
    def _():
        wout = wout_ref[...]
        gain = gain_ref[...]
        for chunk in range(4):
            rows = slice(chunk * PR, (chunk + 1) * PR)
            middle = x_ref[rows, :].astype(F32) + dot_nn(att_ref[rows, :], wout)
            mid_ref[rows, :] = middle
            nm_ref[rows, :] = (middle * rms_inv(middle) * gain).astype(BF)

    wup = wup_ref[...]
    wdown = wdown_ref[...]
    dout = dout_ref[...]
    hidden = dot_nn(nm_ref[...], wup)
    inner = GELU_C * (hidden + GELU_A * hidden * hidden * hidden)
    th = jnp.tanh(inner)
    active = (0.5 * hidden * (1.0 + th)).astype(BF)
    d_active = dot_nt(dout, wdown)
    slope = 0.5 * (1.0 + th) + 0.5 * hidden * (1.0 - th * th) * (
        GELU_C * (1.0 + 3.0 * GELU_A * hidden * hidden)
    )
    d_hidden = (d_active * slope).astype(BF)
    part_out = dot_nn(active, wdown)
    part_e = dot_nt(d_hidden, wup)

    @pl.when(step == 0)
    def _():
        acc_ref[...] = part_out
        e_ref[...] = part_e

    @pl.when(step > 0)
    def _():
        acc_ref[...] += part_out
        e_ref[...] += part_e

    dwdown_ref[...] = dot_tn(active, dout).astype(BF)
    dwup_ref[...] = dot_tn(nm_ref[...], d_hidden).astype(BF)

    @pl.when(step == pl.num_programs(0) - 1)
    def _():
        gain = gain_ref[...]
        wout = wout_ref[...]
        dgain = jnp.zeros((1, D), F32)
        for chunk in range(4):
            rows = slice(chunk * PR, (chunk + 1) * PR)
            middle = mid_ref[rows, :]
            out_ref[rows, :] = (middle + acc_ref[rows, :]).astype(BF)
            inv = rms_inv(middle)
            unit = middle * inv
            grad = e_ref[rows, :]
            scaled = gain * grad
            mean = jnp.mean(unit * scaled, axis=-1, keepdims=True)
            d_mid = dout_ref[rows, :].astype(F32) + inv * (scaled - unit * mean)
            dmid_ref[rows, :] = d_mid
            dgain = dgain + jnp.sum(grad * unit, axis=0, keepdims=True)
            branch = d_mid.astype(BF)
            nm_ref[rows, :] = branch
            datt_ref[rows, :] = dot_nt(branch, wout).astype(BF)
        dgain_ref[...] = dgain
        dwout_ref[...] = dot_tn(att_ref[...], nm_ref[...]).astype(BF)


def mlp(x_own, attended, d_out, gain, w_out, w_up, w_down):
    whole = lambda i: (0, 0)
    cols = lambda i: (0, i)
    down = lambda i: (i, 0)
    return pl.pallas_call(
        mlp_kernel,
        grid=(FF // FCHUNK,),
        in_specs=[
            pl.BlockSpec((ROWS, D), whole),
            pl.BlockSpec((ROWS, D), whole),
            pl.BlockSpec((ROWS, D), whole),
            pl.BlockSpec((1, D), whole),
            pl.BlockSpec((D, D), whole),
            pl.BlockSpec((D, FCHUNK), cols),
            pl.BlockSpec((FCHUNK, D), down),
        ],
        out_specs=[
            pl.BlockSpec((ROWS, D), whole),
            pl.BlockSpec((ROWS, D), whole),
            pl.BlockSpec((ROWS, D), whole),
            pl.BlockSpec((D, D), whole),
            pl.BlockSpec((D, FCHUNK), cols),
            pl.BlockSpec((FCHUNK, D), down),
            pl.BlockSpec((1, D), whole),
        ],
        out_shape=[
            jax.ShapeDtypeStruct((ROWS, D), BF),
            jax.ShapeDtypeStruct((ROWS, D), F32),
            jax.ShapeDtypeStruct((ROWS, D), BF),
            jax.ShapeDtypeStruct((D, D), BF),
            jax.ShapeDtypeStruct((D, FF), BF),
            jax.ShapeDtypeStruct((FF, D), BF),
            jax.ShapeDtypeStruct((1, D), F32),
        ],
        scratch_shapes=[
            pltpu.VMEM((ROWS, D), F32),
            pltpu.VMEM((ROWS, D), BF),
            pltpu.VMEM((ROWS, D), F32),
            pltpu.VMEM((ROWS, D), F32),
        ],
        compiler_params=pltpu.CompilerParams(vmem_limit_bytes=VMEM_LIMIT),
        cost_estimate=pl.CostEstimate(
            flops=17_000_000_000, bytes_accessed=27_000_000, transcendentals=1_600_000
        ),
    )(x_own, attended, d_out, gain, w_out, w_up, w_down)


def attn_bwd_kernel(
    x_ref, gain_ref, wq_ref, wk_ref, wv_ref, q_ref, k_ref, v_ref, e_ref, ec_ref, o_ref, r_ref,
    g_ref, dwq_ref, dwk_ref, dwv_ref, f_ref, dgain_ref,
    normed_ref, qs_ref, gs_ref, ds_ref, dk_ref, dv_ref, dq_ref,
):
    step = pl.program_id(0)

    @pl.when(step == 0)
    def _():
        fill_normed(x_ref, gain_ref, normed_ref)

    scaled_grad = g_ref[...].astype(F32) * r_ref[...]
    prod = scaled_grad * o_ref[...].astype(F32)
    low_grad = scaled_grad.astype(BF)
    query = q_ref[...]
    dq_parts = []
    for head in range(2):
        half = lane_half(head)
        grad_h = jnp.where(half, low_grad, jnp.zeros_like(low_grad))
        query_h = jnp.where(half, query, jnp.zeros_like(query))
        delta = jnp.sum(jnp.where(half, prod, 0.0), axis=-1, keepdims=True)
        gs_ref[...] = grad_h
        qs_ref[...] = query_h
        for chunk in range(4):
            rows = slice(chunk * PR, (chunk + 1) * PR)
            d_soft = dot_nt(gs_ref[rows, :], v_ref[0:PLEN, :])
            ds_ref[rows, :] = (
                e_ref[head, rows, :].astype(F32) * (d_soft - delta[rows])
            ).astype(BF)
        d_query = dot_nn(ds_ref[...], k_ref[0:PLEN, :])
        d_key = dot_tn(ds_ref[...], qs_ref[...])
        d_value = dot_tn(e_ref[head], gs_ref[...])
        near_q, near_k, near_v = [], [], []
        for part in range(2):
            own = slice(PLEN + part * PR, PLEN + (part + 1) * PR)
            mine = slice((2 + part) * PR, (3 + part) * PR)
            near = ec_ref[head, part * PR : (part + 1) * PR, :]
            d_soft = dot_nt(gs_ref[mine, :], v_ref[own, :])
            d_near = (near.astype(F32) * (d_soft - delta[mine])).astype(BF)
            near_q.append(dot_nn(d_near, k_ref[own, :]))
            near_k.append(dot_tn(d_near, qs_ref[mine, :]))
            near_v.append(dot_tn(near, gs_ref[mine, :]))
        dq_parts.append((d_query, near_q))
        if head == 0:
            dk_ref[0:PLEN, :] = d_key
            dv_ref[0:PLEN, :] = d_value
            for part in range(2):
                own = slice(PLEN + part * PR, PLEN + (part + 1) * PR)
                dk_ref[own, :] = near_k[part]
                dv_ref[own, :] = near_v[part]
        else:
            dk_ref[0:PLEN, :] += d_key
            dv_ref[0:PLEN, :] += d_value
            for part in range(2):
                own = slice(PLEN + part * PR, PLEN + (part + 1) * PR)
                dk_ref[own, :] += near_k[part]
                dv_ref[own, :] += near_v[part]
    low_half = lane_half(0)
    dq_ref[0 : 2 * PR, :] = (
        jnp.where(low_half, dq_parts[0][0][0 : 2 * PR], dq_parts[1][0][0 : 2 * PR]) * SCALE
    ).astype(BF)
    for part in range(2):
        mine = slice((2 + part) * PR, (3 + part) * PR)
        both = [dq_parts[h][0][mine] + dq_parts[h][1][part] for h in range(2)]
        dq_ref[mine, :] = (jnp.where(low_half, both[0], both[1]) * SCALE).astype(BF)
    d_key = dk_ref[...].astype(BF)
    d_value = dv_ref[...].astype(BF)
    d_query = dq_ref[...]
    dwk_ref[...] = dot_tn(normed_ref[...], d_key).astype(BF)
    dwv_ref[...] = dot_tn(normed_ref[...], d_value).astype(BF)
    dwq_ref[...] = (
        dot_tn(normed_ref[0 : 2 * PR, :], d_query[0 : 2 * PR])
        + dot_tn(normed_ref[PLEN:, :], d_query[2 * PR :])
    ).astype(BF)
    part_kv = dot_nt(d_key, wk_ref[...]) + dot_nt(d_value, wv_ref[...])
    part_q = dot_nt(d_query, wq_ref[...])

    @pl.when(step == 0)
    def _():
        f_ref[...] = part_kv

    @pl.when(step > 0)
    def _():
        f_ref[...] += part_kv

    f_ref[0 : 2 * PR, :] += part_q[0 : 2 * PR]
    f_ref[PLEN:, :] += part_q[2 * PR :]

    @pl.when(step == pl.num_programs(0) - 1)
    def _():
        total = jnp.zeros((1, D), F32)
        for block in range(KEYS // PR):
            rows = slice(block * PR, (block + 1) * PR)
            part = x_ref[rows, :].astype(F32)
            total = total + jnp.sum(f_ref[rows, :] * (part * rms_inv(part)), axis=0, keepdims=True)
        dgain_ref[...] = total


def attn_bwd(x_all, gain, w_qkv, saved, d_att):
    pair = lambda n: (lambda i: (0, n * PAIRS + i))
    whole = lambda i: (0, 0)
    heads = lambda i: (i, 0, 0)
    width = 2 * HDIM
    q, k, v, e, ec, o, r = saved
    return pl.pallas_call(
        attn_bwd_kernel,
        grid=(PAIRS,),
        in_specs=[
            pl.BlockSpec((KEYS, D), whole),
            pl.BlockSpec((1, D), whole),
            pl.BlockSpec((D, width), pair(0)),
            pl.BlockSpec((D, width), pair(1)),
            pl.BlockSpec((D, width), pair(2)),
            pl.BlockSpec((ROWS, width), pair(0)),
            pl.BlockSpec((KEYS, width), pair(0)),
            pl.BlockSpec((KEYS, width), pair(0)),
            pl.BlockSpec((2, ROWS, PLEN), heads),
            pl.BlockSpec((2, 2 * PR, PR), heads),
            pl.BlockSpec((ROWS, width), pair(0)),
            pl.BlockSpec((ROWS, width), pair(0)),
            pl.BlockSpec((ROWS, width), pair(0)),
        ],
        out_specs=[
            pl.BlockSpec((D, width), pair(0)),
            pl.BlockSpec((D, width), pair(0)),
            pl.BlockSpec((D, width), pair(0)),
            pl.BlockSpec((KEYS, D), whole),
            pl.BlockSpec((1, D), whole),
        ],
        out_shape=[
            jax.ShapeDtypeStruct((D, D), BF),
            jax.ShapeDtypeStruct((D, D), BF),
            jax.ShapeDtypeStruct((D, D), BF),
            jax.ShapeDtypeStruct((KEYS, D), F32),
            jax.ShapeDtypeStruct((1, D), F32),
        ],
        scratch_shapes=[
            pltpu.VMEM((KEYS, D), BF),
            pltpu.VMEM((ROWS, width), BF),
            pltpu.VMEM((ROWS, width), BF),
            pltpu.VMEM((ROWS, PLEN), BF),
            pltpu.VMEM((KEYS, width), F32),
            pltpu.VMEM((KEYS, width), F32),
            pltpu.VMEM((ROWS, width), BF),
        ],
        compiler_params=pltpu.CompilerParams(vmem_limit_bytes=VMEM_LIMIT),
        cost_estimate=pl.CostEstimate(
            flops=30_000_000_000, bytes_accessed=30_000_000, transcendentals=1000
        ),
    )(x_all, gain, w_qkv, w_qkv, w_qkv, q, k, v, e, ec, o, r, d_att)


def tail_kernel(x_ref, f_ref, dmid_ref, gain_ref, out_ref):
    gain = gain_ref[...]
    part = x_ref[...].astype(F32)
    inv = rms_inv(part)
    unit = part * inv
    scaled = gain * f_ref[...]
    mean = jnp.mean(unit * scaled, axis=-1, keepdims=True)
    out_ref[...] = dmid_ref[...] + inv * (scaled - unit * mean)


def tail(x_own, f_own, d_mid, gain):
    rows = lambda i: (i, 0)
    return pl.pallas_call(
        tail_kernel,
        grid=(4,),
        in_specs=[
            pl.BlockSpec((PR, D), rows),
            pl.BlockSpec((PR, D), rows),
            pl.BlockSpec((PR, D), rows),
            pl.BlockSpec((1, D), lambda i: (0, 0)),
        ],
        out_specs=pl.BlockSpec((PR, D), rows),
        out_shape=jax.ShapeDtypeStruct((ROWS, D), F32),
        compiler_params=pltpu.CompilerParams(vmem_limit_bytes=VMEM_LIMIT),
    )(x_own, f_own, d_mid, gain)


def xor_shard(value, bits):
    size = lax.axis_size("shard")
    return lax.ppermute(value, "shard", [(i, i ^ bits) for i in range(size)])


def part_of(values, start, rows=PR):
    return lax.dynamic_slice_in_dim(values, start, rows, 0)


def per_device(tokens, w_qkv, w_out, w_up, w_down, gain_attn, gain_mlp, d_out):
    shards = lax.axis_size("shard")
    shard = lax.axis_index("shard")
    pos = shard % 8
    side = pos % 2

    def swap(values):
        mine_p = part_of(values, side * PR)
        mine_c = part_of(values, (2 + side) * PR)
        give = jnp.concatenate(
            [part_of(values, (1 - side) * PR), part_of(values, (3 - side) * PR)], axis=0
        )
        got = xor_shard(give, 1)
        return jnp.concatenate([mine_p, got[:PR], mine_c, got[PR:]], axis=0)

    def swap_back(values):
        got = xor_shard(
            jnp.concatenate([values[PR : 2 * PR], values[3 * PR :]], axis=0).astype(BF), 1
        ).astype(values.dtype)
        mine_p, mine_c = values[:PR], values[2 * PR : 3 * PR]
        first = side == 0
        return jnp.concatenate(
            [
                jnp.where(first, mine_p, got[:PR]),
                jnp.where(first, got[:PR], mine_p),
                jnp.where(first, mine_c, got[PR:]),
                jnp.where(first, got[PR:], mine_c),
            ],
            axis=0,
        )

    full_qkv = lax.all_gather(w_qkv, "shard", axis=0, tiled=True)
    full_gain_attn = lax.all_gather(gain_attn, "shard", axis=0, tiled=True)
    full_gain_mlp = lax.all_gather(gain_mlp, "shard", axis=0, tiled=True)
    full_out = lax.all_gather(w_out, "shard", axis=0, tiled=True)
    full_up = lax.all_gather(w_up, "shard", axis=0, tiled=True)
    full_down = lax.all_gather(w_down, "shard", axis=0, tiled=True)
    attn_gain = full_gain_attn.astype(F32).reshape(1, D)
    mlp_gain = full_gain_mlp.astype(F32).reshape(1, D)

    x_own = swap(tokens)
    g_own = swap(d_out)
    near = x_own[: 2 * PR]
    others = [xor_shard(near, 2 * k) for k in range(1, 4)]
    x_all = jnp.concatenate([near] + others + [x_own[2 * PR :]], axis=0)

    saved = attn_fwd(pos.reshape(1).astype(jnp.int32), x_all, attn_gain, full_qkv)
    attended = saved[5]
    block_rows, d_mid, d_att, d_wout, d_wup, d_wdown, d_gain_mlp = mlp(
        x_own, attended, g_own, mlp_gain, full_out, full_up, full_down
    )
    block_out = swap_back(block_rows)
    d_wq, d_wk, d_wv, f_all, d_gain_attn = attn_bwd(x_all, attn_gain, full_qkv, saved, d_att)
    f_near = f_all[: 2 * PR]
    for k in range(1, 4):
        sent = f_all[2 * k * PR : 2 * (k + 1) * PR].astype(BF)
        f_near = f_near + xor_shard(sent, 2 * k).astype(F32)
    f_own = jnp.concatenate([f_near, f_all[PLEN:]], axis=0)
    d_tokens = swap_back(tail(x_own, f_own, d_mid, attn_gain))

    d_wqkv = jnp.concatenate([d_wq, d_wk, d_wv], axis=1)

    def reduce(grad):
        part = lax.psum_scatter(grad, "shard", scatter_dimension=0, tiled=True)
        return lax.psum(part, "rep").astype(F32)

    return (
        block_out,
        d_tokens,
        reduce(d_wqkv),
        reduce(d_wout),
        reduce(d_wup),
        reduce(d_wdown),
        lax.psum(lax.psum_scatter(d_gain_attn.reshape(D), "shard", scatter_dimension=0, tiled=True), "rep"),
        lax.psum(lax.psum_scatter(d_gain_mlp.reshape(D), "shard", scatter_dimension=0, tiled=True), "rep"),
    )


def solution(mesh):
    weights = P("shard", None)
    rows = P(("rep", "shard"), None)
    return jax.shard_map(
        per_device,
        mesh=mesh,
        in_specs=(rows, weights, weights, weights, weights, P("shard"), P("shard"), rows),
        out_specs=(rows, rows, weights, weights, weights, weights, P("shard"), P("shard")),
        check_vma=False,
    )
```

```python
import jax
import jax.numpy as jnp
from jax import lax
from jax.experimental import pallas as pl
from jax.experimental.pallas import tpu as pltpu
from jax.sharding import PartitionSpec as P

D = 768
HEADS = 12
HDIM = 64
FF = 3072
PR = 128
PLEN = 1024
KEYS = PLEN + 2 * PR
ROWS = 4 * PR
PAIRS = HEADS // 2
WIDTH = 2 * HDIM
HALF = 1536
WIDE = HALF + 128
SUB = 48
LEFT = 896
FSUB = 96
FQ = FF // 4
norm_eps = 1e-05
neg_fill = -1e30
SCALE = HDIM ** (-0.5)
GELU_C = 0.7978845608028654
GELU_A = 0.044715
BF = jnp.bfloat16
F32 = jnp.float32
VMEM_LIMIT = 60 * 1024 * 1024
BLOCKS = (0, 1, 2, 3, 4, 5, 6, 7)
ORDER = (0, 2, 4, 6, 1, 3, 5, 7)


def dot_nt(a, b):
    return lax.dot_general(a, b, (((1,), (1,)), ((), ())), preferred_element_type=F32)


def dot_tn(a, b):
    return lax.dot_general(a, b, (((0,), (0,)), ((), ())), preferred_element_type=F32)


def dot_nn(a, b):
    return jnp.dot(a, b, preferred_element_type=F32)


def rms_inv(values):
    return lax.rsqrt(jnp.mean(values * values, axis=-1, keepdims=True) + norm_eps)


def params():
    return pltpu.CompilerParams(vmem_limit_bytes=VMEM_LIMIT)


def shape(dims, dtype):
    return jax.ShapeDtypeStruct(dims, dtype)


def fill_normed(x_ref, gain, normed_ref):
    @pl.loop(0, KEYS, step=PR)
    def _(row):
        rows = pl.ds(pl.multiple_of(row, PR), PR)
        part = x_ref[rows, :].astype(F32)
        normed_ref[rows, :] = (part * rms_inv(part) * gain).astype(BF)


def lane_half(head):
    lanes = lax.broadcasted_iota(jnp.int32, (1, WIDTH), 1)
    return (lanes >= HDIM) if head else (lanes < HDIM)


def gain_row(column):
    return column.astype(F32).T[0:1, :]


def attn_fwd_kernel(
    where_ref, x_ref, l00_ref, l10_ref, l01_ref, l11_ref, r00_ref, r10_ref, r01_ref, r11_ref,
    w_ref, q_ref, k_ref, v_ref, e_ref, ec_ref, o_ref, r_ref, mid_ref, nm_ref,
    normed_ref, bias_ref, att_ref, sems,
):
    step = pl.program_id(0)

    @pl.when(step == 0)
    def _():
        side, core = where_ref[1], where_ref[2]
        copies = []
        for at, (dx, dc, piece) in enumerate(
            ((0, 0, l00_ref), (1, 0, l10_ref), (0, 1, l01_ref), (1, 1, l11_ref))
        ):
            for i in range(8):
                start = where_ref[8 + i] * (2 * SUB) + jnp.bitwise_xor(side, dx) * SUB
                copies.append(
                    pltpu.make_async_copy(
                        piece.at[i],
                        w_ref.at[
                            jnp.bitwise_xor(core, dc),
                            pl.ds(pl.multiple_of(start, 16), SUB),
                            pl.ds(0, LEFT),
                        ],
                        sems.at[at * 8 + i],
                    )
                )
        for at, (far, dc, piece) in enumerate(
            ((0, 0, r00_ref), (1, 0, r10_ref), (0, 1, r01_ref), (1, 1, r11_ref))
        ):
            for i in range(8):
                start = where_ref[8 + far * 4 + i % 4] * (2 * SUB)
                start = start + jnp.bitwise_xor(side, i // 4) * SUB
                copies.append(
                    pltpu.make_async_copy(
                        piece.at[i],
                        w_ref.at[
                            jnp.bitwise_xor(core, dc),
                            pl.ds(pl.multiple_of(start, 16), SUB),
                            pl.ds(LEFT, WIDE - LEFT),
                        ],
                        sems.at[32 + at * 8 + i],
                    )
                )
        for copy in copies:
            copy.start()
        pos = where_ref[0]
        row = lax.broadcasted_iota(jnp.int32, (PR, PR), 0)
        col = lax.broadcasted_iota(jnp.int32, (PR, PR), 1)
        tri = jnp.where(col <= row, 0.0, neg_fill)
        for part in range(2):
            mine = jnp.bitwise_xor(pos, BLOCKS[part])
            for block in range(8):
                at = (pl.ds(part * PR, PR), pl.ds(block * PR, PR))
                if block == part:
                    bias_ref[at] = tri
                else:
                    seen = jnp.bitwise_xor(pos, BLOCKS[block]) < mine
                    bias_ref[at] = jnp.full((PR, PR), jnp.where(seen, 0.0, neg_fill), F32)
        for copy in copies:
            copy.wait()
        fill_normed(x_ref, gain_row(w_ref[0, :, HALF:]), normed_ref)

    at = pl.ds(pl.multiple_of(step * WIDTH, WIDTH), WIDTH)
    at_k = pl.ds(pl.multiple_of(D + step * WIDTH, WIDTH), WIDTH)
    k_ref[...] = dot_nn(normed_ref[...], w_ref[0, :, at_k]).astype(BF)
    v_ref[...] = dot_nn(normed_ref[...], w_ref[1, :, at]).astype(BF)
    wq = w_ref[0, :, at]
    q_ref[0 : 2 * PR, :] = (dot_nn(normed_ref[0 : 2 * PR, :], wq) * SCALE).astype(BF)
    q_ref[2 * PR :, :] = (dot_nn(normed_ref[PLEN:, :], wq) * SCALE).astype(BF)
    row = lax.broadcasted_iota(jnp.int32, (PR, PR), 0)
    col = lax.broadcasted_iota(jnp.int32, (PR, PR), 1)
    tri = jnp.where(col <= row, 0.0, neg_fill)
    for chunk in range(4):
        rows = slice(chunk * PR, (chunk + 1) * PR)
        query = q_ref[rows, :]
        outs, invs = [], []
        for head in range(2):
            masked = jnp.where(lane_half(head), query, jnp.zeros_like(query))
            scores = dot_nt(masked, k_ref[0:PLEN, :])
            if chunk < 2:
                scores = scores + bias_ref[rows, :]
                top = jnp.max(scores, axis=-1, keepdims=True)
                terms = jnp.exp(scores - top)
                total = jnp.sum(terms, axis=-1, keepdims=True)
                low_terms = terms.astype(BF)
                e_ref[head, rows, :] = low_terms
                out = dot_nn(low_terms, v_ref[0:PLEN, :])
            else:
                own = slice(PLEN + (chunk - 2) * PR, PLEN + (chunk - 1) * PR)
                near = dot_nt(masked, k_ref[own, :]) + tri
                top = jnp.maximum(
                    jnp.max(scores, axis=-1, keepdims=True), jnp.max(near, axis=-1, keepdims=True)
                )
                terms = jnp.exp(scores - top)
                near_terms = jnp.exp(near - top)
                total = jnp.sum(terms, axis=-1, keepdims=True) + jnp.sum(
                    near_terms, axis=-1, keepdims=True
                )
                low_terms = terms.astype(BF)
                low_near = near_terms.astype(BF)
                e_ref[head, rows, :] = low_terms
                ec_ref[head, (chunk - 2) * PR : (chunk - 1) * PR, :] = low_near
                out = dot_nn(low_terms, v_ref[0:PLEN, :]) + dot_nn(low_near, v_ref[own, :])
            inv = 1.0 / total
            outs.append(out * inv)
            invs.append(jnp.broadcast_to(inv, (PR, WIDTH)))
        low_half = lane_half(0)
        attended = jnp.where(low_half, outs[0], outs[1]).astype(BF)
        o_ref[rows, :] = attended
        att_ref[rows, at] = attended
        r_ref[rows, :] = jnp.where(low_half, invs[0], invs[1])

    @pl.when(step == PAIRS - 1)
    def _():
        wout = w_ref[1, :, D:HALF]
        gain = gain_row(w_ref[1, :, HALF:])
        for chunk in range(4):
            rows = slice(chunk * PR, (chunk + 1) * PR)
            from_row = chunk * PR if chunk < 2 else PLEN + (chunk - 2) * PR
            middle = x_ref[from_row : from_row + PR, :].astype(F32) + dot_nn(att_ref[rows, :], wout)
            mid_ref[rows, :] = middle
            nm_ref[rows, :] = (middle * rms_inv(middle) * gain).astype(BF)


def attn_fwd(where, x_all, pieces):
    pair = lambda i: (0, i)
    whole = lambda i: (0, 0)
    heads = lambda i: (i, 0, 0)
    anywhere = pl.BlockSpec(memory_space=pl.ANY)
    return pl.pallas_call(
        attn_fwd_kernel,
        grid=(PAIRS,),
        in_specs=[
            pl.BlockSpec(memory_space=pltpu.SMEM),
            pl.BlockSpec((KEYS, D), whole),
            *[anywhere] * 8,
        ],
        out_specs=[
            pl.BlockSpec((2, D, WIDE), lambda i: (0, 0, 0)),
            pl.BlockSpec((ROWS, WIDTH), pair),
            pl.BlockSpec((KEYS, WIDTH), pair),
            pl.BlockSpec((KEYS, WIDTH), pair),
            pl.BlockSpec((2, ROWS, PLEN), heads),
            pl.BlockSpec((2, 2 * PR, PR), heads),
            pl.BlockSpec((ROWS, WIDTH), pair),
            pl.BlockSpec((ROWS, WIDTH), pair),
            pl.BlockSpec((ROWS, D), whole),
            pl.BlockSpec((ROWS, D), whole),
        ],
        out_shape=[
            shape((2, D, WIDE), BF),
            shape((ROWS, D), BF),
            shape((KEYS, D), BF),
            shape((KEYS, D), BF),
            shape((HEADS, ROWS, PLEN), BF),
            shape((HEADS, 2 * PR, PR), BF),
            shape((ROWS, D), BF),
            shape((ROWS, D), F32),
            shape((ROWS, D), F32),
            shape((ROWS, D), BF),
        ],
        scratch_shapes=[
            pltpu.VMEM((KEYS, D), BF),
            pltpu.VMEM((2 * PR, PLEN), F32),
            pltpu.VMEM((ROWS, D), BF),
            pltpu.SemaphoreType.DMA((64,)),
        ],
        compiler_params=params(),
        cost_estimate=pl.CostEstimate(
            flops=30_000_000_000, bytes_accessed=30_000_000, transcendentals=6_300_000
        ),
    )(where, x_all, *pieces)


def mlp_kernel(first, where_ref, *refs):
    if first:
        nm0_ref, nm1_ref, g0_ref, g1_ref = refs[:4]
        e0_ref, e1_ref, y0_ref, y1_ref, dup_ref, ddown_ref = refs[8:14]
        wup_ref, wdown_ref, sems = refs[14:]
    else:
        nm0_ref, nm1_ref, g0_ref, g1_ref = refs[:4]
        up_in_ref, down_in_ref = refs[8:10]
        e0_ref, e1_ref, y0_ref, y1_ref, grad_ref = refs[10:15]
        wup_ref, wdown_ref, dup_ref, ddown_ref, sems = refs[15:]
    copies = []
    for i in range(8):
        piece = refs[4 + i % 4].at[i // 4]
        rows = pl.ds(pl.multiple_of(where_ref[8 + i] * FSUB, 16), FSUB)
        copies.append(
            pltpu.make_async_copy(piece.at[pl.ds(0, FSUB), :], wup_ref.at[rows, :], sems.at[2 * i])
        )
        copies.append(
            pltpu.make_async_copy(
                piece.at[pl.ds(FSUB, FSUB), :], wdown_ref.at[rows, :], sems.at[2 * i + 1]
            )
        )
    for copy in copies:
        copy.start()
    for copy in copies:
        copy.wait()
    for block, (nm_ref, g_ref, e_ref, y_ref) in enumerate(
        ((nm0_ref, g0_ref, e0_ref, y0_ref), (nm1_ref, g1_ref, e1_ref, y1_ref))
    ):
        nm = nm_ref[...]
        grad = g_ref[...]
        wup = wup_ref[...]
        wdown = wdown_ref[...]
        hidden = dot_nn(nm, wup)
        square = hidden * hidden
        th = jnp.tanh(GELU_C * (hidden + GELU_A * square * hidden))
        left = 0.5 * (1.0 + th)
        active = (hidden * left).astype(BF)
        slope = left + 0.5 * hidden * (1.0 - th * th) * (GELU_C * (1.0 + 3.0 * GELU_A * square))
        d_hidden = (dot_nt(grad, wdown) * slope).astype(BF)
        y_ref[...] = dot_nn(active, wdown).astype(BF)
        e_ref[...] = dot_nt(d_hidden, wup).astype(BF)
        d_down = dot_tn(active, grad)
        d_up = dot_tn(nm, d_hidden)
        if block == 0:
            if first:
                dup_ref[...] = d_up
                ddown_ref[...] = d_down
            else:
                dup_ref[...] = up_in_ref[...] + d_up
                ddown_ref[...] = down_in_ref[...] + d_down
        else:
            dup_ref[...] += d_up
            ddown_ref[...] += d_down
    if not first:
        for s in range(8):
            rows = slice(s * FSUB, (s + 1) * FSUB)
            grad_ref[s, 0:FSUB, :] = dup_ref[rows, :].astype(BF)
            grad_ref[s, FSUB:, :] = ddown_ref[rows, :].astype(BF)


def mlp(where, normed, grads, pieces, sums=None):
    first = sums is None
    vmem = pl.BlockSpec(memory_space=pltpu.VMEM)
    anywhere = pl.BlockSpec(memory_space=pl.ANY)
    rows = [shape((ROWS, D), BF)] * 4
    square = pltpu.VMEM((D, FQ), F32)
    return pl.pallas_call(
        lambda *refs: mlp_kernel(first, *refs),
        in_specs=[pl.BlockSpec(memory_space=pltpu.SMEM)]
        + [vmem] * 4
        + [anywhere] * 4
        + ([] if first else [vmem] * 2),
        out_specs=[vmem] * (6 if first else 5),
        out_shape=rows
        + ([shape((D, FQ), F32)] * 2 if first else [shape((8, 2 * FSUB, FQ), BF)]),
        scratch_shapes=[pltpu.VMEM((D, FQ), BF)] * 2
        + ([] if first else [square] * 2)
        + [pltpu.SemaphoreType.DMA((16,))],
        compiler_params=params(),
        cost_estimate=pl.CostEstimate(
            flops=9_000_000_000, bytes_accessed=14_000_000, transcendentals=800_000
        ),
    )(where, *normed, *grads, *pieces, *([] if first else sums))


def branch_kernel(
    mid_ref, g_ref, e0_ref, e1_ref, e2_ref, att_ref, w_ref, dmid_ref, datt_ref, dwout_ref, dgain_ref,
    low_ref, prod_ref,
):
    gain = gain_row(w_ref[0, :, HALF:])
    wout = w_ref[0, :, D:HALF]
    for chunk in range(4):
        rows = slice(chunk * PR, (chunk + 1) * PR)
        middle = mid_ref[rows, :]
        inv = rms_inv(middle)
        unit = middle * inv
        grad = (
            e0_ref[rows, :].astype(F32) + e1_ref[rows, :].astype(F32) + e2_ref[rows, :].astype(F32)
        )
        scaled = gain * grad
        mean = jnp.mean(unit * scaled, axis=-1, keepdims=True)
        d_mid = g_ref[rows, :].astype(F32) + inv * (scaled - unit * mean)
        dmid_ref[rows, :] = d_mid
        prod_ref[rows, :] = (grad * unit).astype(BF)
        branch = d_mid.astype(BF)
        low_ref[rows, :] = branch
        datt_ref[rows, :] = dot_nt(branch, wout).astype(BF)
    dgain_ref[...] = dot_tn(prod_ref[...], jnp.ones((ROWS, 128), BF)).astype(BF)
    dwout_ref[...] = dot_tn(att_ref[...], low_ref[...]).astype(BF)


def branch(middle, d_out, terms, attended, w_all):
    vmem = pl.BlockSpec(memory_space=pltpu.VMEM)
    return pl.pallas_call(
        branch_kernel,
        grid=(1,),
        in_specs=[pl.BlockSpec((ROWS, D), lambda i: (0, 0))] * 6
        + [pl.BlockSpec((1, D, WIDE), lambda i: (1, 0, 0))],
        out_specs=[
            pl.BlockSpec((ROWS, D), lambda i: (0, 0)),
            pl.BlockSpec((ROWS, D), lambda i: (0, 0)),
            pl.BlockSpec((D, D), lambda i: (0, 0)),
            pl.BlockSpec((D, 128), lambda i: (0, 0)),
        ],
        out_shape=[shape((ROWS, D), F32), shape((ROWS, D), BF), shape((D, D), BF), shape((D, 128), BF)],
        scratch_shapes=[pltpu.VMEM((ROWS, D), BF), pltpu.VMEM((ROWS, D), BF)],
        compiler_params=params(),
        cost_estimate=pl.CostEstimate(
            flops=2_000_000_000, bytes_accessed=9_000_000, transcendentals=1000
        ),
    )(middle, d_out, *terms, attended, w_all)


def attn_bwd_kernel(
    x_ref, gcol_ref, wq_ref, wk_ref, wv_ref, q_ref, k_ref, v_ref, e_ref, ec_ref, o_ref, r_ref,
    g_ref, dwq_ref, dwk_ref, dwv_ref, f_ref, fc_ref, dgain_ref,
    normed_ref, qs_ref, gs_ref, ds_ref, dk_ref, dv_ref, dq_ref, acc_ref,
):
    step = pl.program_id(0)

    @pl.when(step == 0)
    def _():
        fill_normed(x_ref, gain_row(gcol_ref[0]), normed_ref)

    scaled_grad = g_ref[...].astype(F32) * r_ref[...]
    prod = scaled_grad * o_ref[...].astype(F32)
    low_grad = scaled_grad.astype(BF)
    query = q_ref[...]
    dq_parts = []
    for head in range(2):
        half = lane_half(head)
        grad_h = jnp.where(half, low_grad, jnp.zeros_like(low_grad))
        query_h = jnp.where(half, query, jnp.zeros_like(query))
        delta = jnp.sum(jnp.where(half, prod, 0.0), axis=-1, keepdims=True)
        gs_ref[...] = grad_h
        qs_ref[...] = query_h
        for chunk in range(4):
            rows = slice(chunk * PR, (chunk + 1) * PR)
            d_soft = dot_nt(gs_ref[rows, :], v_ref[0:PLEN, :])
            ds_ref[rows, :] = (
                e_ref[head, rows, :].astype(F32) * (d_soft - delta[rows])
            ).astype(BF)
        d_query = dot_nn(ds_ref[...], k_ref[0:PLEN, :])
        d_key = dot_tn(ds_ref[...], qs_ref[...])
        d_value = dot_tn(e_ref[head], gs_ref[...])
        near_q, near_k, near_v = [], [], []
        for part in range(2):
            own = slice(PLEN + part * PR, PLEN + (part + 1) * PR)
            mine = slice((2 + part) * PR, (3 + part) * PR)
            near = ec_ref[head, part * PR : (part + 1) * PR, :]
            d_soft = dot_nt(gs_ref[mine, :], v_ref[own, :])
            d_near = (near.astype(F32) * (d_soft - delta[mine])).astype(BF)
            near_q.append(dot_nn(d_near, k_ref[own, :]))
            near_k.append(dot_tn(d_near, qs_ref[mine, :]))
            near_v.append(dot_tn(near, gs_ref[mine, :]))
        dq_parts.append((d_query, near_q))
        for part in range(2):
            own = slice(PLEN + part * PR, PLEN + (part + 1) * PR)
            if head == 0:
                dk_ref[own, :] = near_k[part]
                dv_ref[own, :] = near_v[part]
            else:
                dk_ref[own, :] += near_k[part]
                dv_ref[own, :] += near_v[part]
        if head == 0:
            dk_ref[0:PLEN, :] = d_key
            dv_ref[0:PLEN, :] = d_value
        else:
            dk_ref[0:PLEN, :] += d_key
            dv_ref[0:PLEN, :] += d_value
    low_half = lane_half(0)
    dq_ref[0 : 2 * PR, :] = (
        jnp.where(low_half, dq_parts[0][0][0 : 2 * PR], dq_parts[1][0][0 : 2 * PR]) * SCALE
    ).astype(BF)
    for part in range(2):
        mine = slice((2 + part) * PR, (3 + part) * PR)
        both = [dq_parts[h][0][mine] + dq_parts[h][1][part] for h in range(2)]
        dq_ref[mine, :] = (jnp.where(low_half, both[0], both[1]) * SCALE).astype(BF)
    d_key = dk_ref[...].astype(BF)
    d_value = dv_ref[...].astype(BF)
    d_query = dq_ref[...]
    dwk_ref[...] = dot_tn(normed_ref[...], d_key).astype(BF)
    dwv_ref[...] = dot_tn(normed_ref[...], d_value).astype(BF)
    dwq_ref[...] = (
        dot_tn(normed_ref[0 : 2 * PR, :], d_query[0 : 2 * PR])
        + dot_tn(normed_ref[PLEN:, :], d_query[2 * PR :])
    ).astype(BF)
    part_kv = dot_nt(d_key, wk_ref[0]) + dot_nt(d_value, wv_ref[0])
    part_q = dot_nt(d_query, wq_ref[0])

    @pl.when(step == 0)
    def _():
        acc_ref[...] = part_kv

    @pl.when(step > 0)
    def _():
        acc_ref[...] += part_kv

    acc_ref[0 : 2 * PR, :] += part_q[0 : 2 * PR]
    acc_ref[PLEN:, :] += part_q[2 * PR :]

    @pl.when(step == PAIRS - 1)
    def _():
        for block in range(KEYS // PR):
            rows = slice(block * PR, (block + 1) * PR)
            part = x_ref[rows, :].astype(F32)
            normed_ref[rows, :] = (acc_ref[rows, :] * (part * rms_inv(part))).astype(BF)
        dgain_ref[...] = dot_tn(normed_ref[...], jnp.ones((KEYS, 128), BF)).astype(BF)
        f_ref[...] = acc_ref[0:PLEN, :].astype(BF)
        fc_ref[...] = acc_ref[PLEN:, :]


def attn_bwd(x_all, w_all, saved, d_att):
    pair = lambda i: (0, i)
    whole = lambda i: (0, 0)
    heads = lambda i: (i, 0, 0)
    return pl.pallas_call(
        attn_bwd_kernel,
        grid=(PAIRS,),
        in_specs=[
            pl.BlockSpec((KEYS, D), whole),
            pl.BlockSpec((1, D, WIDTH), lambda i: (0, 0, HALF // WIDTH)),
            pl.BlockSpec((1, D, WIDTH), lambda i: (0, 0, i)),
            pl.BlockSpec((1, D, WIDTH), lambda i: (0, 0, PAIRS + i)),
            pl.BlockSpec((1, D, WIDTH), lambda i: (1, 0, i)),
            pl.BlockSpec((ROWS, WIDTH), pair),
            pl.BlockSpec((KEYS, WIDTH), pair),
            pl.BlockSpec((KEYS, WIDTH), pair),
            pl.BlockSpec((2, ROWS, PLEN), heads),
            pl.BlockSpec((2, 2 * PR, PR), heads),
            pl.BlockSpec((ROWS, WIDTH), pair),
            pl.BlockSpec((ROWS, WIDTH), pair),
            pl.BlockSpec((ROWS, WIDTH), pair),
        ],
        out_specs=[
            pl.BlockSpec((D, WIDTH), pair),
            pl.BlockSpec((D, WIDTH), pair),
            pl.BlockSpec((D, WIDTH), pair),
            pl.BlockSpec((PLEN, D), whole),
            pl.BlockSpec((2 * PR, D), whole),
            pl.BlockSpec((D, 128), whole),
        ],
        out_shape=[
            shape((D, D), BF),
            shape((D, D), BF),
            shape((D, D), BF),
            shape((PLEN, D), BF),
            shape((2 * PR, D), F32),
            shape((D, 128), BF),
        ],
        scratch_shapes=[
            pltpu.VMEM((KEYS, D), BF),
            pltpu.VMEM((ROWS, WIDTH), BF),
            pltpu.VMEM((ROWS, WIDTH), BF),
            pltpu.VMEM((ROWS, PLEN), BF),
            pltpu.VMEM((KEYS, WIDTH), F32),
            pltpu.VMEM((KEYS, WIDTH), F32),
            pltpu.VMEM((ROWS, WIDTH), BF),
            pltpu.VMEM((KEYS, D), F32),
        ],
        compiler_params=params(),
        cost_estimate=pl.CostEstimate(
            flops=40_000_000_000, bytes_accessed=30_000_000, transcendentals=1000
        ),
    )(x_all, w_all, w_all, w_all, w_all, *saved, d_att)


def tail_kernel(x_ref, f0_ref, f1_ref, f2_ref, f3_ref, fc_ref, dmid_ref, w_ref, out_ref):
    gain = gain_row(w_ref[0])
    for chunk in range(4):
        rows = slice(chunk * PR, (chunk + 1) * PR)
        part = x_ref[rows, :].astype(F32)
        inv = rms_inv(part)
        unit = part * inv
        if chunk < 2:
            grad = f0_ref[rows, :].astype(F32)
            for f_ref in (f1_ref, f2_ref, f3_ref):
                grad = grad + f_ref[rows, :].astype(F32)
        else:
            grad = fc_ref[(chunk - 2) * PR : (chunk - 1) * PR, :]
        scaled = gain * grad
        mean = jnp.mean(unit * scaled, axis=-1, keepdims=True)
        out_ref[rows, :] = dmid_ref[rows, :] + inv * (scaled - unit * mean)


def tail(x_own, f_parts, f_cont, d_mid, w_all):
    whole = lambda i: (0, 0)
    half = pl.BlockSpec((2 * PR, D), whole)
    full = pl.BlockSpec((ROWS, D), whole)
    return pl.pallas_call(
        tail_kernel,
        grid=(1,),
        in_specs=[full, half, half, half, half, half, full]
        + [pl.BlockSpec((1, D, 128), lambda i: (0, 0, HALF // 128))],
        out_specs=full,
        out_shape=shape((ROWS, D), F32),
        compiler_params=params(),
        cost_estimate=pl.CostEstimate(flops=20_000_000, bytes_accessed=7_000_000, transcendentals=1000),
    )(x_own, *f_parts, f_cont, d_mid, w_all)


def over(axis, value, bits):
    return lax.ppermute(value, axis, [(i, i ^ bits) for i in range(lax.axis_size(axis))])


def cut(values, start, rows=PR):
    return lax.dynamic_slice_in_dim(values, start, rows, 0)


def pick(values, at):
    return lax.dynamic_index_in_dim(values, at, 0, keepdims=False)


def pick_of(values, at, axis):
    return lax.dynamic_index_in_dim(values, at, axis, keepdims=False)


def tie(*values):
    return lax.optimization_barrier(values)


def add(mine, got):
    return (mine.astype(F32) + got.astype(F32)).astype(BF)


def per_device(tokens, w_qkv, w_out, w_up, w_down, gain_attn, gain_mlp, d_out):
    staged = lax.axis_size("shard") == 8
    shard = lax.axis_index("shard")
    rep = lax.axis_index("rep")
    side, core = rep // 2, rep % 2
    pos = shard % 8
    y_at, z_at = pos % 2, pos // 2
    table = [pos ^ d for d in ORDER] if staged else [jnp.int32(2 * (d % 4) + d // 4) for d in range(8)]
    where = jnp.stack([pos, side, core] + [jnp.int32(0)] * 5 + table).astype(jnp.int32)

    def to_give(values):
        return jnp.concatenate([cut(values, (1 - y_at) * PR), cut(values, (3 - y_at) * PR)], axis=0)

    def own_rows(values, got):
        mine_p, mine_c = cut(values, y_at * PR), cut(values, (2 + y_at) * PR)
        return jnp.concatenate([mine_p, got[:PR], mine_c, got[PR:]], axis=0)

    def to_return(values):
        return jnp.concatenate([values[PR : 2 * PR], values[3 * PR :]], axis=0).astype(BF)

    def home_rows(values, got):
        got = got.astype(values.dtype)
        mine_p, mine_c = values[:PR], values[2 * PR : 3 * PR]
        first = y_at == 0
        return jnp.concatenate(
            [
                jnp.where(first, mine_p, got[:PR]),
                jnp.where(first, got[:PR], mine_p),
                jnp.where(first, mine_c, got[PR:]),
                jnp.where(first, got[PR:], mine_c),
            ],
            axis=0,
        )

    def halves(qkv, out, gain_a, gain_m):
        wide = lambda gain: jnp.broadcast_to(gain[:, None], (gain.shape[0], 128))
        return (
            jnp.concatenate([qkv[:, :HALF], wide(gain_a)], axis=1),
            jnp.concatenate([qkv[:, HALF:], out, wide(gain_m)], axis=1),
        )

    def quarter(up):
        return pick_of(up.reshape(up.shape[0], 8, 4, FSUB), rep, 2).reshape(up.shape[0], FQ)

    def unpack_up(quarters):
        rows = quarters.shape[1]
        return quarters.reshape(4, rows, 8, FSUB).transpose(1, 2, 0, 3).reshape(rows, FF)

    if staged:
        low, high = halves(w_qkv, w_out, gain_attn, gain_mlp)
        own_piece = cut(jnp.where(core == 0, low, high), side * SUB, SUB)
        own_mlp = jnp.concatenate([quarter(w_up), cut(w_down, rep * FSUB, FSUB)], axis=0)
        t_got, z1, z2, z3, m_got = tie(
            over("shard", to_give(tokens), 1),
            *[over("shard", own_piece, k) for k in (2, 4, 6)],
            over("shard", own_mlp, 1),
        )
        x_own = own_rows(tokens, t_got)
        near = x_own[: 2 * PR]
        line = (own_piece, z1, z2, z3)
        left = jnp.stack([part[:, :LEFT] for part in line])
        right = jnp.stack([part[:, LEFT:] for part in line])
        near2, left_y, right_x, g_got = tie(
            over("shard", near, 4),
            over("shard", left, 1),
            over("rep", right, 2),
            over("shard", to_give(d_out), 1),
        )
        left = jnp.concatenate([left, left_y], axis=0)
        right = jnp.concatenate([right, right_x], axis=0)
        near, left, right = tie(near, left, right)
        near1, near3, left_x, right_y = tie(
            over("shard", near, 2),
            over("shard", near, 6),
            over("rep", left, 2),
            over("shard", right, 1),
        )
        pieces = tie(
            left, left_x, over("rep", left, 1), over("rep", left_x, 1),
            right, right_y, over("rep", right, 1), over("rep", right_y, 1),
        )
        mlp_own = jnp.stack([own_mlp, m_got])
        mlp_own, pieces = tie(mlp_own, pieces)
        mlp_pieces = (mlp_own, *[over("shard", mlp_own, k) for k in (2, 4, 6)])
    else:
        gathered = [
            lax.all_gather(w, "shard", axis=0, tiled=True)
            for w in (w_qkv, w_out, gain_attn, gain_mlp, w_up, w_down)
        ]
        natural = jnp.stack(halves(*gathered[:4])).reshape(2, 4, 2, 2, SUB, WIDE)
        pieces = []
        for dc in (0, 1):
            by_core = pick(natural, core ^ dc)
            for dx in (0, 1):
                both = pick_of(by_core[..., :LEFT], side ^ dx, 2)
                pieces.append(jnp.concatenate([both[:, 0], both[:, 1]], axis=0))
        for dc in (0, 1):
            by_core = pick(natural, core ^ dc)[..., LEFT:]
            for dy in (0, 1):
                both = [pick_of(by_core[:, dy], side ^ dx, 1) for dx in (0, 1)]
                pieces.append(jnp.concatenate(both, axis=0))
        pieces = tuple(pieces)
        up_q = quarter(gathered[4]).reshape(4, 2, FSUB, FQ)
        down_q = pick_of(gathered[5].reshape(8, 4, FSUB, D), rep, 1).reshape(4, 2, FSUB, D)
        both = jnp.concatenate([up_q, down_q], axis=2)
        mlp_pieces = (both[0], both[1], both[2], both[3])
        x_own = own_rows(tokens, over("shard", to_give(tokens), 1))
        near = x_own[: 2 * PR]
        near1, near2, near3 = [over("shard", near, k) for k in (2, 4, 6)]
        g_got = over("shard", to_give(d_out), 1)
    x_all = jnp.concatenate([near, near1, near2, near3, x_own[2 * PR :]], axis=0)
    g_own = own_rows(d_out, g_got)
    x_all, g_own = tie(x_all, g_own)

    g_side = over("rep", g_own, 2)
    forward = attn_fwd(where, x_all, pieces)
    forward, mlp_pieces, g_side = tie(forward, mlp_pieces, g_side)
    w_all, q, k, v, e, ec, attended, inv_sum, middle, nm = forward

    nm_core, g_core = tie(over("rep", nm, 1), over("rep", g_own, 1))
    nm, nm_core, g_side = tie(nm, nm_core, g_side)
    nm_side, g_far = over("rep", nm, 2), over("rep", g_side, 1)
    near_out = mlp(where, (nm, nm_core), (g_own, g_core), mlp_pieces)
    nm_side, g_far, near_out = tie(nm_side, g_far, near_out)
    e_own, e_core, y_own, y_core, d_up, d_down = near_out
    nm_far, nm_side, d_up, d_down = tie(over("rep", nm_side, 1), nm_side, d_up, d_down)
    e_chip, y_chip = over("rep", e_core, 1), over("rep", y_core, 1)
    far_out = mlp(where, (nm_side, nm_far), (g_side, g_far), mlp_pieces, (d_up, d_down))
    far_out, e_chip, y_chip = tie(far_out, e_chip, y_chip)
    e_side, e_far, y_side, y_far, d_mlp = far_out
    e_got, y_got = tie(over("rep", e_far, 1), over("rep", y_far, 1))
    e_sum, y_sum = tie(add(e_side, e_got), add(y_side, y_got))
    e_last, y_sum = tie(over("rep", e_sum, 2), y_sum)
    d_mid, d_att, d_wout, d_gain_m = branch(
        middle, g_own, (e_own, e_chip, e_last), attended, w_all
    )

    d_att, d_mlp, y_sum = tie(d_att, d_mlp, y_sum)
    y_last = over("rep", y_sum, 2)
    grid = d_mlp.reshape(d_mlp.shape[0] // 2, 2, 2 * FSUB, FQ)
    if staged:
        mlp_parts = [pick(grid, z_at)] + [
            over("shard", pick(grid, z_at ^ step), 2 * step) for step in (1, 2, 3)
        ]
    else:
        mlp_parts = [d_mlp]
    backward = attn_bwd(x_all, w_all, (q, k, v, e, ec, attended, inv_sum), d_att)
    backward, mlp_parts, y_last = tie(backward, mlp_parts, y_last)
    d_wq, d_wk, d_wv, f_all, f_cont, d_gain_a = backward
    f_parts = f_all.reshape(4, 2 * PR, D)
    block_rows = (
        middle + y_own.astype(F32) + y_chip.astype(F32) + y_last.astype(F32)
    ).astype(BF)
    low = jnp.concatenate([d_wq, d_wk, d_gain_a], axis=1)
    high = jnp.concatenate([d_wv, d_wout, d_gain_m], axis=1)
    if staged:
        mlp_pair = sum(part.astype(F32) for part in mlp_parts).astype(BF)
        chip_got, m_got, b_got = tie(
            over("rep", jnp.where(core == 0, high, low), 1),
            over("shard", pick(mlp_pair, 1 - y_at), 1),
            over("shard", to_return(block_rows), 1),
        )
        chip = add(jnp.where(core == 0, low, high), chip_got).reshape(4, 2, 2, SUB, WIDE)
        mlp_total = add(pick(mlp_pair, y_at), m_got)
        left, right = chip[..., :LEFT], chip[..., LEFT:]
        left_keep, left_give = pick_of(left, side, 2), pick_of(left, 1 - side, 2)
        right_keep, right_give = pick_of(right, y_at, 1), pick_of(right, 1 - y_at, 1)
        f2, left_got, right_got, f_parts = tie(
            over("shard", f_parts[2], 4),
            over("rep", left_give, 2),
            over("shard", right_give, 1),
            f_parts,
        )
        left, right = add(left_keep, left_got), add(right_keep, right_got)
        left_keep, left_give = pick_of(left, y_at, 1), pick_of(left, 1 - y_at, 1)
        right_keep, right_give = pick_of(right, side, 1), pick_of(right, 1 - side, 1)
        f1, f3, left_got, right_got, f2 = tie(
            over("shard", f_parts[1], 2),
            over("shard", f_parts[3], 6),
            over("shard", left_give, 1),
            over("rep", right_give, 2),
            f2,
        )
        line = jnp.concatenate([add(left_keep, left_got), add(right_keep, right_got)], axis=-1)
        token_rows = tail(x_own, (f_parts[0], f1, f2, f3), f_cont, d_mid, w_all)
        total = pick(line, z_at)
        z1, z2, z3, t_got, m_got = tie(
            *[over("shard", pick(line, z_at ^ step), 2 * step) for step in (1, 2, 3)],
            over("shard", to_return(token_rows), 1),
            over("rep", mlp_total, 2),
        )
        total = (
            total.astype(F32) + z1.astype(F32) + z2.astype(F32) + z3.astype(F32)
        ).astype(BF)
        by_side = jnp.stack([mlp_total, m_got])
        other, m_got = tie(over("rep", total, 2), over("rep", by_side, 1))
        by_core = jnp.stack([by_side, m_got])
        rows = jnp.concatenate(
            [jnp.where(side == 0, total, other), jnp.where(side == 0, other, total)], axis=0
        )
        other = over("rep", rows, 1)
        quarters = jnp.stack(
            [pick(pick(by_core, core ^ (r % 2)), side ^ (r // 2)) for r in range(4)]
        )
        d_wup = unpack_up(quarters[:, :FSUB]).astype(F32)
        d_wdown = quarters[:, FSUB:].reshape(4 * FSUB, D).astype(F32)
        low = jnp.where(core == 0, rows, other).astype(F32)
        high = jnp.where(core == 0, other, rows).astype(F32)
    else:
        b_got = over("shard", to_return(block_rows), 1)
        f_terms = [f_parts[0]] + [over("shard", f_parts[i], 2 * i) for i in (1, 2, 3)]
        token_rows = tail(x_own, f_terms, f_cont, d_mid, w_all)
        t_got = over("shard", to_return(token_rows), 1)
        quarters = lax.all_gather(d_mlp.reshape(8, 2, FSUB, FQ), "rep")
        up = unpack_up(quarters[:, :, 0].reshape(4, D, FQ))
        down = quarters[:, :, 1].transpose(1, 0, 2, 3).reshape(FF, D)
        scatter = lambda v: lax.psum_scatter(v, "shard", scatter_dimension=0, tiled=True)
        d_wup, d_wdown = scatter(up).astype(F32), scatter(down).astype(F32)
        low = lax.psum(scatter(low), "rep").astype(F32)
        high = lax.psum(scatter(high), "rep").astype(F32)

    return (
        home_rows(block_rows, b_got),
        home_rows(token_rows, t_got),
        jnp.concatenate([low[:, :HALF], high[:, :D]], axis=1),
        high[:, D:HALF],
        d_wup,
        d_wdown,
        low[:, HALF],
        high[:, HALF],
    )


def solution(mesh):
    weights = P("shard", None)
    rows = P(("rep", "shard"), None)
    return jax.shard_map(
        per_device,
        mesh=mesh,
        in_specs=(rows, weights, weights, weights, weights, P("shard"), P("shard"), rows),
        out_specs=(rows, rows, weights, weights, weights, weights, P("shard"), P("shard")),
        check_vma=False,
    )
```

```python
import jax
import jax.numpy as jnp
from jax import lax
from jax.experimental import pallas as pl
from jax.experimental.pallas import tpu as pltpu
from jax.sharding import PartitionSpec as P

D = 768
HEADS = 12
HDIM = 64
FF = 3072
PR = 128
PLEN = 1024
KEYS = PLEN + 2 * PR
ROWS = 4 * PR
PAIRS = HEADS // 2
WIDTH = 2 * HDIM
HALF = 1536
WIDE = HALF + 128
SUB = 48
LEFT = 896
RIGHT = D + 128
UNIT = 2 * PR
FSUB = 96
FH = FF // 2
norm_eps = 1e-05
neg_fill = -1e30
SCALE = HDIM ** (-0.5)
GELU_C = 0.7978845608028654
GELU_A = 0.044715
BF = jnp.bfloat16
F32 = jnp.float32
VMEM_LIMIT = 60 * 1024 * 1024
BLOCKS = (0, 1, 2, 3, 4, 5, 6, 7)
ORDER = (0, 2, 4, 6, 1, 3, 5, 7)


def dot_nt(a, b):
    return lax.dot_general(a, b, (((1,), (1,)), ((), ())), preferred_element_type=F32)


def dot_tn(a, b):
    return lax.dot_general(a, b, (((0,), (0,)), ((), ())), preferred_element_type=F32)


def dot_nn(a, b):
    return jnp.dot(a, b, preferred_element_type=F32)


def rms_inv(values):
    return lax.rsqrt(jnp.mean(values * values, axis=-1, keepdims=True) + norm_eps)


def params():
    return pltpu.CompilerParams(vmem_limit_bytes=VMEM_LIMIT)


def shape(dims, dtype):
    return jax.ShapeDtypeStruct(dims, dtype)


def fill_normed(x_ref, gain, normed_ref):
    @pl.loop(0, KEYS, step=PR)
    def _(row):
        rows = pl.ds(pl.multiple_of(row, PR), PR)
        part = x_ref[rows, :].astype(F32)
        normed_ref[rows, :] = (part * rms_inv(part) * gain).astype(BF)


def lane_half(head):
    lanes = lax.broadcasted_iota(jnp.int32, (1, WIDTH), 1)
    return (lanes >= HDIM) if head else (lanes < HDIM)


def gain_row(column):
    return column.astype(F32).T[0:1, :]


def attn_fwd_kernel(
    where_ref, x_ref, l00_ref, l10_ref, l01_ref, l11_ref, r00_ref, r10_ref, r01_ref, r11_ref,
    w_ref, q_ref, k_ref, v_ref, e_ref, ec_ref, o_ref, r_ref, mid_ref, nm_ref, normed_ref,
    bias_ref, att_ref, sems,
):
    step = pl.program_id(0)

    @pl.when(step == 0)
    def _():
        side, core = where_ref[1], where_ref[2]
        copies = []
        for at, (dx, dc, piece) in enumerate(
            ((0, 0, l00_ref), (1, 0, l10_ref), (0, 1, l01_ref), (1, 1, l11_ref))
        ):
            for i in range(8):
                start = where_ref[8 + i] * (2 * SUB) + jnp.bitwise_xor(side, dx) * SUB
                copies.append(
                    pltpu.make_async_copy(
                        piece.at[i],
                        w_ref.at[
                            jnp.bitwise_xor(core, dc),
                            pl.ds(pl.multiple_of(start, 16), SUB),
                            pl.ds(0, LEFT),
                        ],
                        sems.at[at * 8 + i],
                    )
                )
        for at, (far, dc, piece) in enumerate(
            ((0, 0, r00_ref), (1, 0, r10_ref), (0, 1, r01_ref), (1, 1, r11_ref))
        ):
            for i in range(8):
                start = where_ref[8 + far * 4 + i % 4] * (2 * SUB)
                start = start + jnp.bitwise_xor(side, i // 4) * SUB
                copies.append(
                    pltpu.make_async_copy(
                        piece.at[i],
                        w_ref.at[
                            jnp.bitwise_xor(core, dc),
                            pl.ds(pl.multiple_of(start, 16), SUB),
                            pl.ds(LEFT, WIDE - LEFT),
                        ],
                        sems.at[32 + at * 8 + i],
                    )
                )
        for copy in copies:
            copy.start()
        pos = where_ref[0]
        row = lax.broadcasted_iota(jnp.int32, (PR, PR), 0)
        col = lax.broadcasted_iota(jnp.int32, (PR, PR), 1)
        tri = jnp.where(col <= row, 0.0, neg_fill)
        for part in range(2):
            mine = jnp.bitwise_xor(pos, BLOCKS[part])
            for block in range(8):
                at = (pl.ds(part * PR, PR), pl.ds(block * PR, PR))
                if block == part:
                    bias_ref[at] = tri
                else:
                    seen = jnp.bitwise_xor(pos, BLOCKS[block]) < mine
                    bias_ref[at] = jnp.full((PR, PR), jnp.where(seen, 0.0, neg_fill), F32)
        for copy in copies:
            copy.wait()
        fill_normed(x_ref, gain_row(w_ref[0, :, HALF:]), normed_ref)

    at = pl.ds(pl.multiple_of(step * WIDTH, WIDTH), WIDTH)
    at_k = pl.ds(pl.multiple_of(D + step * WIDTH, WIDTH), WIDTH)
    k_ref[...] = dot_nn(normed_ref[...], w_ref[0, :, at_k]).astype(BF)
    v_ref[...] = dot_nn(normed_ref[...], w_ref[1, :, at]).astype(BF)
    wq = w_ref[0, :, at]
    q_ref[0 : 2 * PR, :] = (dot_nn(normed_ref[0 : 2 * PR, :], wq) * SCALE).astype(BF)
    q_ref[2 * PR :, :] = (dot_nn(normed_ref[PLEN:, :], wq) * SCALE).astype(BF)
    row = lax.broadcasted_iota(jnp.int32, (PR, PR), 0)
    col = lax.broadcasted_iota(jnp.int32, (PR, PR), 1)
    tri = jnp.where(col <= row, 0.0, neg_fill)
    for chunk in range(4):
        rows = slice(chunk * PR, (chunk + 1) * PR)
        query = q_ref[rows, :]
        outs, invs = [], []
        for head in range(2):
            masked = jnp.where(lane_half(head), query, jnp.zeros_like(query))
            scores = dot_nt(masked, k_ref[0:PLEN, :])
            if chunk < 2:
                scores = scores + bias_ref[rows, :]
                top = jnp.max(scores, axis=-1, keepdims=True)
                terms = jnp.exp(scores - top)
                total = jnp.sum(terms, axis=-1, keepdims=True)
                low_terms = terms.astype(BF)
                e_ref[head, rows, :] = low_terms
                out = dot_nn(low_terms, v_ref[0:PLEN, :])
            else:
                own = slice(PLEN + (chunk - 2) * PR, PLEN + (chunk - 1) * PR)
                near = dot_nt(masked, k_ref[own, :]) + tri
                top = jnp.maximum(
                    jnp.max(scores, axis=-1, keepdims=True), jnp.max(near, axis=-1, keepdims=True)
                )
                terms = jnp.exp(scores - top)
                near_terms = jnp.exp(near - top)
                total = jnp.sum(terms, axis=-1, keepdims=True) + jnp.sum(
                    near_terms, axis=-1, keepdims=True
                )
                low_terms = terms.astype(BF)
                low_near = near_terms.astype(BF)
                e_ref[head, rows, :] = low_terms
                ec_ref[head, (chunk - 2) * PR : (chunk - 1) * PR, :] = low_near
                out = dot_nn(low_terms, v_ref[0:PLEN, :]) + dot_nn(low_near, v_ref[own, :])
            inv = 1.0 / total
            outs.append(out * inv)
            invs.append(jnp.broadcast_to(inv, (PR, WIDTH)))
        low_half = lane_half(0)
        attended = jnp.where(low_half, outs[0], outs[1]).astype(BF)
        o_ref[rows, :] = attended
        att_ref[rows, at] = attended
        r_ref[rows, :] = jnp.where(low_half, invs[0], invs[1])

    @pl.when(step == PAIRS - 1)
    def _():
        wout = w_ref[1, :, D:HALF]
        gain = gain_row(w_ref[1, :, HALF:])
        for chunk in range(4):
            rows = slice(chunk * PR, (chunk + 1) * PR)
            from_row = chunk * PR if chunk < 2 else PLEN + (chunk - 2) * PR
            middle = x_ref[from_row : from_row + PR, :].astype(F32) + dot_nn(att_ref[rows, :], wout)
            mid_ref[rows, :] = middle
            nm_ref[rows, :] = (middle * rms_inv(middle) * gain).astype(BF)


def attn_fwd(where, x_all, pieces):
    pair = lambda i: (0, i)
    whole = lambda i: (0, 0)
    heads = lambda i: (i, 0, 0)
    anywhere = pl.BlockSpec(memory_space=pl.ANY)
    return pl.pallas_call(
        attn_fwd_kernel,
        grid=(PAIRS,),
        in_specs=[
            pl.BlockSpec(memory_space=pltpu.SMEM),
            pl.BlockSpec((KEYS, D), whole),
            *[anywhere] * 8,
        ],
        out_specs=[
            pl.BlockSpec((2, D, WIDE), lambda i: (0, 0, 0)),
            pl.BlockSpec((ROWS, WIDTH), pair),
            pl.BlockSpec((KEYS, WIDTH), pair),
            pl.BlockSpec((KEYS, WIDTH), pair),
            pl.BlockSpec((2, ROWS, PLEN), heads),
            pl.BlockSpec((2, 2 * PR, PR), heads),
            pl.BlockSpec((ROWS, WIDTH), pair),
            pl.BlockSpec((ROWS, WIDTH), pair),
            pl.BlockSpec((ROWS, D), whole),
            pl.BlockSpec((ROWS, D), whole),
            pl.BlockSpec((KEYS, D), whole),
        ],
        out_shape=[
            shape((2, D, WIDE), BF),
            shape((ROWS, D), BF),
            shape((KEYS, D), BF),
            shape((KEYS, D), BF),
            shape((HEADS, ROWS, PLEN), BF),
            shape((HEADS, 2 * PR, PR), BF),
            shape((ROWS, D), BF),
            shape((ROWS, D), F32),
            shape((ROWS, D), F32),
            shape((ROWS, D), BF),
            shape((KEYS, D), BF),
        ],
        scratch_shapes=[
            pltpu.VMEM((2 * PR, PLEN), F32),
            pltpu.VMEM((ROWS, D), BF),
            pltpu.SemaphoreType.DMA((64,)),
        ],
        compiler_params=params(),
        cost_estimate=pl.CostEstimate(
            flops=30_000_000_000, bytes_accessed=30_000_000, transcendentals=6_300_000
        ),
    )(where, x_all, *pieces)


def mlp_kernel(
    where_ref, nm0_ref, nm1_ref, g0_ref, g1_ref,
    up00_ref, up10_ref, up01_ref, up11_ref, down00_ref, down10_ref, down01_ref, down11_ref,
    e_ref, y_ref, give_e_ref, give_y_ref, up_keep_ref, up_give_ref, down_keep_ref, down_give_ref,
    wup_ref, wdown_ref, nm_ref, g_ref, acc_e_ref, acc_y_ref, part_ref, sems,
):
    step = pl.program_id(0)
    side, y_at = where_ref[1], where_ref[0] % 2

    @pl.when(step == 0)
    def _():
        copies = []
        for dy, ups, downs in (
            (0, (up00_ref, up10_ref), (down00_ref, down10_ref)),
            (1, (up01_ref, up11_ref), (down01_ref, down11_ref)),
        ):
            for dx in range(2):
                for i in range(4):
                    block = where_ref[8 + dy * 4 + i] * 2 + jnp.bitwise_xor(side, dx)
                    rows = pl.ds(pl.multiple_of(block * SUB, 16), SUB)
                    for half in range(2):
                        copies.append(
                            pltpu.make_async_copy(
                                ups[dx].at[i, pl.ds(half * SUB, SUB), :],
                                wup_ref.at[rows, pl.ds(half * D, D)],
                                sems.at[len(copies)],
                            )
                        )
                    copies.append(
                        pltpu.make_async_copy(
                            downs[dx].at[i],
                            wdown_ref.at[pl.ds(pl.multiple_of(block * FSUB, 16), FSUB), :],
                            sems.at[len(copies)],
                        )
                    )
        for copy in copies:
            copy.start()
        nm_ref[0:ROWS, :] = nm0_ref[...]
        nm_ref[ROWS:, :] = nm1_ref[...]
        g_ref[0:ROWS, :] = g0_ref[...]
        g_ref[ROWS:, :] = g1_ref[...]
        for copy in copies:
            copy.wait()

    at = pl.ds(pl.multiple_of(step * D, D), D)
    for block in range(2):
        rows = slice(block * ROWS, (block + 1) * ROWS)
        hidden = dot_nn(nm_ref[rows, :], wup_ref[:, at])
        square = hidden * hidden
        th = jnp.tanh(GELU_C * (hidden + GELU_A * square * hidden))
        left = 0.5 * (1.0 + th)
        active = (hidden * left).astype(BF)
        slope = left + 0.5 * hidden * (1.0 - th * th) * (GELU_C * (1.0 + 3.0 * GELU_A * square))
        d_hidden = (dot_nt(g_ref[rows, :], wdown_ref[at, :]) * slope).astype(BF)
        part_y = dot_nn(active, wdown_ref[at, :])
        part_e = dot_nt(d_hidden, wup_ref[:, at])
        d_down = dot_tn(active, g_ref[rows, :])
        d_up = dot_tn(nm_ref[rows, :], d_hidden)
        if block == 0:
            first_down, first_up = d_down, d_up
        else:
            part_ref[...] = (first_up + d_up).astype(BF).reshape(16, SUB, D)
            at_half = pl.ds(pl.multiple_of(step * SUB, 16), SUB)
            for s in range(8):
                up_keep_ref[s, at_half, :] = part_ref[2 * s + side]
                up_give_ref[s, at_half, :] = part_ref[2 * s + 1 - side]
            part_ref[...] = (first_down + d_down).astype(BF).reshape(16, SUB, D)
            for z in range(2):
                for x in range(2):
                    for h in range(2):
                        at_h = pl.ds(h * SUB, SUB)
                        row = 8 * z + 2 * x + h
                        down_keep_ref[z, x, at_h, :] = part_ref[row + 4 * y_at]
                        down_give_ref[z, x, at_h, :] = part_ref[row + 4 - 4 * y_at]

        @pl.when(step == 0)
        def _():
            acc_y_ref[rows, :] = part_y
            acc_e_ref[rows, :] = part_e

        @pl.when(step == 1)
        def _():
            if block == 0:
                e_ref[...] = (acc_e_ref[rows, :] + part_e).astype(BF)
                y_ref[...] = (acc_y_ref[rows, :] + part_y).astype(BF)
            else:
                give_e_ref[...] = (acc_e_ref[rows, :] + part_e).astype(BF)
                give_y_ref[...] = (acc_y_ref[rows, :] + part_y).astype(BF)


def mlp(where, normed, grads, pieces):
    whole = pl.BlockSpec((ROWS, D), lambda i: (0, 0))
    anywhere = pl.BlockSpec(memory_space=pl.ANY)
    return pl.pallas_call(
        mlp_kernel,
        grid=(2,),
        in_specs=[pl.BlockSpec(memory_space=pltpu.SMEM)] + [whole] * 4 + [anywhere] * 8,
        out_specs=[whole] * 4
        + [pl.BlockSpec((8, 2 * SUB, D), lambda i: (0, 0, 0))] * 2
        + [pl.BlockSpec((2, 2, FSUB, D), lambda i: (i, 0, 0, 0))] * 2,
        out_shape=[shape((ROWS, D), BF)] * 4
        + [shape((8, 2 * SUB, D), BF)] * 2
        + [shape((4, 2, FSUB, D), BF)] * 2,
        scratch_shapes=[
            pltpu.VMEM((D, FH), BF),
            pltpu.VMEM((FH, D), BF),
            pltpu.VMEM((2 * ROWS, D), BF),
            pltpu.VMEM((2 * ROWS, D), BF),
            pltpu.VMEM((2 * ROWS, D), F32),
            pltpu.VMEM((2 * ROWS, D), F32),
            pltpu.VMEM((16, SUB, D), BF),
            pltpu.SemaphoreType.DMA((48,)),
        ],
        compiler_params=params(),
        cost_estimate=pl.CostEstimate(
            flops=20_000_000_000, bytes_accessed=20_000_000, transcendentals=1_600_000
        ),
    )(where, *normed, *grads, *pieces)


def branch_kernel(
    mid_ref, g_ref, e0_ref, e1_ref, att_ref, w_ref, dmid_ref, datt_ref, right_ref,
    low_ref, prod_ref,
):
    gain = gain_row(w_ref[0, :, HALF:])
    wout = w_ref[0, :, D:HALF]
    for chunk in range(4):
        rows = slice(chunk * PR, (chunk + 1) * PR)
        middle = mid_ref[rows, :]
        inv = rms_inv(middle)
        unit = middle * inv
        grad = e0_ref[rows, :].astype(F32) + e1_ref[rows, :].astype(F32)
        scaled = gain * grad
        mean = jnp.mean(unit * scaled, axis=-1, keepdims=True)
        d_mid = g_ref[rows, :].astype(F32) + inv * (scaled - unit * mean)
        dmid_ref[rows, :] = d_mid
        prod_ref[rows, :] = (grad * unit).astype(BF)
        branch = d_mid.astype(BF)
        low_ref[rows, :] = branch
        datt_ref[rows, :] = dot_nt(branch, wout).astype(BF)
    right_ref[:, D:] = dot_tn(prod_ref[...], jnp.ones((ROWS, 128), BF)).astype(BF)
    right_ref[:, 0:D] = dot_tn(att_ref[...], low_ref[...]).astype(BF)


def branch(middle, d_out, own, given, attended, w_all):
    return pl.pallas_call(
        branch_kernel,
        grid=(1,),
        in_specs=[pl.BlockSpec((ROWS, D), lambda i: (0, 0))] * 5
        + [pl.BlockSpec((1, D, WIDE), lambda i: (1, 0, 0))],
        out_specs=[
            pl.BlockSpec((ROWS, D), lambda i: (0, 0)),
            pl.BlockSpec((ROWS, D), lambda i: (0, 0)),
            pl.BlockSpec((D, RIGHT), lambda i: (0, 0)),
        ],
        out_shape=[shape((ROWS, D), F32), shape((ROWS, D), BF), shape((D, RIGHT), BF)],
        scratch_shapes=[pltpu.VMEM((ROWS, D), BF), pltpu.VMEM((ROWS, D), BF)],
        compiler_params=params(),
        cost_estimate=pl.CostEstimate(
            flops=2_000_000_000, bytes_accessed=9_000_000, transcendentals=1000
        ),
    )(middle, d_out, own, given, attended, w_all)


def attn_bwd_kernel(units, *refs):
    first, last = units == (2,), units[0] == 0
    q_ref, g_ref, o_ref, r_ref, *refs = refs
    keyed = []
    for _ in units:
        keyed.append(refs[:3])
        refs = refs[3:]
    if last:
        ec_ref, kc_ref, vc_ref, *refs = refs
    if not first:
        dq_in_ref, *refs = refs
    wk_ref, wv_ref, *refs = refs
    if last:
        where_ref, wq_ref, x_ref, normed_ref, kv1_ref, kv2_ref, kv3_ref, *refs = refs
        f1_ref, f2_ref, f3_ref, right_ref, *refs = refs
        keep_ref, give_ref, f0_ref, fc_ref, *refs = refs
        dkv_ref, dq_ref, low_ref, high_ref, prod_ref, sems, *refs = refs
    else:
        dkv_refs, refs = refs[: len(units)], refs[len(units) :]
        f_refs, refs = refs[: len(units)], refs[len(units) :]
        dq_ref, *refs = refs
    qs_ref, gs_ref, ds_ref, *refs = refs
    if last:
        sum_ref, near_ref, near_e_ref, near_qs_ref, near_gs_ref = refs
    step = pl.program_id(0)
    if last:

        @pl.when(step == 0)
        def _():
            for at, ref in enumerate((kv1_ref, kv2_ref, kv3_ref)):
                rows = pl.ds((at + 1) * UNIT, UNIT)
                pltpu.make_async_copy(ref, dkv_ref.at[:, rows, :], sems.at[at]).start()
            high_ref[:, D:] = right_ref[...]

    low_half = lane_half(0)
    for pair in range(2):
        lanes = slice(pair * WIDTH, (pair + 1) * WIDTH)
        lanes_v = slice((2 + pair) * WIDTH, (3 + pair) * WIDTH)
        scaled_grad = g_ref[:, lanes].astype(F32) * r_ref[:, lanes]
        prod = scaled_grad * o_ref[:, lanes].astype(F32)
        low_grad = scaled_grad.astype(BF)
        query = q_ref[:, lanes]
        deltas = []
        for head in range(2):
            half = lane_half(head)
            rows = slice(head * ROWS, (head + 1) * ROWS)
            deltas.append(jnp.sum(jnp.where(half, prod, 0.0), axis=-1, keepdims=True))
            gs_ref[rows, :] = jnp.where(half, low_grad, jnp.zeros_like(low_grad))
            qs_ref[rows, :] = jnp.where(half, query, jnp.zeros_like(query))
        delta = jnp.concatenate(deltas, axis=0)
        d_query = None
        for u, (e_ref, k_ref, v_ref) in enumerate(keyed):
            out_ref = dkv_ref if last else dkv_refs[u]
            terms = e_ref[2 * pair : 2 * pair + 2].reshape(2 * ROWS, UNIT)
            d_soft = dot_nt(gs_ref[...], v_ref[:, lanes])
            ds_ref[...] = terms * (d_soft - delta).astype(BF)
            more = dot_nn(ds_ref[...], k_ref[:, lanes])
            d_query = more if d_query is None else d_query + more
            out_ref[step, 0:UNIT, lanes] = dot_tn(ds_ref[...], qs_ref[...]).astype(BF)
            out_ref[step, 0:UNIT, lanes_v] = dot_tn(terms, gs_ref[...]).astype(BF)
        total = jnp.where(low_half, d_query[0:ROWS], d_query[ROWS:])
        if not first:
            total = total + dq_in_ref[:, lanes]
        if not last:
            dq_ref[:, lanes] = total
            continue
        sum_ref[...] = total
        for side in range(2):
            own = slice(side * PR, (side + 1) * PR)
            mine = slice((2 + side) * PR, (3 + side) * PR)
            near_q = []
            for head in range(2):
                rows = slice(head * ROWS + mine.start, head * ROWS + mine.stop)
                at = slice(head * PR, (head + 1) * PR)
                near = ec_ref[2 * pair + head, own, :]
                d_soft = dot_nt(gs_ref[rows, :], vc_ref[own, lanes])
                near_ref[at, :] = near * (d_soft - deltas[head][mine]).astype(BF)
                near_e_ref[at, :] = near
                near_qs_ref[at, :] = qs_ref[rows, :]
                near_gs_ref[at, :] = gs_ref[rows, :]
                near_q.append(dot_nn(near_ref[at, :], kc_ref[own, lanes]))
            sum_ref[mine, :] += jnp.where(low_half, near_q[0], near_q[1])
            rows = slice(PLEN + side * PR, PLEN + (side + 1) * PR)
            dkv_ref[step, rows, lanes] = dot_tn(near_ref[...], near_qs_ref[...]).astype(BF)
            dkv_ref[step, rows, lanes_v] = dot_tn(near_e_ref[...], near_gs_ref[...]).astype(BF)
        dq_ref[step, :, lanes] = (sum_ref[...] * SCALE).astype(BF)

    def back_to_rows(dkv, rows):
        grad = None
        for i in range(3):
            at = slice(i * UNIT, (i + 1) * UNIT)
            more = dot_nt(dkv[i, rows, 0:UNIT], wk_ref[0, :, at])
            more = more + dot_nt(dkv[i, rows, UNIT:], wv_ref[0, :, at])
            grad = more if grad is None else grad + more
        return grad

    @pl.when(step == pl.num_programs(0) - 1)
    def _():
        if not last:
            for dkv, f_ref in zip(dkv_refs, f_refs):
                f_ref[...] = back_to_rows(dkv, slice(0, UNIT)).astype(BF)
            return
        for at, ref in enumerate((kv1_ref, kv2_ref, kv3_ref)):
            rows = pl.ds((at + 1) * UNIT, UNIT)
            pltpu.make_async_copy(ref, dkv_ref.at[:, rows, :], sems.at[at]).wait()
        for out_ref, rows, q_rows in (
            (f0_ref, slice(0, UNIT), slice(0, UNIT)),
            (fc_ref, slice(PLEN, KEYS), slice(UNIT, ROWS)),
        ):
            grad = back_to_rows(dkv_ref, rows)
            for i in range(3):
                at = slice(i * UNIT, (i + 1) * UNIT)
                grad = grad + dot_nt(dq_ref[i, q_rows, :], wq_ref[0, :, at])
            out_ref[...] = grad
        for at, f_ref in enumerate((f0_ref, f1_ref, f2_ref, f3_ref, fc_ref)):
            rows = slice(at * UNIT, (at + 1) * UNIT)
            tokens = x_ref[rows, :].astype(F32)
            prod_ref[rows, :] = (f_ref[...].astype(F32) * (tokens * rms_inv(tokens))).astype(BF)
        low_ref[:, HALF:] = dot_tn(prod_ref[...], jnp.ones((KEYS, 128), BF)).astype(BF)
        for i in range(3):
            at = slice(i * UNIT, (i + 1) * UNIT)
            low_ref[:, at] = (
                dot_tn(normed_ref[0:UNIT, :], dq_ref[i, 0:UNIT, :])
                + dot_tn(normed_ref[PLEN:, :], dq_ref[i, UNIT:, :])
            ).astype(BF)
            both = dot_tn(normed_ref[...], dkv_ref[i]).astype(BF)
            low_ref[:, D + i * UNIT : D + (i + 1) * UNIT] = both[:, 0:UNIT]
            high_ref[:, at] = both[:, UNIT:]

        for core, low_out, high_out in ((0, keep_ref, give_ref), (1, give_ref, keep_ref)):

            @pl.when(where_ref[2] == core)
            def _():
                copies = [
                    pltpu.make_async_copy(low_ref, low_out, sems.at[3]),
                    pltpu.make_async_copy(high_ref, high_out, sems.at[4]),
                ]
                for copy in copies:
                    copy.start()
                for copy in copies:
                    copy.wait()


def attn_bwd(units, saved, d_att, w_all, dq=None, rest=None):
    first, last = units == (2,), units[0] == 0
    q, k, v, e, ec, o, r = saved
    width = 2 * WIDTH
    lanes = lambda i: (0, i)
    full = lambda *dims: pl.BlockSpec(dims, lambda i: (0,) * len(dims))
    rows = pl.BlockSpec((ROWS, width), lanes)
    anywhere = pl.BlockSpec(memory_space=pl.ANY)
    weight = lambda half, at: pl.BlockSpec((1, D, D), lambda i: (half, 0, at))
    specs, args = [rows] * 4, [q, d_att, o, r]
    for u in units:
        specs += [
            pl.BlockSpec((4, ROWS, UNIT), lambda i, u=u: (i, 0, u)),
            pl.BlockSpec((UNIT, width), lambda i, u=u: (u, i)),
            pl.BlockSpec((UNIT, width), lambda i, u=u: (u, i)),
        ]
        args += [e, k, v]
    if last:
        specs += [
            pl.BlockSpec((4, UNIT, PR), lambda i: (i, 0, 0)),
            pl.BlockSpec((UNIT, width), lambda i: (4, i)),
            pl.BlockSpec((UNIT, width), lambda i: (4, i)),
        ]
        args += [ec, k, v]
    if not first:
        specs.append(rows)
        args.append(dq)
    specs += [weight(0, 1), weight(1, 0)]
    args += [w_all, w_all]
    kv = (3, UNIT, 2 * UNIT)
    if last:
        where, x_all, normed, kvs, fs, right = rest
        specs += [pl.BlockSpec(memory_space=pltpu.SMEM), weight(0, 0)]
        specs += [full(KEYS, D), full(KEYS, D)] + [anywhere] * 3 + [full(UNIT, D)] * 3 + [full(D, RIGHT)]
        args += [where, w_all, x_all, normed, *kvs, *fs, right]
        outs = [anywhere, anywhere, full(UNIT, D), full(UNIT, D)]
        out_shapes = [shape((D, WIDE), BF)] * 2 + [shape((UNIT, D), F32)] * 2
        scratch = [
            pltpu.VMEM((3, KEYS, 2 * UNIT), BF),
            pltpu.VMEM((3, ROWS, UNIT), BF),
            pltpu.VMEM((D, WIDE), BF),
            pltpu.VMEM((D, WIDE), BF),
            pltpu.VMEM((KEYS, D), BF),
            pltpu.SemaphoreType.DMA((5,)),
        ]
    else:
        outs = [full(*kv)] * len(units) + [full(UNIT, D)] * len(units) + [rows]
        out_shapes = [shape(kv, BF)] * len(units) + [shape((UNIT, D), BF)] * len(units)
        out_shapes.append(shape((ROWS, D), F32))
        scratch = []
    return pl.pallas_call(
        lambda *refs: attn_bwd_kernel(units, *refs),
        grid=(3,),
        in_specs=specs,
        out_specs=outs,
        out_shape=out_shapes,
        scratch_shapes=scratch
        + [
            pltpu.VMEM((2 * ROWS, WIDTH), BF),
            pltpu.VMEM((2 * ROWS, WIDTH), BF),
            pltpu.VMEM((2 * ROWS, UNIT), BF),
        ]
        + ([pltpu.VMEM((ROWS, WIDTH), F32)] + [pltpu.VMEM((UNIT, WIDTH), BF)] * 4 if last else []),
        compiler_params=params(),
        cost_estimate=pl.CostEstimate(
            flops=10_000_000_000 * (len(units) + last), bytes_accessed=10_000_000, transcendentals=1000
        ),
    )(*args)


def tail_kernel(x_ref, f0_ref, f1_ref, f2_ref, f3_ref, fc_ref, dmid_ref, w_ref, keep_ref, give_ref):
    gain = gain_row(w_ref[0])
    for chunk in range(4):
        rows = slice(chunk * PR, (chunk + 1) * PR)
        part = x_ref[rows, :].astype(F32)
        inv = rms_inv(part)
        unit = part * inv
        if chunk < 2:
            grad = f0_ref[rows, :].astype(F32)
            for f_ref in (f1_ref, f2_ref, f3_ref):
                grad = grad + f_ref[rows, :].astype(F32)
        else:
            grad = fc_ref[(chunk - 2) * PR : (chunk - 1) * PR, :]
        scaled = gain * grad
        mean = jnp.mean(unit * scaled, axis=-1, keepdims=True)
        out_ref = give_ref if chunk % 2 else keep_ref
        at = slice(chunk // 2 * PR, (chunk // 2 + 1) * PR)
        out_ref[at, :] = (dmid_ref[rows, :] + inv * (scaled - unit * mean)).astype(out_ref.dtype)


def tail(x_own, f_parts, f_cont, d_mid, w_all):
    whole = lambda i: (0, 0)
    half = pl.BlockSpec((2 * PR, D), whole)
    full = pl.BlockSpec((ROWS, D), whole)
    return pl.pallas_call(
        tail_kernel,
        grid=(1,),
        in_specs=[full, half, half, half, half, half, full]
        + [pl.BlockSpec((1, D, 128), lambda i: (0, 0, HALF // 128))],
        out_specs=[half, half],
        out_shape=[shape((2 * PR, D), F32), shape((2 * PR, D), BF)],
        compiler_params=params(),
        cost_estimate=pl.CostEstimate(flops=20_000_000, bytes_accessed=7_000_000, transcendentals=1000),
    )(x_own, *f_parts, f_cont, d_mid, w_all)


def total_of(*parts):
    total = parts[0].astype(F32)
    for part in parts[1:]:
        total = total + part.astype(F32)
    return total.astype(BF)


def run_whole(kernel, outs, *args):
    return pl.pallas_call(
        kernel,
        in_specs=[pl.BlockSpec(memory_space=pltpu.SMEM)]
        + [pl.BlockSpec(memory_space=pltpu.VMEM)] * (len(args) - 1),
        out_specs=[pl.BlockSpec(memory_space=pltpu.VMEM)] * len(outs),
        out_shape=[shape(dims, BF) for dims in outs],
        compiler_params=params(),
        cost_estimate=pl.CostEstimate(flops=1_000_000, bytes_accessed=7_000_000, transcendentals=0),
    )(*args)


def fold_two_kernel(where_ref, a0_ref, a1_ref, b0_ref, b1_ref, ak_ref, ag_ref, bk_ref, bg_ref):
    y_at, side = where_ref[0] % 2, where_ref[1]
    for z in range(4):
        ak_ref[z] = total_of(a0_ref[z, y_at], a1_ref[z, y_at])
        ag_ref[z] = total_of(a0_ref[z, 1 - y_at], a1_ref[z, 1 - y_at])
        bk_ref[z] = total_of(b0_ref[z, side], b1_ref[z, side])
        bg_ref[z] = total_of(b0_ref[z, 1 - side], b1_ref[z, 1 - side])


def fold_rows_kernel(where_ref, a0_ref, a1_ref, b0_ref, b1_ref, *outs):
    z_at = where_ref[0] // 2
    rows = a0_ref.shape[1]
    for step, out_ref in enumerate(outs):
        z = jnp.bitwise_xor(z_at, step)
        out_ref[0:rows, :] = total_of(a0_ref[z], a1_ref[z])
        out_ref[rows:, :] = total_of(b0_ref[z], b1_ref[z])


def fold_cols_kernel(where_ref, a0_ref, a1_ref, b0_ref, b1_ref, *outs):
    z_at = where_ref[0] // 2
    cols = a0_ref.shape[2]
    for step, out_ref in enumerate(outs):
        z = jnp.bitwise_xor(z_at, step)
        out_ref[:, 0:cols] = total_of(a0_ref[z], a1_ref[z])
        out_ref[:, cols:] = total_of(b0_ref[z], b1_ref[z])


def fold_core_kernel(where_ref, own_ref, got_ref, ak_ref, ag_ref, bk_ref, bg_ref):
    y_at, side = where_ref[0] % 2, where_ref[1]
    left, right = slice(0, LEFT), slice(LEFT, WIDE)

    def block(s, x, cols):
        rows = pl.ds(pl.multiple_of((2 * s + x) * SUB, 16), SUB)
        return total_of(own_ref[rows, cols], got_ref[rows, cols])

    for s in range(8):
        ak_ref[s // 2, s % 2] = block(s, side, left)
        ag_ref[s // 2, s % 2] = block(s, 1 - side, left)
    for z in range(4):
        for x in range(2):
            bk_ref[z, x] = block(2 * z + y_at, x, right)
            bg_ref[z, x] = block(2 * z + 1 - y_at, x, right)


def over(axis, value, bits):
    return lax.ppermute(value, axis, [(i, i ^ bits) for i in range(lax.axis_size(axis))])


def cut(values, start, rows=PR):
    return lax.dynamic_slice_in_dim(values, start, rows, 0)


def pick(values, at):
    return lax.dynamic_index_in_dim(values, at, 0, keepdims=False)


def pick_of(values, at, axis):
    return lax.dynamic_index_in_dim(values, at, axis, keepdims=False)


def tie(*values):
    return lax.optimization_barrier(values)


def per_device(tokens, w_qkv, w_out, w_up, w_down, gain_attn, gain_mlp, d_out):
    staged = lax.axis_size("shard") == 8
    shard = lax.axis_index("shard")
    rep = lax.axis_index("rep")
    side, core = rep // 2, rep % 2
    pos = shard % 8
    y_at, z_at = pos % 2, pos // 2
    table = [pos ^ d for d in ORDER] if staged else [jnp.int32(2 * (d % 4) + d // 4) for d in range(8)]
    where = jnp.stack([pos, side, core] + [jnp.int32(0)] * 5 + table).astype(jnp.int32)

    def to_give(values):
        return jnp.concatenate([cut(values, (1 - y_at) * PR), cut(values, (3 - y_at) * PR)], axis=0)

    def own_rows(values, got):
        mine_p, mine_c = cut(values, y_at * PR), cut(values, (2 + y_at) * PR)
        return jnp.concatenate([mine_p, got[:PR], mine_c, got[PR:]], axis=0)

    def to_return(values):
        return jnp.concatenate([values[PR : 2 * PR], values[3 * PR :]], axis=0)

    def home_rows(keep_p, keep_c, got):
        got = got.astype(keep_p.dtype)
        first = y_at == 0
        return jnp.concatenate(
            [
                jnp.where(first, keep_p, got[:PR]),
                jnp.where(first, got[:PR], keep_p),
                jnp.where(first, keep_c, got[PR:]),
                jnp.where(first, got[PR:], keep_c),
            ],
            axis=0,
        )

    def halves(qkv, out, gain_a, gain_m):
        wide = lambda gain: jnp.broadcast_to(gain[:, None], (gain.shape[0], 128))
        return (
            jnp.concatenate([qkv[:, :HALF], wide(gain_a)], axis=1),
            jnp.concatenate([qkv[:, HALF:], out, wide(gain_m)], axis=1),
        )

    def half_up(up):
        return pick_of(up.reshape(up.shape[0], 8, 2, 2 * FSUB), core, 2).reshape(up.shape[0], FH)

    def own_up(up):
        mine = half_up(cut(up, side * SUB, SUB))
        return jnp.concatenate([mine[:, :D], mine[:, D:]], axis=0)

    if staged:
        low, high = halves(w_qkv, w_out, gain_attn, gain_mlp)
        own_piece = cut(jnp.where(core == 0, low, high), side * SUB, SUB)
        own_mlp = jnp.concatenate(
            [own_up(w_up), cut(w_down, core * 2 * FSUB + side * FSUB, FSUB)], axis=0
        )
        t_got, z1, z2, z3 = tie(
            over("shard", to_give(tokens), 1),
            *[over("shard", own_piece, k) for k in (2, 4, 6)],
        )
        x_own = own_rows(tokens, t_got)
        near = x_own[: 2 * PR]
        line = (own_piece, z1, z2, z3)
        left = jnp.stack([part[:, :LEFT] for part in line])
        right = jnp.stack([part[:, LEFT:] for part in line])
        own_mlp, left, right, near = tie(own_mlp, left, right, near)
        m1, m2, m3, left_y, right_x, g_got = tie(
            *[over("shard", own_mlp, k) for k in (2, 4, 6)],
            over("shard", left, 1),
            over("rep", right, 2),
            over("shard", to_give(d_out), 1),
        )
        left = jnp.concatenate([left, left_y], axis=0)
        right = jnp.concatenate([right, right_x], axis=0)
        mlp_line = (own_mlp, m1, m2, m3)
        up = jnp.stack([part[: 2 * SUB] for part in mlp_line])
        down = jnp.stack([part[2 * SUB :] for part in mlp_line])
        near, left, right, up, down = tie(near, left, right, up, down)
        near1, near2, near3, left_x, right_y, up_y, down_x = tie(
            *[over("shard", near, k) for k in (2, 4, 6)],
            over("rep", left, 2),
            over("shard", right, 1),
            over("shard", up, 1),
            over("rep", down, 2),
        )
        pieces = tie(
            left, left_x, over("rep", left, 1), over("rep", left_x, 1),
            right, right_y, over("rep", right, 1), over("rep", right_y, 1),
        )
        up, up_y, down, down_x, pieces = tie(up, up_y, down, down_x, pieces)
        mlp_pieces = (
            up, over("rep", up, 2), up_y, over("rep", up_y, 2),
            down, down_x, over("shard", down, 1), over("shard", down_x, 1),
        )
    else:
        gathered = [
            lax.all_gather(w, "shard", axis=0, tiled=True)
            for w in (w_qkv, w_out, gain_attn, gain_mlp, w_up, w_down)
        ]
        natural = jnp.stack(halves(*gathered[:4])).reshape(2, 4, 2, 2, SUB, WIDE)
        pieces = []
        for dc in (0, 1):
            by_core = pick(natural, core ^ dc)
            for dx in (0, 1):
                both = pick_of(by_core[..., :LEFT], side ^ dx, 2)
                pieces.append(jnp.concatenate([both[:, 0], both[:, 1]], axis=0))
        for dc in (0, 1):
            by_core = pick(natural, core ^ dc)[..., LEFT:]
            for dy in (0, 1):
                both = [pick_of(by_core[:, dy], side ^ dx, 1) for dx in (0, 1)]
                pieces.append(jnp.concatenate(both, axis=0))
        pieces = tuple(pieces)
        up = half_up(gathered[4]).reshape(4, 2, 2, SUB, 2, D).transpose(1, 0, 2, 4, 3, 5)
        up = up.reshape(2, 4, 2, 2 * SUB, D)
        down = pick_of(gathered[5].reshape(4, 2, 2, 2, FSUB, D), core, 2).transpose(1, 0, 2, 3, 4)
        mlp_pieces = tuple(
            pick_of(both[dy], side ^ dx, 1) for both in (up, down) for dy in (0, 1) for dx in (0, 1)
        )
        x_own = own_rows(tokens, over("shard", to_give(tokens), 1))
        near = x_own[: 2 * PR]
        near1, near2, near3 = [over("shard", near, k) for k in (2, 4, 6)]
        g_got = over("shard", to_give(d_out), 1)
    x_all = jnp.concatenate([near, near1, near2, near3, x_own[2 * PR :]], axis=0)
    g_own = own_rows(d_out, g_got)
    x_all, g_own = tie(x_all, g_own)

    g_core = over("rep", g_own, 1)
    forward = attn_fwd(where, x_all, pieces)
    forward, mlp_pieces, g_core = tie(forward, mlp_pieces, g_core)
    w_all, q, k, v, e, ec, attended, inv_sum, middle, nm, normed = forward

    nm_core, nm = tie(over("rep", nm, 1), nm)
    e_own, y_own, e_give, y_give, *mlp_grads = mlp(
        where, (nm, nm_core), (g_own, g_core), mlp_pieces
    )
    e_got, y_give, mlp_grads = tie(over("rep", e_give, 1), y_give, mlp_grads)
    up_keep, up_give, down_keep, down_give = mlp_grads
    y_got = over("rep", y_give, 1)
    if staged:
        up_got, down_got = over("rep", up_give, 2), over("shard", down_give, 1)
    d_mid, d_att, d_right = branch(middle, g_own, e_own, e_got, attended, w_all)

    saved = (q, k, v, e, ec, attended, inv_sum)
    kv2, f2_give, dq = attn_bwd((2,), saved, d_att, w_all)
    y_got, dq = tie(y_got, dq)
    block_rows = (middle + y_own.astype(F32) + y_got.astype(F32)).astype(BF)
    block_give = to_return(block_rows)
    if staged:
        up_got, down_got, dq, f2_give = tie(up_got, down_got, dq, f2_give)
        by_pair = (4, 2, 2 * SUB, D)
        folded = run_whole(
            fold_two_kernel, [(4, 2 * SUB, D)] * 4, where,
            up_keep.reshape(by_pair), up_got.reshape(by_pair), down_keep, down_got,
        )
        (up_keep, up_give, down_keep, down_give), dq, block_give = tie(folded, dq, block_give)
        up_got, down_got = over("shard", up_give, 1), over("rep", down_give, 2)
    f2 = over("shard", f2_give, 4)
    kv3, kv1, f3_give, f1_give, dq = attn_bwd((3, 1), saved, d_att, w_all, dq)
    f2, f3_give, f1_give, dq, block_give = tie(f2, f3_give, f1_give, dq, block_give)
    if staged:
        up_got, down_got, dq = tie(up_got, down_got, dq)
    f1, f3, b_got = over("shard", f1_give, 2), over("shard", f3_give, 6), over("shard", block_give, 1)
    keep, give, f0, f_cont = attn_bwd(
        (0,), saved, d_att, w_all, dq,
        (where, x_all, normed, (kv1, kv2, kv3), (f1_give, f2_give, f3_give), d_right),
    )
    f1, f3, b_got, keep, give, f0, f_cont = tie(f1, f3, b_got, keep, give, f0, f_cont)
    if staged:
        mlp_total, *mlp_gives = run_whole(
            fold_rows_kernel, [(4 * SUB, D)] * 4, where, up_keep, up_got, down_keep, down_got
        )
        chip_got, m1, mlp_gives = tie(
            over("rep", give, 1), over("shard", mlp_gives[0], 2), mlp_gives
        )
        left, right = (4, 2, SUB, LEFT), (4, 2, SUB, WIDE - LEFT)
        left_keep, left_give, right_keep, right_give = run_whole(
            fold_core_kernel, [left, left, right, right], where, keep, chip_got
        )
        left_give, right_give, mlp_gives = tie(left_give, right_give, mlp_gives)
        left_got, right_got, m2, mlp_gives = tie(
            over("rep", left_give, 2),
            over("shard", right_give, 1),
            over("shard", mlp_gives[1], 4),
            mlp_gives,
        )
        left_keep, left_give, right_keep, right_give = run_whole(
            fold_two_kernel,
            [(4, SUB, LEFT)] * 2 + [(4, SUB, WIDE - LEFT)] * 2,
            where, left_keep, left_got, right_keep, right_got,
        )
        left_got, right_got, m3, f1, f2, f3 = tie(
            over("shard", left_give, 1),
            over("rep", right_give, 2),
            over("shard", mlp_gives[2], 6),
            f1,
            f2,
            f3,
        )
        total, *gives = run_whole(
            fold_cols_kernel, [(SUB, WIDE)] * 4, where, left_keep, left_got, right_keep, right_got
        )
        gives, m3, token_keep, token_give = tie(
            gives, m3, *tail(x_own, (f0, f1, f2, f3), f_cont, d_mid, w_all)
        )
        mlp_total = total_of(mlp_total, m1, m2, m3)
        z1, z2, z3, m_got, mlp_total, t_got = tie(
            *[over("shard", gives[step - 1], 2 * step) for step in (1, 2, 3)],
            over("rep", mlp_total, 2),
            mlp_total,
            over("shard", token_give, 1),
        )
        by_side = jnp.stack([mlp_total, m_got])
        total = total_of(total, z1, z2, z3)
        other, core_got, m_got, by_side = tie(
            over("rep", total, 2), over("rep", total, 1), over("rep", by_side, 1), by_side
        )
        rest = over("rep", other, 1)
        first, near_side = core == 0, side == 0
        arrange = lambda a, b: jnp.concatenate(
            [jnp.where(near_side, a, b), jnp.where(near_side, b, a)], axis=0
        )
        mine, theirs = arrange(total, other), arrange(core_got, rest)
        low = jnp.where(first, mine, theirs).astype(F32)
        high = jnp.where(first, theirs, mine).astype(F32)
        by_core = jnp.stack([by_side, m_got])
        by_core = jnp.stack([pick(by_core, core), pick(by_core, 1 - core)])
        by_core = jnp.stack([pick_of(by_core, side, 1), pick_of(by_core, 1 - side, 1)])
        d_wup = by_core[:, :, : 2 * SUB].reshape(2, 2, 2, SUB, 4, 2 * FSUB)
        d_wup = d_wup.transpose(0, 3, 2, 4, 1, 5).reshape(2 * SUB, FF).astype(F32)
        d_wdown = by_core[:, :, 2 * SUB :].transpose(1, 0, 2, 3).reshape(4 * FSUB, D).astype(F32)
    else:
        token_keep, token_give = tail(x_own, (f0, f1, f2, f3), f_cont, d_mid, w_all)
        t_got = over("shard", token_give, 1)
        low, high = jnp.where(core == 0, keep, give), jnp.where(core == 0, give, keep)

        def by_side_of(keep, give, at):
            first = at == 0
            return jnp.stack([jnp.where(first, keep, give), jnp.where(first, give, keep)])

        up = by_side_of(up_keep, up_give, side).reshape(2, 8, 2, SUB, D)
        up = up.transpose(1, 0, 3, 2, 4).reshape(D, 8, 1, 2 * FSUB)
        down = by_side_of(down_keep, down_give, y_at).transpose(1, 0, 2, 3, 4)
        down = down.reshape(8, 1, 2 * FSUB, D)
        peer_up, peer_down = over("rep", up, 1), over("rep", down, 1)
        first = core == 0
        up, peer_up = jnp.where(first, up, peer_up), jnp.where(first, peer_up, up)
        down, peer_down = jnp.where(first, down, peer_down), jnp.where(first, peer_down, down)
        up = jnp.concatenate([up, peer_up], axis=2).reshape(D, FF)
        down = jnp.concatenate([down, peer_down], axis=1).reshape(FF, D)
        rest = lambda v: (v.astype(F32) + over("rep", v, 2).astype(F32)).astype(BF)
        up, down = rest(up), rest(down)
        scatter = lambda v: lax.psum_scatter(v, "shard", scatter_dimension=0, tiled=True)
        d_wup, d_wdown = scatter(up).astype(F32), scatter(down).astype(F32)
        low = lax.psum(scatter(low), "rep").astype(F32)
        high = lax.psum(scatter(high), "rep").astype(F32)

    return (
        home_rows(block_rows[:PR], block_rows[2 * PR : 3 * PR], b_got),
        home_rows(token_keep[:PR], token_keep[PR:], t_got),
        jnp.concatenate([low[:, :HALF], high[:, :D]], axis=1),
        high[:, D:HALF],
        d_wup,
        d_wdown,
        low[:, HALF],
        high[:, HALF],
    )


def solution(mesh):
    weights = P("shard", None)
    rows = P(("rep", "shard"), None)
    return jax.shard_map(
        per_device,
        mesh=mesh,
        in_specs=(rows, weights, weights, weights, weights, P("shard"), P("shard"), rows),
        out_specs=(rows, rows, weights, weights, weights, weights, P("shard"), P("shard")),
        check_vma=False,
    )
```

```python
import jax
import jax.numpy as jnp
from jax import lax
from jax.experimental import pallas as pl
from jax.experimental.pallas import tpu as pltpu
from jax.sharding import PartitionSpec as P

D = 768
HEADS = 12
HDIM = 64
FF = 3072
PR = 128
PLEN = 1024
KEYS = PLEN + 2 * PR
ROWS = 4 * PR
PAIRS = HEADS // 2
WIDTH = 2 * HDIM
HALF = 1536
WIDE = HALF + 128
SUB = 48
LEFT = 896
RIGHT = D + 128
UNIT = 2 * PR
FSUB = 96
FH = FF // 2
norm_eps = 1e-05
neg_fill = -1e30
SCALE = HDIM ** (-0.5)
GELU_C = 0.7978845608028654
GELU_A = 0.044715
BF = jnp.bfloat16
F32 = jnp.float32
VMEM_LIMIT = 60 * 1024 * 1024
BLOCKS = (0, 1, 2, 3, 4, 5, 6, 7)
ORDER = (0, 2, 4, 6, 1, 3, 5, 7)


def dot_nt(a, b):
    return lax.dot_general(a, b, (((1,), (1,)), ((), ())), preferred_element_type=F32)


def dot_tn(a, b):
    return lax.dot_general(a, b, (((0,), (0,)), ((), ())), preferred_element_type=F32)


def dot_nn(a, b):
    return jnp.dot(a, b, preferred_element_type=F32)


def rms_inv(values):
    return lax.rsqrt(jnp.mean(values * values, axis=-1, keepdims=True) + norm_eps)


def params():
    return pltpu.CompilerParams(vmem_limit_bytes=VMEM_LIMIT)


def shape(dims, dtype):
    return jax.ShapeDtypeStruct(dims, dtype)


def fill_normed(x_ref, gain, normed_ref):
    @pl.loop(0, KEYS, step=PR)
    def _(row):
        rows = pl.ds(pl.multiple_of(row, PR), PR)
        part = x_ref[rows, :].astype(F32)
        normed_ref[rows, :] = (part * rms_inv(part) * gain).astype(BF)


def lane_half(head):
    lanes = lax.broadcasted_iota(jnp.int32, (1, WIDTH), 1)
    return (lanes >= HDIM) if head else (lanes < HDIM)


def gain_row(column):
    return column.astype(F32).T[0:1, :]


def attn_fwd_kernel(
    where_ref, x_ref, l00_ref, l10_ref, l01_ref, l11_ref, r00_ref, r10_ref, r01_ref, r11_ref,
    w_ref, q_ref, k_ref, v_ref, e_ref, ec_ref, o_ref, r_ref, mid_ref, nm_ref, normed_ref,
    bias_ref, att_ref, qs_ref, s_ref, inv_ref, out_ref, sems,
):
    step = pl.program_id(0)

    @pl.when(step == 0)
    def _():
        side, core = where_ref[1], where_ref[2]
        copies = []
        for at, (dx, dc, piece) in enumerate(
            ((0, 0, l00_ref), (1, 0, l10_ref), (0, 1, l01_ref), (1, 1, l11_ref))
        ):
            for i in range(8):
                start = where_ref[8 + i] * (2 * SUB) + jnp.bitwise_xor(side, dx) * SUB
                copies.append(
                    pltpu.make_async_copy(
                        piece.at[i],
                        w_ref.at[
                            jnp.bitwise_xor(core, dc),
                            pl.ds(pl.multiple_of(start, 16), SUB),
                            pl.ds(0, LEFT),
                        ],
                        sems.at[at * 8 + i],
                    )
                )
        for at, (far, dc, piece) in enumerate(
            ((0, 0, r00_ref), (1, 0, r10_ref), (0, 1, r01_ref), (1, 1, r11_ref))
        ):
            for i in range(8):
                start = where_ref[8 + far * 4 + i % 4] * (2 * SUB)
                start = start + jnp.bitwise_xor(side, i // 4) * SUB
                copies.append(
                    pltpu.make_async_copy(
                        piece.at[i],
                        w_ref.at[
                            jnp.bitwise_xor(core, dc),
                            pl.ds(pl.multiple_of(start, 16), SUB),
                            pl.ds(LEFT, WIDE - LEFT),
                        ],
                        sems.at[32 + at * 8 + i],
                    )
                )
        for copy in copies:
            copy.start()
        pos = where_ref[0]
        row = lax.broadcasted_iota(jnp.int32, (PR, PR), 0)
        col = lax.broadcasted_iota(jnp.int32, (PR, PR), 1)
        tri = jnp.where(col <= row, 0.0, neg_fill)
        for part in range(2):
            mine = jnp.bitwise_xor(pos, BLOCKS[part])
            for block in range(8):
                at = (pl.ds(part * PR, PR), pl.ds(block * PR, PR))
                if block == part:
                    bias_ref[at] = tri
                else:
                    seen = jnp.bitwise_xor(pos, BLOCKS[block]) < mine
                    bias_ref[at] = jnp.full((PR, PR), jnp.where(seen, 0.0, neg_fill), F32)
        for copy in copies:
            copy.wait()
        fill_normed(x_ref, gain_row(w_ref[0, :, HALF:]), normed_ref)

    at = pl.ds(pl.multiple_of(step * UNIT, UNIT), UNIT)
    at_k = pl.ds(pl.multiple_of(D + step * UNIT, UNIT), UNIT)
    k_ref[...] = dot_nn(normed_ref[...], w_ref[0, :, at_k]).astype(BF)
    v_ref[...] = dot_nn(normed_ref[...], w_ref[1, :, at]).astype(BF)
    wq = w_ref[0, :, at]
    q_ref[0:UNIT, :] = (dot_nn(normed_ref[0:UNIT, :], wq) * SCALE).astype(BF)
    q_ref[UNIT:, :] = (dot_nn(normed_ref[PLEN:, :], wq) * SCALE).astype(BF)
    row = lax.broadcasted_iota(jnp.int32, (PR, PR), 0)
    col = lax.broadcasted_iota(jnp.int32, (PR, PR), 1)
    tri = jnp.where(col <= row, 0.0, neg_fill)
    low_half = lane_half(0)
    for pair in range(2):
        lanes = slice(pair * WIDTH, (pair + 1) * WIDTH)
        query = q_ref[:, lanes]
        for head in range(2):
            rows = slice(head * ROWS, (head + 1) * ROWS)
            qs_ref[rows, :] = jnp.where(lane_half(head), query, jnp.zeros_like(query))
        s_ref[...] = dot_nt(qs_ref[...], k_ref[0:PLEN, lanes])
        for head in range(2):
            for chunk in range(4):
                mine = slice(chunk * PR, (chunk + 1) * PR)
                rows = slice(head * ROWS + chunk * PR, head * ROWS + (chunk + 1) * PR)
                scores = s_ref[rows, :]
                if chunk < 2:
                    scores = scores + bias_ref[mine, :]
                    top = jnp.max(scores, axis=-1, keepdims=True)
                    terms = jnp.exp(scores - top)
                    total = jnp.sum(terms, axis=-1, keepdims=True)
                else:
                    own = slice(PLEN + (chunk - 2) * PR, PLEN + (chunk - 1) * PR)
                    near = dot_nt(qs_ref[rows, :], k_ref[own, lanes]) + tri
                    top = jnp.maximum(
                        jnp.max(scores, axis=-1, keepdims=True),
                        jnp.max(near, axis=-1, keepdims=True),
                    )
                    terms = jnp.exp(scores - top)
                    near_terms = jnp.exp(near - top)
                    total = jnp.sum(terms, axis=-1, keepdims=True) + jnp.sum(
                        near_terms, axis=-1, keepdims=True
                    )
                    ec_ref[2 * pair + head, (chunk - 2) * PR : (chunk - 1) * PR, :] = (
                        near_terms.astype(BF)
                    )
                e_ref[2 * pair + head, mine, :] = terms.astype(BF)
                inv_ref[rows, :] = jnp.broadcast_to(1.0 / total, (PR, WIDTH))
        terms = e_ref[2 * pair : 2 * pair + 2].reshape(2 * ROWS, PLEN)
        out_ref[...] = dot_nn(terms, v_ref[0:PLEN, lanes])
        for head in range(2):
            for side in range(2):
                own = slice(PLEN + side * PR, PLEN + (side + 1) * PR)
                start = head * ROWS + (2 + side) * PR
                near = ec_ref[2 * pair + head, side * PR : (side + 1) * PR, :]
                out_ref[start : start + PR, :] += dot_nn(near, v_ref[own, lanes])
        inv = jnp.where(low_half, inv_ref[0:ROWS, :], inv_ref[ROWS:, :])
        r_ref[:, lanes] = inv
        o_ref[:, lanes] = (
            jnp.where(low_half, out_ref[0:ROWS, :], out_ref[ROWS:, :]) * inv
        ).astype(BF)
    att_ref[step] = o_ref[...]

    @pl.when(step == pl.num_programs(0) - 1)
    def _():
        wout = w_ref[1, :, D:HALF]
        gain = gain_row(w_ref[1, :, HALF:])
        for chunk in range(4):
            rows = slice(chunk * PR, (chunk + 1) * PR)
            from_row = chunk * PR if chunk < 2 else PLEN + (chunk - 2) * PR
            middle = x_ref[from_row : from_row + PR, :].astype(F32)
            for i in range(3):
                middle = middle + dot_nn(att_ref[i, rows, :], wout[i * UNIT : (i + 1) * UNIT, :])
            mid_ref[rows, :] = middle
            nm_ref[rows, :] = (middle * rms_inv(middle) * gain).astype(BF)


def attn_fwd(where, x_all, pieces):
    pair = lambda i: (0, i)
    whole = lambda i: (0, 0)
    heads = lambda i: (i, 0, 0)
    anywhere = pl.BlockSpec(memory_space=pl.ANY)
    return pl.pallas_call(
        attn_fwd_kernel,
        grid=(3,),
        in_specs=[
            pl.BlockSpec(memory_space=pltpu.SMEM),
            pl.BlockSpec((KEYS, D), whole),
            *[anywhere] * 8,
        ],
        out_specs=[
            pl.BlockSpec((2, D, WIDE), lambda i: (0, 0, 0)),
            pl.BlockSpec((ROWS, UNIT), pair),
            pl.BlockSpec((KEYS, UNIT), pair),
            pl.BlockSpec((KEYS, UNIT), pair),
            pl.BlockSpec((4, ROWS, PLEN), heads),
            pl.BlockSpec((4, UNIT, PR), heads),
            pl.BlockSpec((ROWS, UNIT), pair),
            pl.BlockSpec((ROWS, UNIT), pair),
            pl.BlockSpec((ROWS, D), whole),
            pl.BlockSpec((ROWS, D), whole),
            pl.BlockSpec((KEYS, D), whole),
        ],
        out_shape=[
            shape((2, D, WIDE), BF),
            shape((ROWS, D), BF),
            shape((KEYS, D), BF),
            shape((KEYS, D), BF),
            shape((HEADS, ROWS, PLEN), BF),
            shape((HEADS, 2 * PR, PR), BF),
            shape((ROWS, D), BF),
            shape((ROWS, D), F32),
            shape((ROWS, D), F32),
            shape((ROWS, D), BF),
            shape((KEYS, D), BF),
        ],
        scratch_shapes=[
            pltpu.VMEM((2 * PR, PLEN), F32),
            pltpu.VMEM((3, ROWS, UNIT), BF),
            pltpu.VMEM((2 * ROWS, WIDTH), BF),
            pltpu.VMEM((2 * ROWS, PLEN), F32),
            pltpu.VMEM((2 * ROWS, WIDTH), F32),
            pltpu.VMEM((2 * ROWS, WIDTH), F32),
            pltpu.SemaphoreType.DMA((64,)),
        ],
        compiler_params=params(),
        cost_estimate=pl.CostEstimate(
            flops=30_000_000_000, bytes_accessed=30_000_000, transcendentals=6_300_000
        ),
    )(where, x_all, *pieces)


def mlp_kernel(
    where_ref, nm0_ref, nm1_ref, g0_ref, g1_ref,
    up00_ref, up10_ref, up01_ref, up11_ref, down00_ref, down10_ref, down01_ref, down11_ref,
    e_ref, y_ref, give_e_ref, give_y_ref, up_keep_ref, up_give_ref, down_keep_ref, down_give_ref,
    wup_ref, wdown_ref, nm_ref, g_ref, acc_e_ref, acc_y_ref, part_ref, active_ref, d_hidden_ref, sems,
):
    step = pl.program_id(0)
    side, y_at = where_ref[1], where_ref[0] % 2

    @pl.when(step == 0)
    def _():
        copies = []
        for dy, ups, downs in (
            (0, (up00_ref, up10_ref), (down00_ref, down10_ref)),
            (1, (up01_ref, up11_ref), (down01_ref, down11_ref)),
        ):
            for dx in range(2):
                for i in range(4):
                    block = where_ref[8 + dy * 4 + i] * 2 + jnp.bitwise_xor(side, dx)
                    rows = pl.ds(pl.multiple_of(block * SUB, 16), SUB)
                    for half in range(2):
                        copies.append(
                            pltpu.make_async_copy(
                                ups[dx].at[i, pl.ds(half * SUB, SUB), :],
                                wup_ref.at[rows, pl.ds(half * D, D)],
                                sems.at[len(copies)],
                            )
                        )
                    copies.append(
                        pltpu.make_async_copy(
                            downs[dx].at[i],
                            wdown_ref.at[pl.ds(pl.multiple_of(block * FSUB, 16), FSUB), :],
                            sems.at[len(copies)],
                        )
                    )
        for copy in copies:
            copy.start()
        nm_ref[0:ROWS, :] = nm0_ref[...]
        nm_ref[ROWS:, :] = nm1_ref[...]
        g_ref[0:ROWS, :] = g0_ref[...]
        g_ref[ROWS:, :] = g1_ref[...]
        for copy in copies:
            copy.wait()

    at = pl.ds(pl.multiple_of(step * D, D), D)
    for start in range(0, 2 * ROWS, 256):
        rows = slice(start, start + 256)
        hidden = dot_nn(nm_ref[rows, :], wup_ref[:, at])
        square = hidden * hidden
        th = jnp.tanh(hidden * (GELU_C + GELU_C * GELU_A * square))
        left = 0.5 + 0.5 * th
        active_ref[rows, :] = (hidden * left).astype(BF)
        slope = left + hidden * (0.5 - 0.5 * th * th) * (GELU_C + 3.0 * GELU_A * GELU_C * square)
        d_hidden_ref[rows, :] = (dot_nt(g_ref[rows, :], wdown_ref[at, :]) * slope).astype(BF)
    part_y = dot_nn(active_ref[...], wdown_ref[at, :])
    part_e = dot_nt(d_hidden_ref[...], wup_ref[:, at])

    @pl.when(step == 0)
    def _():
        acc_y_ref[...] = part_y
        acc_e_ref[...] = part_e

    @pl.when(step == 1)
    def _():
        e_ref[...] = (acc_e_ref[0:ROWS, :] + part_e[0:ROWS]).astype(BF)
        y_ref[...] = (acc_y_ref[0:ROWS, :] + part_y[0:ROWS]).astype(BF)
        give_e_ref[...] = (acc_e_ref[ROWS:, :] + part_e[ROWS:]).astype(BF)
        give_y_ref[...] = (acc_y_ref[ROWS:, :] + part_y[ROWS:]).astype(BF)

    part_ref[...] = dot_tn(nm_ref[...], d_hidden_ref[...]).astype(BF).reshape(16, SUB, D)
    at_half = pl.ds(pl.multiple_of(step * SUB, 16), SUB)
    for s in range(8):
        up_keep_ref[s, at_half, :] = part_ref[2 * s + side]
        up_give_ref[s, at_half, :] = part_ref[2 * s + 1 - side]
    part_ref[...] = dot_tn(active_ref[...], g_ref[...]).astype(BF).reshape(16, SUB, D)
    for z in range(2):
        for x in range(2):
            for h in range(2):
                at_h = pl.ds(h * SUB, SUB)
                row = 8 * z + 2 * x + h
                down_keep_ref[z, x, at_h, :] = part_ref[row + 4 * y_at]
                down_give_ref[z, x, at_h, :] = part_ref[row + 4 - 4 * y_at]


def mlp(where, normed, grads, pieces):
    whole = pl.BlockSpec((ROWS, D), lambda i: (0, 0))
    anywhere = pl.BlockSpec(memory_space=pl.ANY)
    return pl.pallas_call(
        mlp_kernel,
        grid=(2,),
        in_specs=[pl.BlockSpec(memory_space=pltpu.SMEM)] + [whole] * 4 + [anywhere] * 8,
        out_specs=[whole] * 4
        + [pl.BlockSpec((8, 2 * SUB, D), lambda i: (0, 0, 0))] * 2
        + [pl.BlockSpec((2, 2, FSUB, D), lambda i: (i, 0, 0, 0))] * 2,
        out_shape=[shape((ROWS, D), BF)] * 4
        + [shape((8, 2 * SUB, D), BF)] * 2
        + [shape((4, 2, FSUB, D), BF)] * 2,
        scratch_shapes=[
            pltpu.VMEM((D, FH), BF),
            pltpu.VMEM((FH, D), BF),
            pltpu.VMEM((2 * ROWS, D), BF),
            pltpu.VMEM((2 * ROWS, D), BF),
            pltpu.VMEM((2 * ROWS, D), F32),
            pltpu.VMEM((2 * ROWS, D), F32),
            pltpu.VMEM((16, SUB, D), BF),
            pltpu.VMEM((2 * ROWS, D), BF),
            pltpu.VMEM((2 * ROWS, D), BF),
            pltpu.SemaphoreType.DMA((48,)),
        ],
        compiler_params=params(),
        cost_estimate=pl.CostEstimate(
            flops=20_000_000_000, bytes_accessed=20_000_000, transcendentals=1_600_000
        ),
    )(where, *normed, *grads, *pieces)


def branch_kernel(
    mid_ref, g_ref, e0_ref, e1_ref, att_ref, w_ref, dmid_ref, datt_ref, right_ref,
    low_ref, prod_ref,
):
    gain = gain_row(w_ref[0, :, HALF:])
    wout = w_ref[0, :, D:HALF]
    for chunk in range(4):
        rows = slice(chunk * PR, (chunk + 1) * PR)
        middle = mid_ref[rows, :]
        inv = rms_inv(middle)
        unit = middle * inv
        grad = e0_ref[rows, :].astype(F32) + e1_ref[rows, :].astype(F32)
        scaled = gain * grad
        mean = jnp.mean(unit * scaled, axis=-1, keepdims=True)
        d_mid = g_ref[rows, :].astype(F32) + inv * (scaled - unit * mean)
        dmid_ref[rows, :] = d_mid
        prod_ref[rows, :] = (grad * unit).astype(BF)
        branch = d_mid.astype(BF)
        low_ref[rows, :] = branch
        datt_ref[rows, :] = dot_nt(branch, wout).astype(BF)
    right_ref[:, D:] = dot_tn(prod_ref[...], jnp.ones((ROWS, 128), BF)).astype(BF)
    right_ref[:, 0:D] = dot_tn(att_ref[...], low_ref[...]).astype(BF)


def branch(middle, d_out, own, given, attended, w_all):
    return pl.pallas_call(
        branch_kernel,
        grid=(1,),
        in_specs=[pl.BlockSpec((ROWS, D), lambda i: (0, 0))] * 5
        + [pl.BlockSpec((1, D, WIDE), lambda i: (1, 0, 0))],
        out_specs=[
            pl.BlockSpec((ROWS, D), lambda i: (0, 0)),
            pl.BlockSpec((ROWS, D), lambda i: (0, 0)),
            pl.BlockSpec((D, RIGHT), lambda i: (0, 0)),
        ],
        out_shape=[shape((ROWS, D), F32), shape((ROWS, D), BF), shape((D, RIGHT), BF)],
        scratch_shapes=[pltpu.VMEM((ROWS, D), BF), pltpu.VMEM((ROWS, D), BF)],
        compiler_params=params(),
        cost_estimate=pl.CostEstimate(
            flops=2_000_000_000, bytes_accessed=9_000_000, transcendentals=1000
        ),
    )(middle, d_out, own, given, attended, w_all)


def attn_bwd_kernel(units, *refs):
    first, last = units == (2,), units[0] == 0
    q_ref, g_ref, o_ref, r_ref, *refs = refs
    keyed = []
    for _ in units:
        keyed.append(refs[:3])
        refs = refs[3:]
    if last:
        ec_ref, kc_ref, vc_ref, *refs = refs
    if not first:
        dq_in_ref, *refs = refs
    wk_ref, wv_ref, *refs = refs
    if last:
        where_ref, wq_ref, x_ref, normed_ref, kv1_ref, kv2_ref, kv3_ref, *refs = refs
        f1_ref, f2_ref, f3_ref, right_ref, *refs = refs
        keep_ref, give_ref, f0_ref, fc_ref, *refs = refs
        late_in = (wq_ref, wk_ref, wv_ref, x_ref, normed_ref, right_ref)
        *late, sems_late = refs[:7]
        refs = refs[7:]
        wq_ref, wk_ref, wv_ref, x_ref, normed_ref, right_ref = late
        dkv_ref, dq_ref, low_ref, high_ref, prod_ref, sems, *refs = refs
    else:
        dkv_refs, refs = refs[: len(units)], refs[len(units) :]
        f_refs, refs = refs[: len(units)], refs[len(units) :]
        dq_ref, *refs = refs
    qs_ref, gs_ref, ds_ref, *refs = refs
    if last:
        sum_ref, near_ref, near_e_ref, near_qs_ref, near_gs_ref = refs
    step = pl.program_id(0)

    def late_copies():
        sources = (
            late_in[0].at[pl.ds(0, 1), :, pl.ds(0, D)],
            late_in[1].at[pl.ds(0, 1), :, pl.ds(D, D)],
            late_in[2].at[pl.ds(1, 1), :, pl.ds(0, D)],
            *late_in[3:],
        )
        return [
            pltpu.make_async_copy(source, target, sems_late.at[at])
            for at, (source, target) in enumerate(zip(sources, late))
        ]

    if last:

        @pl.when(step == 0)
        def _():
            for at, ref in enumerate((kv1_ref, kv2_ref, kv3_ref)):
                rows = pl.ds((at + 1) * UNIT, UNIT)
                pltpu.make_async_copy(ref, dkv_ref.at[:, rows, :], sems.at[at]).start()
            for copy in late_copies():
                copy.start()

    low_half = lane_half(0)
    for pair in range(2):
        lanes = slice(pair * WIDTH, (pair + 1) * WIDTH)
        lanes_v = slice((2 + pair) * WIDTH, (3 + pair) * WIDTH)
        scaled_grad = g_ref[:, lanes].astype(F32) * r_ref[:, lanes]
        prod = scaled_grad * o_ref[:, lanes].astype(F32)
        low_grad = scaled_grad.astype(BF)
        query = q_ref[:, lanes]
        deltas = []
        for head in range(2):
            half = lane_half(head)
            rows = slice(head * ROWS, (head + 1) * ROWS)
            deltas.append(jnp.sum(jnp.where(half, prod, 0.0), axis=-1, keepdims=True))
            gs_ref[rows, :] = jnp.where(half, low_grad, jnp.zeros_like(low_grad))
            qs_ref[rows, :] = jnp.where(half, query, jnp.zeros_like(query))
        delta = jnp.concatenate(deltas, axis=0)
        d_query = None
        for u, (e_ref, k_ref, v_ref) in enumerate(keyed):
            out_ref = dkv_ref if last else dkv_refs[u]
            terms = e_ref[2 * pair : 2 * pair + 2].reshape(2 * ROWS, UNIT)
            d_soft = dot_nt(gs_ref[...], v_ref[:, lanes])
            ds_ref[...] = terms * (d_soft - delta).astype(BF)
            more = dot_nn(ds_ref[...], k_ref[:, lanes])
            d_query = more if d_query is None else d_query + more
            out_ref[step, 0:UNIT, lanes] = dot_tn(ds_ref[...], qs_ref[...]).astype(BF)
            out_ref[step, 0:UNIT, lanes_v] = dot_tn(terms, gs_ref[...]).astype(BF)
        total = jnp.where(low_half, d_query[0:ROWS], d_query[ROWS:])
        if not first:
            total = total + dq_in_ref[:, lanes]
        if not last:
            dq_ref[:, lanes] = total
            continue
        sum_ref[...] = total
        for side in range(2):
            own = slice(side * PR, (side + 1) * PR)
            mine = slice((2 + side) * PR, (3 + side) * PR)
            near_q = []
            for head in range(2):
                rows = slice(head * ROWS + mine.start, head * ROWS + mine.stop)
                at = slice(head * PR, (head + 1) * PR)
                near = ec_ref[2 * pair + head, own, :]
                d_soft = dot_nt(gs_ref[rows, :], vc_ref[own, lanes])
                near_ref[at, :] = near * (d_soft - deltas[head][mine]).astype(BF)
                near_e_ref[at, :] = near
                near_qs_ref[at, :] = qs_ref[rows, :]
                near_gs_ref[at, :] = gs_ref[rows, :]
                near_q.append(dot_nn(near_ref[at, :], kc_ref[own, lanes]))
            sum_ref[mine, :] += jnp.where(low_half, near_q[0], near_q[1])
            rows = slice(PLEN + side * PR, PLEN + (side + 1) * PR)
            dkv_ref[step, rows, lanes] = dot_tn(near_ref[...], near_qs_ref[...]).astype(BF)
            dkv_ref[step, rows, lanes_v] = dot_tn(near_e_ref[...], near_gs_ref[...]).astype(BF)
        dq_ref[step, :, lanes] = (sum_ref[...] * SCALE).astype(BF)

    def back_to_rows(dkv, rows):
        grad = None
        for i in range(3):
            at = slice(i * UNIT, (i + 1) * UNIT)
            more = dot_nt(dkv[i, rows, 0:UNIT], wk_ref[0, :, at])
            more = more + dot_nt(dkv[i, rows, UNIT:], wv_ref[0, :, at])
            grad = more if grad is None else grad + more
        return grad

    @pl.when(step == pl.num_programs(0) - 1)
    def _():
        if not last:
            for dkv, f_ref in zip(dkv_refs, f_refs):
                f_ref[...] = back_to_rows(dkv, slice(0, UNIT)).astype(BF)
            return
        for at, ref in enumerate((kv1_ref, kv2_ref, kv3_ref)):
            rows = pl.ds((at + 1) * UNIT, UNIT)
            pltpu.make_async_copy(ref, dkv_ref.at[:, rows, :], sems.at[at]).wait()
        for copy in late_copies():
            copy.wait()
        high_ref[:, D:] = right_ref[...]
        for out_ref, rows, q_rows in (
            (f0_ref, slice(0, UNIT), slice(0, UNIT)),
            (fc_ref, slice(PLEN, KEYS), slice(UNIT, ROWS)),
        ):
            grad = back_to_rows(dkv_ref, rows)
            for i in range(3):
                at = slice(i * UNIT, (i + 1) * UNIT)
                grad = grad + dot_nt(dq_ref[i, q_rows, :], wq_ref[0, :, at])
            out_ref[...] = grad
        for at, f_ref in enumerate((f0_ref, f1_ref, f2_ref, f3_ref, fc_ref)):
            rows = slice(at * UNIT, (at + 1) * UNIT)
            tokens = x_ref[rows, :].astype(F32)
            prod_ref[rows, :] = (f_ref[...].astype(F32) * (tokens * rms_inv(tokens))).astype(BF)
        low_ref[:, HALF:] = dot_tn(prod_ref[...], jnp.ones((KEYS, 128), BF)).astype(BF)
        for i in range(3):
            at = slice(i * UNIT, (i + 1) * UNIT)
            low_ref[:, at] = (
                dot_tn(normed_ref[0:UNIT, :], dq_ref[i, 0:UNIT, :])
                + dot_tn(normed_ref[PLEN:, :], dq_ref[i, UNIT:, :])
            ).astype(BF)
            both = dot_tn(normed_ref[...], dkv_ref[i]).astype(BF)
            low_ref[:, D + i * UNIT : D + (i + 1) * UNIT] = both[:, 0:UNIT]
            high_ref[:, at] = both[:, UNIT:]

        for core, low_out, high_out in ((0, keep_ref, give_ref), (1, give_ref, keep_ref)):

            @pl.when(where_ref[2] == core)
            def _():
                copies = [
                    pltpu.make_async_copy(low_ref, low_out, sems.at[3]),
                    pltpu.make_async_copy(high_ref, high_out, sems.at[4]),
                ]
                for copy in copies:
                    copy.start()
                for copy in copies:
                    copy.wait()


def attn_bwd(units, saved, d_att, w_all, dq=None, rest=None):
    first, last = units == (2,), units[0] == 0
    q, k, v, e, ec, o, r = saved
    width = 2 * WIDTH
    lanes = lambda i: (0, i)
    full = lambda *dims: pl.BlockSpec(dims, lambda i: (0,) * len(dims))
    rows = pl.BlockSpec((ROWS, width), lanes)
    anywhere = pl.BlockSpec(memory_space=pl.ANY)
    weight = lambda half, at: pl.BlockSpec((1, D, D), lambda i: (half, 0, at))
    specs, args = [rows] * 4, [q, d_att, o, r]
    for u in units:
        specs += [
            pl.BlockSpec((4, ROWS, UNIT), lambda i, u=u: (i, 0, u)),
            pl.BlockSpec((UNIT, width), lambda i, u=u: (u, i)),
            pl.BlockSpec((UNIT, width), lambda i, u=u: (u, i)),
        ]
        args += [e, k, v]
    if last:
        specs += [
            pl.BlockSpec((4, UNIT, PR), lambda i: (i, 0, 0)),
            pl.BlockSpec((UNIT, width), lambda i: (4, i)),
            pl.BlockSpec((UNIT, width), lambda i: (4, i)),
        ]
        args += [ec, k, v]
    if not first:
        specs.append(rows)
        args.append(dq)
    specs += [anywhere, anywhere] if last else [weight(0, 1), weight(1, 0)]
    args += [w_all, w_all]
    kv = (3, UNIT, 2 * UNIT)
    if last:
        where, x_all, normed, kvs, fs, right = rest
        specs += [pl.BlockSpec(memory_space=pltpu.SMEM)] + [anywhere] * 6
        specs += [full(UNIT, D)] * 3 + [anywhere]
        args += [where, w_all, x_all, normed, *kvs, *fs, right]
        outs = [anywhere, anywhere, full(UNIT, D), full(UNIT, D)]
        out_shapes = [shape((D, WIDE), BF)] * 2 + [shape((UNIT, D), F32)] * 2
        scratch = [
            pltpu.VMEM((1, D, D), BF),
            pltpu.VMEM((1, D, D), BF),
            pltpu.VMEM((1, D, D), BF),
            pltpu.VMEM((KEYS, D), BF),
            pltpu.VMEM((KEYS, D), BF),
            pltpu.VMEM((D, RIGHT), BF),
            pltpu.SemaphoreType.DMA((6,)),
            pltpu.VMEM((3, KEYS, 2 * UNIT), BF),
            pltpu.VMEM((3, ROWS, UNIT), BF),
            pltpu.VMEM((D, WIDE), BF),
            pltpu.VMEM((D, WIDE), BF),
            pltpu.VMEM((KEYS, D), BF),
            pltpu.SemaphoreType.DMA((5,)),
        ]
    else:
        outs = [full(*kv)] * len(units) + [full(UNIT, D)] * len(units) + [rows]
        out_shapes = [shape(kv, BF)] * len(units) + [shape((UNIT, D), BF)] * len(units)
        out_shapes.append(shape((ROWS, D), F32))
        scratch = []
    return pl.pallas_call(
        lambda *refs: attn_bwd_kernel(units, *refs),
        grid=(3,),
        in_specs=specs,
        out_specs=outs,
        out_shape=out_shapes,
        scratch_shapes=scratch
        + [
            pltpu.VMEM((2 * ROWS, WIDTH), BF),
            pltpu.VMEM((2 * ROWS, WIDTH), BF),
            pltpu.VMEM((2 * ROWS, UNIT), BF),
        ]
        + ([pltpu.VMEM((ROWS, WIDTH), F32)] + [pltpu.VMEM((UNIT, WIDTH), BF)] * 4 if last else []),
        compiler_params=params(),
        cost_estimate=pl.CostEstimate(
            flops=10_000_000_000 * (len(units) + last), bytes_accessed=10_000_000, transcendentals=1000
        ),
    )(*args)


def tail_kernel(x_ref, f0_ref, f1_ref, f2_ref, f3_ref, fc_ref, dmid_ref, w_ref, keep_ref, give_ref):
    gain = gain_row(w_ref[0])
    for chunk in range(4):
        rows = slice(chunk * PR, (chunk + 1) * PR)
        part = x_ref[rows, :].astype(F32)
        inv = rms_inv(part)
        unit = part * inv
        if chunk < 2:
            grad = f0_ref[rows, :].astype(F32)
            for f_ref in (f1_ref, f2_ref, f3_ref):
                grad = grad + f_ref[rows, :].astype(F32)
        else:
            grad = fc_ref[(chunk - 2) * PR : (chunk - 1) * PR, :]
        scaled = gain * grad
        mean = jnp.mean(unit * scaled, axis=-1, keepdims=True)
        out_ref = give_ref if chunk % 2 else keep_ref
        at = slice(chunk // 2 * PR, (chunk // 2 + 1) * PR)
        out_ref[at, :] = (dmid_ref[rows, :] + inv * (scaled - unit * mean)).astype(out_ref.dtype)


def tail(x_own, f_parts, f_cont, d_mid, w_all):
    whole = lambda i: (0, 0)
    half = pl.BlockSpec((2 * PR, D), whole)
    full = pl.BlockSpec((ROWS, D), whole)
    return pl.pallas_call(
        tail_kernel,
        grid=(1,),
        in_specs=[full, half, half, half, half, half, full]
        + [pl.BlockSpec((1, D, 128), lambda i: (0, 0, HALF // 128))],
        out_specs=[half, half],
        out_shape=[shape((2 * PR, D), F32), shape((2 * PR, D), BF)],
        compiler_params=params(),
        cost_estimate=pl.CostEstimate(flops=20_000_000, bytes_accessed=7_000_000, transcendentals=1000),
    )(x_own, *f_parts, f_cont, d_mid, w_all)


def total_of(*parts):
    total = parts[0].astype(F32)
    for part in parts[1:]:
        total = total + part.astype(F32)
    return total.astype(BF)


def run_whole(kernel, outs, *args, dtype=BF):
    return pl.pallas_call(
        kernel,
        in_specs=[pl.BlockSpec(memory_space=pltpu.SMEM)]
        + [pl.BlockSpec(memory_space=pltpu.VMEM)] * (len(args) - 1),
        out_specs=[pl.BlockSpec(memory_space=pltpu.VMEM)] * len(outs),
        out_shape=[shape(dims, dtype) for dims in outs],
        compiler_params=params(),
        cost_estimate=pl.CostEstimate(flops=1_000_000, bytes_accessed=7_000_000, transcendentals=0),
    )(*args)


def fold_two_kernel(where_ref, a0_ref, a1_ref, b0_ref, b1_ref, ak_ref, ag_ref, bk_ref, bg_ref):
    y_at, side = where_ref[0] % 2, where_ref[1]
    for z in range(4):
        ak_ref[z] = total_of(a0_ref[z, y_at], a1_ref[z, y_at])
        ag_ref[z] = total_of(a0_ref[z, 1 - y_at], a1_ref[z, 1 - y_at])
        bk_ref[z] = total_of(b0_ref[z, side], b1_ref[z, side])
        bg_ref[z] = total_of(b0_ref[z, 1 - side], b1_ref[z, 1 - side])


def fold_rows_kernel(where_ref, a0_ref, a1_ref, b0_ref, b1_ref, *outs):
    z_at = where_ref[0] // 2
    rows = a0_ref.shape[1]
    for step, out_ref in enumerate(outs):
        z = jnp.bitwise_xor(z_at, step)
        out_ref[0:rows, :] = total_of(a0_ref[z], a1_ref[z])
        out_ref[rows:, :] = total_of(b0_ref[z], b1_ref[z])


def fold_cols_kernel(where_ref, a0_ref, a1_ref, b0_ref, b1_ref, *outs):
    z_at = where_ref[0] // 2
    cols = a0_ref.shape[2]
    for step, out_ref in enumerate(outs):
        z = jnp.bitwise_xor(z_at, step)
        out_ref[:, 0:cols] = total_of(a0_ref[z], a1_ref[z])
        out_ref[:, cols:] = total_of(b0_ref[z], b1_ref[z])


def fold_core_kernel(where_ref, own_ref, got_ref, ak_ref, ag_ref, bk_ref, bg_ref):
    y_at, side = where_ref[0] % 2, where_ref[1]
    left, right = slice(0, LEFT), slice(LEFT, WIDE)

    def block(s, x, cols):
        rows = pl.ds(pl.multiple_of((2 * s + x) * SUB, 16), SUB)
        return total_of(own_ref[rows, cols], got_ref[rows, cols])

    for s in range(8):
        ak_ref[s // 2, s % 2] = block(s, side, left)
        ag_ref[s // 2, s % 2] = block(s, 1 - side, left)
    for z in range(4):
        for x in range(2):
            bk_ref[z, x] = block(2 * z + y_at, x, right)
            bg_ref[z, x] = block(2 * z + 1 - y_at, x, right)


def unpack_kernel(where_ref, here_ref, far_ref, up_ref, down_ref):
    side, core = where_ref[1], where_ref[2]
    first = core == 0
    for x in range(2):
        at = jnp.bitwise_xor(side, x)
        rows = slice(x * SUB, (x + 1) * SUB)
        here, far = here_ref[at].astype(F32), far_ref[at].astype(F32)
        low, high = jnp.where(first, here, far), jnp.where(first, far, here)
        down_ref[x * FSUB : (x + 1) * FSUB, :] = low[2 * SUB :]
        down_ref[(2 + x) * FSUB : (3 + x) * FSUB, :] = high[2 * SUB :]
        for half in range(2):
            own = slice(half * SUB, (half + 1) * SUB)
            for i in range(4):
                cols = slice(i * 2 * FSUB, (i + 1) * 2 * FSUB)
                start = (half * 4 + i) * 4 * FSUB
                up_ref[rows, start : start + 4 * FSUB] = jnp.concatenate(
                    [low[own, cols], high[own, cols]], axis=1
                )


def finish_kernel(where_ref, own_ref, side_ref, core_ref, far_ref, qkv_ref, out_ref, gain_ref):
    first, near = where_ref[2] == 0, where_ref[1] == 0
    for x in range(2):
        mine = jnp.where(near == (x == 0), own_ref[...], side_ref[...]).astype(F32)
        theirs = jnp.where(near == (x == 0), core_ref[...], far_ref[...]).astype(F32)
        low, high = jnp.where(first, mine, theirs), jnp.where(first, theirs, mine)
        rows = slice(x * SUB, (x + 1) * SUB)
        qkv_ref[rows, 0:HALF] = low[:, 0:HALF]
        qkv_ref[rows, HALF:] = high[:, 0:D]
        out_ref[rows, :] = high[:, D:HALF]
        gain_ref[rows, 0:128] = low[:, HALF:]
        gain_ref[rows, 128:] = high[:, HALF:]


def over(axis, value, bits):
    return lax.ppermute(value, axis, [(i, i ^ bits) for i in range(lax.axis_size(axis))])


def cut(values, start, rows=PR):
    return lax.dynamic_slice_in_dim(values, start, rows, 0)


def pick(values, at):
    return lax.dynamic_index_in_dim(values, at, 0, keepdims=False)


def pick_of(values, at, axis):
    return lax.dynamic_index_in_dim(values, at, axis, keepdims=False)


def tie(*values):
    return lax.optimization_barrier(values)


def per_device(tokens, w_qkv, w_out, w_up, w_down, gain_attn, gain_mlp, d_out):
    staged = lax.axis_size("shard") == 8
    shard = lax.axis_index("shard")
    rep = lax.axis_index("rep")
    side, core = rep // 2, rep % 2
    pos = shard % 8
    y_at, z_at = pos % 2, pos // 2
    table = [pos ^ d for d in ORDER] if staged else [jnp.int32(2 * (d % 4) + d // 4) for d in range(8)]
    where = jnp.stack([pos, side, core] + [jnp.int32(0)] * 5 + table).astype(jnp.int32)

    def to_give(values):
        return jnp.concatenate([cut(values, (1 - y_at) * PR), cut(values, (3 - y_at) * PR)], axis=0)

    def own_rows(values, got):
        mine_p, mine_c = cut(values, y_at * PR), cut(values, (2 + y_at) * PR)
        return jnp.concatenate([mine_p, got[:PR], mine_c, got[PR:]], axis=0)

    def to_return(values):
        return jnp.concatenate([values[PR : 2 * PR], values[3 * PR :]], axis=0)

    def home_rows(keep_p, keep_c, got):
        got = got.astype(keep_p.dtype)
        first = y_at == 0
        return jnp.concatenate(
            [
                jnp.where(first, keep_p, got[:PR]),
                jnp.where(first, got[:PR], keep_p),
                jnp.where(first, keep_c, got[PR:]),
                jnp.where(first, got[PR:], keep_c),
            ],
            axis=0,
        )

    def halves(qkv, out, gain_a, gain_m):
        wide = lambda gain: jnp.broadcast_to(gain[:, None], (gain.shape[0], 128))
        return (
            jnp.concatenate([qkv[:, :HALF], wide(gain_a)], axis=1),
            jnp.concatenate([qkv[:, HALF:], out, wide(gain_m)], axis=1),
        )

    def half_up(up):
        return pick_of(up.reshape(up.shape[0], 8, 2, 2 * FSUB), core, 2).reshape(up.shape[0], FH)

    def own_up(up):
        mine = half_up(cut(up, side * SUB, SUB))
        return jnp.concatenate([mine[:, :D], mine[:, D:]], axis=0)

    if staged:
        low, high = halves(w_qkv, w_out, gain_attn, gain_mlp)
        own_piece = cut(jnp.where(core == 0, low, high), side * SUB, SUB)
        own_mlp = jnp.concatenate(
            [own_up(w_up), cut(w_down, core * 2 * FSUB + side * FSUB, FSUB)], axis=0
        )
        t_got, z1, z2, z3 = tie(
            over("shard", to_give(tokens), 1),
            *[over("shard", own_piece, k) for k in (2, 4, 6)],
        )
        x_own = own_rows(tokens, t_got)
        near = x_own[: 2 * PR]
        line = (own_piece, z1, z2, z3)
        left = jnp.stack([part[:, :LEFT] for part in line])
        right = jnp.stack([part[:, LEFT:] for part in line])
        own_mlp, left, right, near = tie(own_mlp, left, right, near)
        m1, m2, m3, left_y, right_x, g_got = tie(
            *[over("shard", own_mlp, k) for k in (2, 4, 6)],
            over("shard", left, 1),
            over("rep", right, 2),
            over("shard", to_give(d_out), 1),
        )
        left = jnp.concatenate([left, left_y], axis=0)
        right = jnp.concatenate([right, right_x], axis=0)
        mlp_line = (own_mlp, m1, m2, m3)
        up = jnp.stack([part[: 2 * SUB] for part in mlp_line])
        down = jnp.stack([part[2 * SUB :] for part in mlp_line])
        near, left, right, up, down = tie(near, left, right, up, down)
        near1, near2, near3, left_x, right_y, up_y, down_x = tie(
            *[over("shard", near, k) for k in (2, 4, 6)],
            over("rep", left, 2),
            over("shard", right, 1),
            over("shard", up, 1),
            over("rep", down, 2),
        )
        pieces = tie(
            left, left_x, over("rep", left, 1), over("rep", left_x, 1),
            right, right_y, over("rep", right, 1), over("rep", right_y, 1),
        )
        up, up_y, down, down_x, pieces = tie(up, up_y, down, down_x, pieces)
        mlp_pieces = (
            up, over("rep", up, 2), up_y, over("rep", up_y, 2),
            down, down_x, over("shard", down, 1), over("shard", down_x, 1),
        )
    else:
        gathered = [
            lax.all_gather(w, "shard", axis=0, tiled=True)
            for w in (w_qkv, w_out, gain_attn, gain_mlp, w_up, w_down)
        ]
        natural = jnp.stack(halves(*gathered[:4])).reshape(2, 4, 2, 2, SUB, WIDE)
        pieces = []
        for dc in (0, 1):
            by_core = pick(natural, core ^ dc)
            for dx in (0, 1):
                both = pick_of(by_core[..., :LEFT], side ^ dx, 2)
                pieces.append(jnp.concatenate([both[:, 0], both[:, 1]], axis=0))
        for dc in (0, 1):
            by_core = pick(natural, core ^ dc)[..., LEFT:]
            for dy in (0, 1):
                both = [pick_of(by_core[:, dy], side ^ dx, 1) for dx in (0, 1)]
                pieces.append(jnp.concatenate(both, axis=0))
        pieces = tuple(pieces)
        up = half_up(gathered[4]).reshape(4, 2, 2, SUB, 2, D).transpose(1, 0, 2, 4, 3, 5)
        up = up.reshape(2, 4, 2, 2 * SUB, D)
        down = pick_of(gathered[5].reshape(4, 2, 2, 2, FSUB, D), core, 2).transpose(1, 0, 2, 3, 4)
        mlp_pieces = tuple(
            pick_of(both[dy], side ^ dx, 1) for both in (up, down) for dy in (0, 1) for dx in (0, 1)
        )
        x_own = own_rows(tokens, over("shard", to_give(tokens), 1))
        near = x_own[: 2 * PR]
        near1, near2, near3 = [over("shard", near, k) for k in (2, 4, 6)]
        g_got = over("shard", to_give(d_out), 1)
    x_all = jnp.concatenate([near, near1, near2, near3, x_own[2 * PR :]], axis=0)
    g_own = own_rows(d_out, g_got)
    x_all, g_own = tie(x_all, g_own)

    g_core = over("rep", g_own, 1)
    forward = attn_fwd(where, x_all, pieces)
    forward, mlp_pieces, g_core = tie(forward, mlp_pieces, g_core)
    w_all, q, k, v, e, ec, attended, inv_sum, middle, nm, normed = forward

    nm_core, nm = tie(over("rep", nm, 1), nm)
    e_own, y_own, e_give, y_give, *mlp_grads = mlp(
        where, (nm, nm_core), (g_own, g_core), mlp_pieces
    )
    e_got, y_give, mlp_grads = tie(over("rep", e_give, 1), y_give, mlp_grads)
    up_keep, up_give, down_keep, down_give = mlp_grads
    y_got = over("rep", y_give, 1)
    if staged:
        up_got, down_got = over("rep", up_give, 2), over("shard", down_give, 1)
    d_mid, d_att, d_right = branch(middle, g_own, e_own, e_got, attended, w_all)

    saved = (q, k, v, e, ec, attended, inv_sum)
    kv2, f2_give, dq = attn_bwd((2,), saved, d_att, w_all)
    y_got, dq = tie(y_got, dq)
    block_rows = (middle + y_own.astype(F32) + y_got.astype(F32)).astype(BF)
    block_give = to_return(block_rows)
    f2_give, dq, block_give = tie(f2_give, dq, block_give)
    f2 = over("shard", f2_give, 4)
    kv3, kv1, f3_give, f1_give, dq = attn_bwd((3, 1), saved, d_att, w_all, dq)
    f2, f3_give, f1_give, dq, block_give = tie(f2, f3_give, f1_give, dq, block_give)
    if staged:
        up_got, down_got, dq = tie(up_got, down_got, dq)
        by_pair = (4, 2, 2 * SUB, D)
        folded = run_whole(
            fold_two_kernel, [(4, 2 * SUB, D)] * 4, where,
            up_keep.reshape(by_pair), up_got.reshape(by_pair), down_keep, down_got,
        )
        (up_keep, up_give, down_keep, down_give), dq, f3_give, f1_give, block_give = tie(
            folded, dq, f3_give, f1_give, block_give
        )
        up_got, down_got = over("shard", up_give, 1), over("rep", down_give, 2)
    f1, f3, b_got = over("shard", f1_give, 2), over("shard", f3_give, 6), over("shard", block_give, 1)
    keep, give, f0, f_cont = attn_bwd(
        (0,), saved, d_att, w_all, dq,
        (where, x_all, normed, (kv1, kv2, kv3), (f1_give, f2_give, f3_give), d_right),
    )
    f1, f3, b_got, keep, give, f0, f_cont = tie(f1, f3, b_got, keep, give, f0, f_cont)
    if staged:
        up_got, down_got, give = tie(up_got, down_got, give)
        mlp_total, *mlp_gives = run_whole(
            fold_rows_kernel, [(4 * SUB, D)] * 4, where, up_keep, up_got, down_keep, down_got
        )
        chip_got, mlp_gives = tie(over("rep", give, 1), mlp_gives)
        left, right = (4, 2, SUB, LEFT), (4, 2, SUB, WIDE - LEFT)
        left_keep, left_give, right_keep, right_give = run_whole(
            fold_core_kernel, [left, left, right, right], where, keep, chip_got
        )
        left_give, right_give, mlp_gives, f0 = tie(left_give, right_give, mlp_gives, f0)
        left_got, right_got, m2, mlp_gives, token_keep, token_give = tie(
            over("rep", left_give, 2),
            over("shard", right_give, 1),
            over("shard", mlp_gives[1], 4),
            mlp_gives,
            *tail(x_own, (f0, f1, f2, f3), f_cont, d_mid, w_all),
        )
        left_keep, left_give, right_keep, right_give = run_whole(
            fold_two_kernel,
            [(4, SUB, LEFT)] * 2 + [(4, SUB, WIDE - LEFT)] * 2,
            where, left_keep, left_got, right_keep, right_got,
        )
        left_got, right_got, m1, m3 = tie(
            over("shard", left_give, 1),
            over("rep", right_give, 2),
            over("shard", mlp_gives[0], 2),
            over("shard", mlp_gives[2], 6),
        )
        total, *gives = run_whole(
            fold_cols_kernel, [(SUB, WIDE)] * 4, where, left_keep, left_got, right_keep, right_got
        )
        gives, m1, m3 = tie(gives, m1, m3)
        mlp_total = total_of(mlp_total, m1, m2, m3)
        z1, z2, z3, m_got, mlp_total, t_got = tie(
            *[over("shard", gives[step - 1], 2 * step) for step in (1, 2, 3)],
            over("rep", mlp_total, 2),
            mlp_total,
            over("shard", token_give, 1),
        )
        total = total_of(total, z1, z2, z3)
        by_side = jnp.stack([mlp_total, m_got])
        other, core_got, m_got, by_side = tie(
            over("rep", total, 2), over("rep", total, 1), over("rep", by_side, 1), by_side
        )
        far = over("rep", other, 1)
        d_wup, d_wdown = run_whole(
            unpack_kernel, [(2 * SUB, FF), (4 * FSUB, D)], where, by_side, m_got, dtype=F32
        )
        d_wqkv, d_wout, d_gains = run_whole(
            finish_kernel, [(2 * SUB, 3 * D), (2 * SUB, D), (2 * SUB, 256)],
            where, total, other, core_got, far, dtype=F32,
        )
        d_gain_attn, d_gain_mlp = d_gains[:, 0], d_gains[:, 128]
    else:
        token_keep, token_give = tail(x_own, (f0, f1, f2, f3), f_cont, d_mid, w_all)
        t_got = over("shard", token_give, 1)
        low, high = jnp.where(core == 0, keep, give), jnp.where(core == 0, give, keep)

        def by_side_of(keep, give, at):
            first = at == 0
            return jnp.stack([jnp.where(first, keep, give), jnp.where(first, give, keep)])

        up = by_side_of(up_keep, up_give, side).reshape(2, 8, 2, SUB, D)
        up = up.transpose(1, 0, 3, 2, 4).reshape(D, 8, 1, 2 * FSUB)
        down = by_side_of(down_keep, down_give, y_at).transpose(1, 0, 2, 3, 4)
        down = down.reshape(8, 1, 2 * FSUB, D)
        peer_up, peer_down = over("rep", up, 1), over("rep", down, 1)
        first = core == 0
        up, peer_up = jnp.where(first, up, peer_up), jnp.where(first, peer_up, up)
        down, peer_down = jnp.where(first, down, peer_down), jnp.where(first, peer_down, down)
        up = jnp.concatenate([up, peer_up], axis=2).reshape(D, FF)
        down = jnp.concatenate([down, peer_down], axis=1).reshape(FF, D)
        rest = lambda v: (v.astype(F32) + over("rep", v, 2).astype(F32)).astype(BF)
        up, down = rest(up), rest(down)
        scatter = lambda v: lax.psum_scatter(v, "shard", scatter_dimension=0, tiled=True)
        d_wup, d_wdown = scatter(up).astype(F32), scatter(down).astype(F32)
        low = lax.psum(scatter(low), "rep").astype(F32)
        high = lax.psum(scatter(high), "rep").astype(F32)
        d_wqkv = jnp.concatenate([low[:, :HALF], high[:, :D]], axis=1)
        d_wout, d_gain_attn, d_gain_mlp = high[:, D:HALF], low[:, HALF], high[:, HALF]

    return (
        home_rows(block_rows[:PR], block_rows[2 * PR : 3 * PR], b_got),
        home_rows(token_keep[:PR], token_keep[PR:], t_got),
        d_wqkv,
        d_wout,
        d_wup,
        d_wdown,
        d_gain_attn,
        d_gain_mlp,
    )


def solution(mesh):
    weights = P("shard", None)
    rows = P(("rep", "shard"), None)
    return jax.shard_map(
        per_device,
        mesh=mesh,
        in_specs=(rows, weights, weights, weights, weights, P("shard"), P("shard"), rows),
        out_specs=(rows, rows, weights, weights, weights, weights, P("shard"), P("shard")),
        check_vma=False,
    )
```

```python
import jax
import jax.numpy as jnp
from jax import lax
from jax.experimental import pallas as pl
from jax.experimental.pallas import tpu as pltpu
from jax.sharding import PartitionSpec as P

D = 768
HEADS = 12
HDIM = 64
FF = 3072
PR = 128
PLEN = 1024
KEYS = PLEN + 2 * PR
ROWS = 4 * PR
PAIRS = HEADS // 2
WIDTH = 2 * HDIM
HALF = 1536
WIDE = HALF + 128
SUB = 48
LEFT = 896
RIGHT = D + 128
UNIT = 2 * PR
FSUB = 96
FH = FF // 2
norm_eps = 1e-05
neg_fill = -1e30
SCALE = HDIM ** (-0.5)
GELU_C = 0.7978845608028654
GELU_A = 0.044715
BF = jnp.bfloat16
F32 = jnp.float32
VMEM_LIMIT = 60 * 1024 * 1024
BLOCKS = (0, 1, 2, 3, 4, 5, 6, 7)
ORDER = (0, 2, 4, 6, 1, 3, 5, 7)


def dot_nt(a, b):
    return lax.dot_general(a, b, (((1,), (1,)), ((), ())), preferred_element_type=F32)


def dot_tn(a, b):
    return lax.dot_general(a, b, (((0,), (0,)), ((), ())), preferred_element_type=F32)


def dot_nn(a, b):
    return jnp.dot(a, b, preferred_element_type=F32)


def rms_inv(values):
    return lax.rsqrt(jnp.mean(values * values, axis=-1, keepdims=True) + norm_eps)


def params():
    return pltpu.CompilerParams(vmem_limit_bytes=VMEM_LIMIT)


def shape(dims, dtype):
    return jax.ShapeDtypeStruct(dims, dtype)


def fill_normed(x_ref, gain, normed_ref):
    @pl.loop(0, KEYS, step=PR)
    def _(row):
        rows = pl.ds(pl.multiple_of(row, PR), PR)
        part = x_ref[rows, :].astype(F32)
        normed_ref[rows, :] = (part * rms_inv(part) * gain).astype(BF)


def lane_half(head):
    lanes = lax.broadcasted_iota(jnp.int32, (1, WIDTH), 1)
    return (lanes >= HDIM) if head else (lanes < HDIM)


def gain_row(column):
    return column.astype(F32).T[0:1, :]


def attn_fwd_kernel(
    where_ref, x0_ref, x1_ref, x2_ref, x3_ref, xc_ref,
    l00_ref, l10_ref, l01_ref, l11_ref, r00_ref, r10_ref, r01_ref, r11_ref,
    w_out_ref, q_ref, k_ref, v_ref, e_ref, ec_ref, o_ref, r_ref, mid_ref, nm_ref, normed_out_ref,
    w_ref, x_ref, normed_ref, bias_ref, att_ref, qs_ref, s_ref, inv_ref, out_ref, sems, out_sems,
):
    step = pl.program_id(0)
    late = [
        pltpu.make_async_copy(w_ref, w_out_ref, out_sems.at[0]),
        pltpu.make_async_copy(normed_ref, normed_out_ref, out_sems.at[1]),
    ]

    @pl.when(step == 0)
    def _():
        side, core = where_ref[1], where_ref[2]
        copies = []
        for at, (dx, dc, piece) in enumerate(
            ((0, 0, l00_ref), (1, 0, l10_ref), (0, 1, l01_ref), (1, 1, l11_ref))
        ):
            for i in range(8):
                start = where_ref[8 + i] * (2 * SUB) + jnp.bitwise_xor(side, dx) * SUB
                copies.append(
                    pltpu.make_async_copy(
                        piece.at[i],
                        w_ref.at[
                            jnp.bitwise_xor(core, dc),
                            pl.ds(pl.multiple_of(start, 16), SUB),
                            pl.ds(0, LEFT),
                        ],
                        sems.at[at * 8 + i],
                    )
                )
        for at, (far, dc, piece) in enumerate(
            ((0, 0, r00_ref), (1, 0, r10_ref), (0, 1, r01_ref), (1, 1, r11_ref))
        ):
            for i in range(8):
                start = where_ref[8 + far * 4 + i % 4] * (2 * SUB)
                start = start + jnp.bitwise_xor(side, i // 4) * SUB
                copies.append(
                    pltpu.make_async_copy(
                        piece.at[i],
                        w_ref.at[
                            jnp.bitwise_xor(core, dc),
                            pl.ds(pl.multiple_of(start, 16), SUB),
                            pl.ds(LEFT, WIDE - LEFT),
                        ],
                        sems.at[32 + at * 8 + i],
                    )
                )
        for at, part in enumerate((x0_ref, x1_ref, x2_ref, x3_ref, xc_ref)):
            copies.append(
                pltpu.make_async_copy(part, x_ref.at[pl.ds(at * UNIT, UNIT), :], sems.at[64 + at])
            )
        for copy in copies:
            copy.start()
        pos = where_ref[0]
        row = lax.broadcasted_iota(jnp.int32, (PR, PR), 0)
        col = lax.broadcasted_iota(jnp.int32, (PR, PR), 1)
        tri = jnp.where(col <= row, 0.0, neg_fill)
        for part in range(2):
            mine = jnp.bitwise_xor(pos, BLOCKS[part])
            for block in range(8):
                at = (pl.ds(part * PR, PR), pl.ds(block * PR, PR))
                if block == part:
                    bias_ref[at] = tri
                else:
                    seen = jnp.bitwise_xor(pos, BLOCKS[block]) < mine
                    bias_ref[at] = jnp.full((PR, PR), jnp.where(seen, 0.0, neg_fill), F32)
        for copy in copies:
            copy.wait()
        late[0].start()
        fill_normed(x_ref, gain_row(w_ref[0, :, HALF:]), normed_ref)
        late[1].start()

    at = pl.ds(pl.multiple_of(step * UNIT, UNIT), UNIT)
    at_k = pl.ds(pl.multiple_of(D + step * UNIT, UNIT), UNIT)
    k_ref[...] = dot_nn(normed_ref[...], w_ref[0, :, at_k]).astype(BF)
    v_ref[...] = dot_nn(normed_ref[...], w_ref[1, :, at]).astype(BF)
    wq = w_ref[0, :, at]
    q_ref[0:UNIT, :] = (dot_nn(normed_ref[0:UNIT, :], wq) * SCALE).astype(BF)
    q_ref[UNIT:, :] = (dot_nn(normed_ref[PLEN:, :], wq) * SCALE).astype(BF)
    row = lax.broadcasted_iota(jnp.int32, (PR, PR), 0)
    col = lax.broadcasted_iota(jnp.int32, (PR, PR), 1)
    tri = jnp.where(col <= row, 0.0, neg_fill)
    low_half = lane_half(0)
    for pair in range(2):
        lanes = slice(pair * WIDTH, (pair + 1) * WIDTH)
        query = q_ref[:, lanes]
        for head in range(2):
            rows = slice(head * ROWS, (head + 1) * ROWS)
            qs_ref[rows, :] = jnp.where(lane_half(head), query, jnp.zeros_like(query))
        s_ref[...] = dot_nt(qs_ref[...], k_ref[0:PLEN, lanes])
        for head in range(2):
            for chunk in range(4):
                mine = slice(chunk * PR, (chunk + 1) * PR)
                rows = slice(head * ROWS + chunk * PR, head * ROWS + (chunk + 1) * PR)
                scores = s_ref[rows, :]
                if chunk < 2:
                    scores = scores + bias_ref[mine, :]
                    top = jnp.max(scores, axis=-1, keepdims=True)
                    terms = jnp.exp(scores - top)
                    total = jnp.sum(terms, axis=-1, keepdims=True)
                else:
                    own = slice(PLEN + (chunk - 2) * PR, PLEN + (chunk - 1) * PR)
                    near = dot_nt(qs_ref[rows, :], k_ref[own, lanes]) + tri
                    top = jnp.maximum(
                        jnp.max(scores, axis=-1, keepdims=True),
                        jnp.max(near, axis=-1, keepdims=True),
                    )
                    terms = jnp.exp(scores - top)
                    near_terms = jnp.exp(near - top)
                    total = jnp.sum(terms, axis=-1, keepdims=True) + jnp.sum(
                        near_terms, axis=-1, keepdims=True
                    )
                    ec_ref[2 * pair + head, (chunk - 2) * PR : (chunk - 1) * PR, :] = (
                        near_terms.astype(BF)
                    )
                e_ref[2 * pair + head, mine, :] = terms.astype(BF)
                inv_ref[rows, :] = jnp.broadcast_to(1.0 / total, (PR, WIDTH))
        terms = e_ref[2 * pair : 2 * pair + 2].reshape(2 * ROWS, PLEN)
        out_ref[...] = dot_nn(terms, v_ref[0:PLEN, lanes])
        for head in range(2):
            for side in range(2):
                own = slice(PLEN + side * PR, PLEN + (side + 1) * PR)
                start = head * ROWS + (2 + side) * PR
                near = ec_ref[2 * pair + head, side * PR : (side + 1) * PR, :]
                out_ref[start : start + PR, :] += dot_nn(near, v_ref[own, lanes])
        inv = jnp.where(low_half, inv_ref[0:ROWS, :], inv_ref[ROWS:, :])
        r_ref[:, lanes] = inv
        o_ref[:, lanes] = (
            jnp.where(low_half, out_ref[0:ROWS, :], out_ref[ROWS:, :]) * inv
        ).astype(BF)
    att_ref[step] = o_ref[...]

    @pl.when(step == pl.num_programs(0) - 1)
    def _():
        wout = w_ref[1, :, D:HALF]
        gain = gain_row(w_ref[1, :, HALF:])
        for chunk in range(4):
            rows = slice(chunk * PR, (chunk + 1) * PR)
            from_row = chunk * PR if chunk < 2 else PLEN + (chunk - 2) * PR
            middle = x_ref[from_row : from_row + PR, :].astype(F32)
            for i in range(3):
                middle = middle + dot_nn(att_ref[i, rows, :], wout[i * UNIT : (i + 1) * UNIT, :])
            mid_ref[rows, :] = middle
            nm_ref[rows, :] = (middle * rms_inv(middle) * gain).astype(BF)
        for copy in late:
            copy.wait()


def attn_fwd(where, parts, pieces):
    pair = lambda i: (0, i)
    whole = lambda i: (0, 0)
    heads = lambda i: (i, 0, 0)
    anywhere = pl.BlockSpec(memory_space=pl.ANY)
    return pl.pallas_call(
        attn_fwd_kernel,
        grid=(3,),
        in_specs=[
            pl.BlockSpec(memory_space=pltpu.SMEM),
            *[anywhere] * 13,
        ],
        out_specs=[
            anywhere,
            pl.BlockSpec((ROWS, UNIT), pair),
            pl.BlockSpec((KEYS, UNIT), pair),
            pl.BlockSpec((KEYS, UNIT), pair),
            pl.BlockSpec((4, ROWS, PLEN), heads),
            pl.BlockSpec((4, UNIT, PR), heads),
            pl.BlockSpec((ROWS, UNIT), pair),
            pl.BlockSpec((ROWS, UNIT), pair),
            pl.BlockSpec((ROWS, D), whole),
            pl.BlockSpec((ROWS, D), whole),
            anywhere,
        ],
        out_shape=[
            shape((2, D, WIDE), BF),
            shape((ROWS, D), BF),
            shape((KEYS, D), BF),
            shape((KEYS, D), BF),
            shape((HEADS, ROWS, PLEN), BF),
            shape((HEADS, 2 * PR, PR), BF),
            shape((ROWS, D), BF),
            shape((ROWS, D), F32),
            shape((ROWS, D), F32),
            shape((ROWS, D), BF),
            shape((KEYS, D), BF),
        ],
        scratch_shapes=[
            pltpu.VMEM((2, D, WIDE), BF),
            pltpu.VMEM((KEYS, D), BF),
            pltpu.VMEM((KEYS, D), BF),
            pltpu.VMEM((2 * PR, PLEN), F32),
            pltpu.VMEM((3, ROWS, UNIT), BF),
            pltpu.VMEM((2 * ROWS, WIDTH), BF),
            pltpu.VMEM((2 * ROWS, PLEN), F32),
            pltpu.VMEM((2 * ROWS, WIDTH), F32),
            pltpu.VMEM((2 * ROWS, WIDTH), F32),
            pltpu.SemaphoreType.DMA((69,)),
            pltpu.SemaphoreType.DMA((2,)),
        ],
        compiler_params=params(),
        cost_estimate=pl.CostEstimate(
            flops=30_000_000_000, bytes_accessed=30_000_000, transcendentals=6_300_000
        ),
    )(where, *parts, *pieces)


def mlp_kernel(
    where_ref, nm0_ref, nm1_ref, g0_ref, g1_ref,
    up00_ref, up10_ref, up01_ref, up11_ref, down00_ref, down10_ref, down01_ref, down11_ref,
    e_ref, y_ref, give_e_ref, give_y_ref, up_keep_ref, up_give_ref, down_keep_ref, down_give_ref,
    wup_ref, wdown_ref, nm_ref, g_ref, acc_e_ref, acc_y_ref, part_ref, active_ref, d_hidden_ref, sems,
):
    step = pl.program_id(0)
    side, y_at = where_ref[1], where_ref[0] % 2

    @pl.when(step == 0)
    def _():
        copies = []
        for dy, ups, downs in (
            (0, (up00_ref, up10_ref), (down00_ref, down10_ref)),
            (1, (up01_ref, up11_ref), (down01_ref, down11_ref)),
        ):
            for dx in range(2):
                for i in range(4):
                    block = where_ref[8 + dy * 4 + i] * 2 + jnp.bitwise_xor(side, dx)
                    rows = pl.ds(pl.multiple_of(block * SUB, 16), SUB)
                    for half in range(2):
                        copies.append(
                            pltpu.make_async_copy(
                                ups[dx].at[i, pl.ds(half * SUB, SUB), :],
                                wup_ref.at[rows, pl.ds(half * D, D)],
                                sems.at[len(copies)],
                            )
                        )
                    copies.append(
                        pltpu.make_async_copy(
                            downs[dx].at[i],
                            wdown_ref.at[pl.ds(pl.multiple_of(block * FSUB, 16), FSUB), :],
                            sems.at[len(copies)],
                        )
                    )
        for copy in copies:
            copy.start()
        nm_ref[0:ROWS, :] = nm0_ref[...]
        nm_ref[ROWS:, :] = nm1_ref[...]
        g_ref[0:ROWS, :] = g0_ref[...]
        g_ref[ROWS:, :] = g1_ref[...]
        for copy in copies:
            copy.wait()

    at = pl.ds(pl.multiple_of(step * D, D), D)
    for start in range(0, 2 * ROWS, 256):
        rows = slice(start, start + 256)
        hidden = dot_nn(nm_ref[rows, :], wup_ref[:, at])
        square = hidden * hidden
        th = jnp.tanh(hidden * (GELU_C + GELU_C * GELU_A * square))
        left = 0.5 + 0.5 * th
        active_ref[rows, :] = (hidden * left).astype(BF)
        slope = left + hidden * (0.5 - 0.5 * th * th) * (GELU_C + 3.0 * GELU_A * GELU_C * square)
        d_hidden_ref[rows, :] = (dot_nt(g_ref[rows, :], wdown_ref[at, :]) * slope).astype(BF)
    part_y = dot_nn(active_ref[...], wdown_ref[at, :])
    part_e = dot_nt(d_hidden_ref[...], wup_ref[:, at])

    @pl.when(step == 0)
    def _():
        acc_y_ref[...] = part_y
        acc_e_ref[...] = part_e

    @pl.when(step == 1)
    def _():
        e_ref[...] = (acc_e_ref[0:ROWS, :] + part_e[0:ROWS]).astype(BF)
        y_ref[...] = (acc_y_ref[0:ROWS, :] + part_y[0:ROWS]).astype(BF)
        give_e_ref[...] = (acc_e_ref[ROWS:, :] + part_e[ROWS:]).astype(BF)
        give_y_ref[...] = (acc_y_ref[ROWS:, :] + part_y[ROWS:]).astype(BF)

    part_ref[...] = dot_tn(nm_ref[...], d_hidden_ref[...]).astype(BF).reshape(16, SUB, D)
    at_half = pl.ds(pl.multiple_of(step * SUB, 16), SUB)
    for s in range(8):
        up_keep_ref[s, at_half, :] = part_ref[2 * s + side]
        up_give_ref[s, at_half, :] = part_ref[2 * s + 1 - side]
    part_ref[...] = dot_tn(active_ref[...], g_ref[...]).astype(BF).reshape(16, SUB, D)
    for z in range(2):
        for x in range(2):
            for h in range(2):
                at_h = pl.ds(h * SUB, SUB)
                row = 8 * z + 2 * x + h
                down_keep_ref[z, x, at_h, :] = part_ref[row + 4 * y_at]
                down_give_ref[z, x, at_h, :] = part_ref[row + 4 - 4 * y_at]


def mlp(where, normed, grads, pieces):
    whole = pl.BlockSpec((ROWS, D), lambda i: (0, 0))
    anywhere = pl.BlockSpec(memory_space=pl.ANY)
    return pl.pallas_call(
        mlp_kernel,
        grid=(2,),
        in_specs=[pl.BlockSpec(memory_space=pltpu.SMEM)] + [whole] * 4 + [anywhere] * 8,
        out_specs=[whole] * 4
        + [pl.BlockSpec((8, 2 * SUB, D), lambda i: (0, 0, 0))] * 2
        + [pl.BlockSpec((2, 2, FSUB, D), lambda i: (i, 0, 0, 0))] * 2,
        out_shape=[shape((ROWS, D), BF)] * 4
        + [shape((8, 2 * SUB, D), BF)] * 2
        + [shape((4, 2, FSUB, D), BF)] * 2,
        scratch_shapes=[
            pltpu.VMEM((D, FH), BF),
            pltpu.VMEM((FH, D), BF),
            pltpu.VMEM((2 * ROWS, D), BF),
            pltpu.VMEM((2 * ROWS, D), BF),
            pltpu.VMEM((2 * ROWS, D), F32),
            pltpu.VMEM((2 * ROWS, D), F32),
            pltpu.VMEM((16, SUB, D), BF),
            pltpu.VMEM((2 * ROWS, D), BF),
            pltpu.VMEM((2 * ROWS, D), BF),
            pltpu.SemaphoreType.DMA((48,)),
        ],
        compiler_params=params(),
        cost_estimate=pl.CostEstimate(
            flops=20_000_000_000, bytes_accessed=20_000_000, transcendentals=1_600_000
        ),
    )(where, *normed, *grads, *pieces)


def branch_kernel(
    mid_ref, g_ref, e0_ref, e1_ref, att_ref, w_ref, dmid_ref, datt_ref, right_ref,
    low_ref, prod_ref,
):
    gain = gain_row(w_ref[0, :, HALF:])
    wout = w_ref[0, :, D:HALF]
    for chunk in range(4):
        rows = slice(chunk * PR, (chunk + 1) * PR)
        middle = mid_ref[rows, :]
        inv = rms_inv(middle)
        unit = middle * inv
        grad = e0_ref[rows, :].astype(F32) + e1_ref[rows, :].astype(F32)
        scaled = gain * grad
        mean = jnp.mean(unit * scaled, axis=-1, keepdims=True)
        d_mid = g_ref[rows, :].astype(F32) + inv * (scaled - unit * mean)
        dmid_ref[rows, :] = d_mid
        prod_ref[rows, :] = (grad * unit).astype(BF)
        branch = d_mid.astype(BF)
        low_ref[rows, :] = branch
        datt_ref[rows, :] = dot_nt(branch, wout).astype(BF)
    right_ref[:, D:] = dot_tn(prod_ref[...], jnp.ones((ROWS, 128), BF)).astype(BF)
    right_ref[:, 0:D] = dot_tn(att_ref[...], low_ref[...]).astype(BF)


def branch(middle, d_out, own, given, attended, w_all):
    return pl.pallas_call(
        branch_kernel,
        grid=(1,),
        in_specs=[pl.BlockSpec((ROWS, D), lambda i: (0, 0))] * 5
        + [pl.BlockSpec((1, D, WIDE), lambda i: (1, 0, 0))],
        out_specs=[
            pl.BlockSpec((ROWS, D), lambda i: (0, 0)),
            pl.BlockSpec((ROWS, D), lambda i: (0, 0)),
            pl.BlockSpec((D, RIGHT), lambda i: (0, 0)),
        ],
        out_shape=[shape((ROWS, D), F32), shape((ROWS, D), BF), shape((D, RIGHT), BF)],
        scratch_shapes=[pltpu.VMEM((ROWS, D), BF), pltpu.VMEM((ROWS, D), BF)],
        compiler_params=params(),
        cost_estimate=pl.CostEstimate(
            flops=2_000_000_000, bytes_accessed=9_000_000, transcendentals=1000
        ),
    )(middle, d_out, own, given, attended, w_all)


def attn_bwd_kernel(units, *refs):
    first, last = units == (2,), units[0] == 0
    q_ref, g_ref, o_ref, r_ref, *refs = refs
    keyed = []
    for _ in units:
        keyed.append(refs[:3])
        refs = refs[3:]
    if last:
        ec_ref, kc_ref, vc_ref, *refs = refs
    if not first:
        dq_in_ref, *refs = refs
    wk_ref, wv_ref, *refs = refs
    if last:
        where_ref, wq_ref, normed_ref, kv1_ref, kv2_ref, kv3_ref, *refs = refs
        x_parts, refs = refs[:5], refs[5:]
        f1_ref, f2_ref, f3_ref, right_ref, *refs = refs
        keep_ref, give_ref, f0_ref, fc_ref, *refs = refs
        late_in = (wq_ref, wk_ref, wv_ref, normed_ref, right_ref, *x_parts)
        *late, sems_late = refs[:7]
        refs = refs[7:]
        wq_ref, wk_ref, wv_ref, normed_ref, right_ref, x_ref = late
        late = late[:5] + [x_ref.at[pl.ds(at * UNIT, UNIT), :] for at in range(5)]
        dkv_ref, dq_ref, low_ref, high_ref, prod_ref, sems, *refs = refs
    else:
        dkv_refs, refs = refs[: len(units)], refs[len(units) :]
        f_refs, refs = refs[: len(units)], refs[len(units) :]
        dq_ref, *refs = refs
    qs_ref, gs_ref, ds_ref, *refs = refs
    if last:
        sum_ref, near_ref, near_e_ref, near_qs_ref, near_gs_ref = refs
    step = pl.program_id(0)

    def late_copies():
        sources = (
            late_in[0].at[pl.ds(0, 1), :, pl.ds(0, D)],
            late_in[1].at[pl.ds(0, 1), :, pl.ds(D, D)],
            late_in[2].at[pl.ds(1, 1), :, pl.ds(0, D)],
            *late_in[3:],
        )
        return [
            pltpu.make_async_copy(source, target, sems_late.at[at])
            for at, (source, target) in enumerate(zip(sources, late))
        ]

    if last:

        @pl.when(step == 0)
        def _():
            for at, ref in enumerate((kv1_ref, kv2_ref, kv3_ref)):
                rows = pl.ds((at + 1) * UNIT, UNIT)
                pltpu.make_async_copy(ref, dkv_ref.at[:, rows, :], sems.at[at]).start()
            for copy in late_copies():
                copy.start()

    low_half = lane_half(0)
    for pair in range(2):
        lanes = slice(pair * WIDTH, (pair + 1) * WIDTH)
        lanes_v = slice((2 + pair) * WIDTH, (3 + pair) * WIDTH)
        scaled_grad = g_ref[:, lanes].astype(F32) * r_ref[:, lanes]
        prod = scaled_grad * o_ref[:, lanes].astype(F32)
        low_grad = scaled_grad.astype(BF)
        query = q_ref[:, lanes]
        deltas = []
        for head in range(2):
            half = lane_half(head)
            rows = slice(head * ROWS, (head + 1) * ROWS)
            deltas.append(jnp.sum(jnp.where(half, prod, 0.0), axis=-1, keepdims=True))
            gs_ref[rows, :] = jnp.where(half, low_grad, jnp.zeros_like(low_grad))
            qs_ref[rows, :] = jnp.where(half, query, jnp.zeros_like(query))
        delta = jnp.concatenate(deltas, axis=0)
        d_query = None
        for u, (e_ref, k_ref, v_ref) in enumerate(keyed):
            out_ref = dkv_ref if last else dkv_refs[u]
            terms = e_ref[2 * pair : 2 * pair + 2].reshape(2 * ROWS, UNIT)
            d_soft = dot_nt(gs_ref[...], v_ref[:, lanes])
            ds_ref[...] = terms * (d_soft - delta).astype(BF)
            more = dot_nn(ds_ref[...], k_ref[:, lanes])
            d_query = more if d_query is None else d_query + more
            out_ref[step, 0:UNIT, lanes] = dot_tn(ds_ref[...], qs_ref[...]).astype(BF)
            out_ref[step, 0:UNIT, lanes_v] = dot_tn(terms, gs_ref[...]).astype(BF)
        total = jnp.where(low_half, d_query[0:ROWS], d_query[ROWS:])
        if not first:
            total = total + dq_in_ref[:, lanes]
        if not last:
            dq_ref[:, lanes] = total
            continue
        sum_ref[...] = total
        for side in range(2):
            own = slice(side * PR, (side + 1) * PR)
            mine = slice((2 + side) * PR, (3 + side) * PR)
            near_q = []
            for head in range(2):
                rows = slice(head * ROWS + mine.start, head * ROWS + mine.stop)
                at = slice(head * PR, (head + 1) * PR)
                near = ec_ref[2 * pair + head, own, :]
                d_soft = dot_nt(gs_ref[rows, :], vc_ref[own, lanes])
                near_ref[at, :] = near * (d_soft - deltas[head][mine]).astype(BF)
                near_e_ref[at, :] = near
                near_qs_ref[at, :] = qs_ref[rows, :]
                near_gs_ref[at, :] = gs_ref[rows, :]
                near_q.append(dot_nn(near_ref[at, :], kc_ref[own, lanes]))
            sum_ref[mine, :] += jnp.where(low_half, near_q[0], near_q[1])
            rows = slice(PLEN + side * PR, PLEN + (side + 1) * PR)
            dkv_ref[step, rows, lanes] = dot_tn(near_ref[...], near_qs_ref[...]).astype(BF)
            dkv_ref[step, rows, lanes_v] = dot_tn(near_e_ref[...], near_gs_ref[...]).astype(BF)
        dq_ref[step, :, lanes] = (sum_ref[...] * SCALE).astype(BF)

    def back_to_rows(dkv, rows):
        grad = None
        for i in range(3):
            at = slice(i * UNIT, (i + 1) * UNIT)
            more = dot_nt(dkv[i, rows, 0:UNIT], wk_ref[0, :, at])
            more = more + dot_nt(dkv[i, rows, UNIT:], wv_ref[0, :, at])
            grad = more if grad is None else grad + more
        return grad

    @pl.when(step == pl.num_programs(0) - 1)
    def _():
        if not last:
            for dkv, f_ref in zip(dkv_refs, f_refs):
                f_ref[...] = back_to_rows(dkv, slice(0, UNIT)).astype(BF)
            return
        for at, ref in enumerate((kv1_ref, kv2_ref, kv3_ref)):
            rows = pl.ds((at + 1) * UNIT, UNIT)
            pltpu.make_async_copy(ref, dkv_ref.at[:, rows, :], sems.at[at]).wait()
        for copy in late_copies():
            copy.wait()
        high_ref[:, D:] = right_ref[...]
        for out_ref, rows, q_rows in (
            (f0_ref, slice(0, UNIT), slice(0, UNIT)),
            (fc_ref, slice(PLEN, KEYS), slice(UNIT, ROWS)),
        ):
            grad = back_to_rows(dkv_ref, rows)
            for i in range(3):
                at = slice(i * UNIT, (i + 1) * UNIT)
                grad = grad + dot_nt(dq_ref[i, q_rows, :], wq_ref[0, :, at])
            out_ref[...] = grad
        for at, f_ref in enumerate((f0_ref, f1_ref, f2_ref, f3_ref, fc_ref)):
            rows = slice(at * UNIT, (at + 1) * UNIT)
            tokens = x_ref[rows, :].astype(F32)
            prod_ref[rows, :] = (f_ref[...].astype(F32) * (tokens * rms_inv(tokens))).astype(BF)
        low_ref[:, HALF:] = dot_tn(prod_ref[...], jnp.ones((KEYS, 128), BF)).astype(BF)
        for i in range(3):
            at = slice(i * UNIT, (i + 1) * UNIT)
            low_ref[:, at] = (
                dot_tn(normed_ref[0:UNIT, :], dq_ref[i, 0:UNIT, :])
                + dot_tn(normed_ref[PLEN:, :], dq_ref[i, UNIT:, :])
            ).astype(BF)
            both = dot_tn(normed_ref[...], dkv_ref[i]).astype(BF)
            low_ref[:, D + i * UNIT : D + (i + 1) * UNIT] = both[:, 0:UNIT]
            high_ref[:, at] = both[:, UNIT:]

        for core, low_out, high_out in ((0, keep_ref, give_ref), (1, give_ref, keep_ref)):

            @pl.when(where_ref[2] == core)
            def _():
                copies = [
                    pltpu.make_async_copy(low_ref, low_out, sems.at[3]),
                    pltpu.make_async_copy(high_ref, high_out, sems.at[4]),
                ]
                for copy in copies:
                    copy.start()
                for copy in copies:
                    copy.wait()


def attn_bwd(units, saved, d_att, w_all, dq=None, rest=None):
    first, last = units == (2,), units[0] == 0
    q, k, v, e, ec, o, r = saved
    width = 2 * WIDTH
    lanes = lambda i: (0, i)
    full = lambda *dims: pl.BlockSpec(dims, lambda i: (0,) * len(dims))
    rows = pl.BlockSpec((ROWS, width), lanes)
    anywhere = pl.BlockSpec(memory_space=pl.ANY)
    weight = lambda half, at: pl.BlockSpec((1, D, D), lambda i: (half, 0, at))
    specs, args = [rows] * 4, [q, d_att, o, r]
    for u in units:
        specs += [
            pl.BlockSpec((4, ROWS, UNIT), lambda i, u=u: (i, 0, u)),
            pl.BlockSpec((UNIT, width), lambda i, u=u: (u, i)),
            pl.BlockSpec((UNIT, width), lambda i, u=u: (u, i)),
        ]
        args += [e, k, v]
    if last:
        specs += [
            pl.BlockSpec((4, UNIT, PR), lambda i: (i, 0, 0)),
            pl.BlockSpec((UNIT, width), lambda i: (4, i)),
            pl.BlockSpec((UNIT, width), lambda i: (4, i)),
        ]
        args += [ec, k, v]
    if not first:
        specs.append(rows)
        args.append(dq)
    specs += [anywhere, anywhere] if last else [weight(0, 1), weight(1, 0)]
    args += [w_all, w_all]
    kv = (3, UNIT, 2 * UNIT)
    if last:
        where, parts, normed, kvs, fs, right = rest
        specs += [pl.BlockSpec(memory_space=pltpu.SMEM)] + [anywhere] * 10
        specs += [full(UNIT, D)] * 3 + [anywhere]
        args += [where, w_all, normed, *kvs, *parts, *fs, right]
        outs = [anywhere, anywhere, full(UNIT, D), full(UNIT, D)]
        out_shapes = [shape((D, WIDE), BF)] * 2 + [shape((UNIT, D), F32)] * 2
        scratch = [
            pltpu.VMEM((1, D, D), BF),
            pltpu.VMEM((1, D, D), BF),
            pltpu.VMEM((1, D, D), BF),
            pltpu.VMEM((KEYS, D), BF),
            pltpu.VMEM((D, RIGHT), BF),
            pltpu.VMEM((KEYS, D), BF),
            pltpu.SemaphoreType.DMA((10,)),
            pltpu.VMEM((3, KEYS, 2 * UNIT), BF),
            pltpu.VMEM((3, ROWS, UNIT), BF),
            pltpu.VMEM((D, WIDE), BF),
            pltpu.VMEM((D, WIDE), BF),
            pltpu.VMEM((KEYS, D), BF),
            pltpu.SemaphoreType.DMA((5,)),
        ]
    else:
        outs = [full(*kv)] * len(units) + [full(UNIT, D)] * len(units) + [rows]
        out_shapes = [shape(kv, BF)] * len(units) + [shape((UNIT, D), BF)] * len(units)
        out_shapes.append(shape((ROWS, D), F32))
        scratch = []
    return pl.pallas_call(
        lambda *refs: attn_bwd_kernel(units, *refs),
        grid=(3,),
        in_specs=specs,
        out_specs=outs,
        out_shape=out_shapes,
        scratch_shapes=scratch
        + [
            pltpu.VMEM((2 * ROWS, WIDTH), BF),
            pltpu.VMEM((2 * ROWS, WIDTH), BF),
            pltpu.VMEM((2 * ROWS, UNIT), BF),
        ]
        + ([pltpu.VMEM((ROWS, WIDTH), F32)] + [pltpu.VMEM((UNIT, WIDTH), BF)] * 4 if last else []),
        compiler_params=params(),
        cost_estimate=pl.CostEstimate(
            flops=10_000_000_000 * (len(units) + last), bytes_accessed=10_000_000, transcendentals=1000
        ),
    )(*args)


def tail_kernel(near_ref, cont_ref, f0_ref, f1_ref, f3_ref, fc_ref, dmid_ref, w_ref, keep_ref, give_ref):
    gain = gain_row(w_ref[0])
    for chunk in range(4):
        rows = slice(chunk * PR, (chunk + 1) * PR)
        at = slice(chunk % 2 * PR, (chunk % 2 + 1) * PR)
        part = (near_ref if chunk < 2 else cont_ref)[at, :].astype(F32)
        inv = rms_inv(part)
        unit = part * inv
        if chunk < 2:
            grad = f0_ref[rows, :].astype(F32)
            for f_ref in (f1_ref, f3_ref):
                grad = grad + f_ref[rows, :].astype(F32)
        else:
            grad = fc_ref[(chunk - 2) * PR : (chunk - 1) * PR, :]
        scaled = gain * grad
        mean = jnp.mean(unit * scaled, axis=-1, keepdims=True)
        out_ref = give_ref if chunk % 2 else keep_ref
        at = slice(chunk // 2 * PR, (chunk // 2 + 1) * PR)
        out_ref[at, :] = (dmid_ref[rows, :] + inv * (scaled - unit * mean)).astype(out_ref.dtype)


def tail(near, cont, f_parts, f_cont, d_mid, w_all):
    whole = lambda i: (0, 0)
    half = pl.BlockSpec((2 * PR, D), whole)
    full = pl.BlockSpec((ROWS, D), whole)
    return pl.pallas_call(
        tail_kernel,
        grid=(1,),
        in_specs=[half, half, half, half, half, half, full]
        + [pl.BlockSpec((1, D, 128), lambda i: (0, 0, HALF // 128))],
        out_specs=[half, half],
        out_shape=[shape((2 * PR, D), F32), shape((2 * PR, D), BF)],
        compiler_params=params(),
        cost_estimate=pl.CostEstimate(flops=20_000_000, bytes_accessed=7_000_000, transcendentals=1000),
    )(near, cont, *f_parts, f_cont, d_mid, w_all)


def total_of(*parts):
    total = parts[0].astype(F32)
    for part in parts[1:]:
        total = total + part.astype(F32)
    return total.astype(BF)


def run_whole(kernel, outs, *args, dtype=BF):
    return pl.pallas_call(
        kernel,
        in_specs=[pl.BlockSpec(memory_space=pltpu.SMEM)]
        + [pl.BlockSpec(memory_space=pltpu.VMEM)] * (len(args) - 1),
        out_specs=[pl.BlockSpec(memory_space=pltpu.VMEM)] * len(outs),
        out_shape=[shape(dims, dtype) for dims in outs],
        compiler_params=params(),
        cost_estimate=pl.CostEstimate(flops=1_000_000, bytes_accessed=7_000_000, transcendentals=0),
    )(*args)


def fold_two_kernel(where_ref, a0_ref, a1_ref, b0_ref, b1_ref, ak_ref, ag_ref, bk_ref, bg_ref):
    y_at, side = where_ref[0] % 2, where_ref[1]
    for z in range(4):
        ak_ref[z] = total_of(a0_ref[z, y_at], a1_ref[z, y_at])
        ag_ref[z] = total_of(a0_ref[z, 1 - y_at], a1_ref[z, 1 - y_at])
        bk_ref[z] = total_of(b0_ref[z, side], b1_ref[z, side])
        bg_ref[z] = total_of(b0_ref[z, 1 - side], b1_ref[z, 1 - side])


def fold_rows_kernel(where_ref, a0_ref, a1_ref, b0_ref, b1_ref, *outs):
    z_at = where_ref[0] // 2
    rows = a0_ref.shape[1]
    for step, out_ref in enumerate(outs):
        z = jnp.bitwise_xor(z_at, step)
        out_ref[0:rows, :] = total_of(a0_ref[z], a1_ref[z])
        out_ref[rows:, :] = total_of(b0_ref[z], b1_ref[z])


def fold_cols_kernel(where_ref, a0_ref, a1_ref, b0_ref, b1_ref, *outs):
    z_at = where_ref[0] // 2
    cols = a0_ref.shape[2]
    for step, out_ref in enumerate(outs):
        z = jnp.bitwise_xor(z_at, step)
        out_ref[:, 0:cols] = total_of(a0_ref[z], a1_ref[z])
        out_ref[:, cols:] = total_of(b0_ref[z], b1_ref[z])


def fold_core_kernel(where_ref, own_ref, got_ref, ak_ref, ag_ref, bk_ref, bg_ref):
    y_at, side = where_ref[0] % 2, where_ref[1]
    left, right = slice(0, LEFT), slice(LEFT, WIDE)

    def block(s, x, cols):
        rows = pl.ds(pl.multiple_of((2 * s + x) * SUB, 16), SUB)
        return total_of(own_ref[rows, cols], got_ref[rows, cols])

    for s in range(8):
        ak_ref[s // 2, s % 2] = block(s, side, left)
        ag_ref[s // 2, s % 2] = block(s, 1 - side, left)
    for z in range(4):
        for x in range(2):
            bk_ref[z, x] = block(2 * z + y_at, x, right)
            bg_ref[z, x] = block(2 * z + 1 - y_at, x, right)


def split_cols_kernel(where_ref, a0_ref, a1_ref, a2_ref, a3_ref, left_ref, right_ref):
    for at, ref in enumerate((a0_ref, a1_ref, a2_ref, a3_ref)):
        left_ref[at] = ref[:, 0:LEFT]
        right_ref[at] = ref[:, LEFT:]


def join_kernel(where_ref, a0_ref, a1_ref, b0_ref, b1_ref, left_ref, right_ref):
    for out_ref, parts in ((left_ref, (a0_ref, a1_ref)), (right_ref, (b0_ref, b1_ref))):
        out_ref[0:4] = parts[0][...]
        out_ref[4:8] = parts[1][...]


def split_rows_kernel(where_ref, m0_ref, m1_ref, m2_ref, m3_ref, up_ref, down_ref):
    for at, ref in enumerate((m0_ref, m1_ref, m2_ref, m3_ref)):
        up_ref[at] = ref[0 : 2 * SUB, :]
        down_ref[at] = ref[2 * SUB :, :]


def unpack_kernel(where_ref, here_ref, far_ref, up_ref, down_ref):
    side, core = where_ref[1], where_ref[2]
    first = core == 0
    for x in range(2):
        at = jnp.bitwise_xor(side, x)
        rows = slice(x * SUB, (x + 1) * SUB)
        here, far = here_ref[at].astype(F32), far_ref[at].astype(F32)
        low, high = jnp.where(first, here, far), jnp.where(first, far, here)
        down_ref[x * FSUB : (x + 1) * FSUB, :] = low[2 * SUB :]
        down_ref[(2 + x) * FSUB : (3 + x) * FSUB, :] = high[2 * SUB :]
        for half in range(2):
            own = slice(half * SUB, (half + 1) * SUB)
            for i in range(4):
                cols = slice(i * 2 * FSUB, (i + 1) * 2 * FSUB)
                start = (half * 4 + i) * 4 * FSUB
                up_ref[rows, start : start + 4 * FSUB] = jnp.concatenate(
                    [low[own, cols], high[own, cols]], axis=1
                )


def finish_kernel(
    where_ref, own_ref, side_ref, core_ref, far_ref, qkv_ref, out_ref, gain_a_ref, gain_m_ref
):
    first, near = where_ref[2] == 0, where_ref[1] == 0
    columns = []
    for x in range(2):
        mine = jnp.where(near == (x == 0), own_ref[...], side_ref[...]).astype(F32)
        theirs = jnp.where(near == (x == 0), core_ref[...], far_ref[...]).astype(F32)
        low, high = jnp.where(first, mine, theirs), jnp.where(first, theirs, mine)
        rows = slice(x * SUB, (x + 1) * SUB)
        qkv_ref[rows, 0:HALF] = low[:, 0:HALF]
        qkv_ref[rows, HALF:] = high[:, 0:D]
        out_ref[rows, :] = high[:, D:HALF]
        columns.append((low[:, HALF:], high[:, HALF:]))
    for at, gain_ref in enumerate((gain_a_ref, gain_m_ref)):
        both = jnp.concatenate([columns[0][at], columns[1][at]], axis=0)
        gain_ref[...] = both.T[0:1, :]


def over(axis, value, bits):
    return lax.ppermute(value, axis, [(i, i ^ bits) for i in range(lax.axis_size(axis))])


def cut(values, start, rows=PR):
    return lax.dynamic_slice_in_dim(values, start, rows, 0)


def pick(values, at):
    return lax.dynamic_index_in_dim(values, at, 0, keepdims=False)


def pick_of(values, at, axis):
    return lax.dynamic_index_in_dim(values, at, axis, keepdims=False)


def tie(*values):
    return lax.optimization_barrier(values)


def per_device(tokens, w_qkv, w_out, w_up, w_down, gain_attn, gain_mlp, d_out):
    staged = lax.axis_size("shard") == 8
    shard = lax.axis_index("shard")
    rep = lax.axis_index("rep")
    side, core = rep // 2, rep % 2
    pos = shard % 8
    y_at, z_at = pos % 2, pos // 2
    table = [pos ^ d for d in ORDER] if staged else [jnp.int32(2 * (d % 4) + d // 4) for d in range(8)]
    where = jnp.stack([pos, side, core] + [jnp.int32(0)] * 5 + table).astype(jnp.int32)

    def to_give(values):
        return jnp.concatenate([cut(values, (1 - y_at) * PR), cut(values, (3 - y_at) * PR)], axis=0)

    def own_parts(values, got):
        mine_p, mine_c = cut(values, y_at * PR), cut(values, (2 + y_at) * PR)
        return (
            jnp.concatenate([mine_p, got[:PR]], axis=0), jnp.concatenate([mine_c, got[PR:]], axis=0)
        )

    def to_return(values):
        return jnp.concatenate([values[PR : 2 * PR], values[3 * PR :]], axis=0)

    def home_rows(keep_p, keep_c, got):
        got = got.astype(keep_p.dtype)
        first = y_at == 0
        return jnp.concatenate(
            [
                jnp.where(first, keep_p, got[:PR]),
                jnp.where(first, got[:PR], keep_p),
                jnp.where(first, keep_c, got[PR:]),
                jnp.where(first, got[PR:], keep_c),
            ],
            axis=0,
        )

    def halves(qkv, out, gain_a, gain_m):
        wide = lambda gain: jnp.broadcast_to(gain[:, None], (gain.shape[0], 128))
        return (
            jnp.concatenate([qkv[:, :HALF], wide(gain_a)], axis=1),
            jnp.concatenate([qkv[:, HALF:], out, wide(gain_m)], axis=1),
        )

    def half_up(up):
        return pick_of(up.reshape(up.shape[0], 8, 2, 2 * FSUB), core, 2).reshape(up.shape[0], FH)

    def own_up(up):
        mine = half_up(cut(up, side * SUB, SUB))
        return jnp.concatenate([mine[:, :D], mine[:, D:]], axis=0)

    if staged:
        low, high = halves(w_qkv, w_out, gain_attn, gain_mlp)
        own_piece = cut(jnp.where(core == 0, low, high), side * SUB, SUB)
        own_mlp = jnp.concatenate(
            [own_up(w_up), cut(w_down, core * 2 * FSUB + side * FSUB, FSUB)], axis=0
        )
        t_got, z1, z2, z3 = tie(
            over("shard", to_give(tokens), 1),
            *[over("shard", own_piece, k) for k in (2, 4, 6)],
        )
        near, cont = own_parts(tokens, t_got)
        left, right = run_whole(
            split_cols_kernel, [(4, SUB, LEFT), (4, SUB, WIDE - LEFT)], where, own_piece, z1, z2, z3
        )
        own_mlp, near, left, right = tie(own_mlp, near, left, right)
        m1, m3, left_y, right_x, g_got = tie(
            over("shard", own_mlp, 2),
            over("shard", own_mlp, 6),
            over("shard", left, 1),
            over("rep", right, 2),
            over("shard", to_give(d_out), 1),
        )
        left, right = run_whole(
            join_kernel, [(8, SUB, LEFT), (8, SUB, WIDE - LEFT)], where, left, left_y, right, right_x
        )
        m3, near, left, right = tie(m3, near, left, right)
        m2, near3, left_x, right_y, left_core, right_core = tie(
            over("shard", m3, 2),
            over("shard", near, 6),
            over("rep", left, 2),
            over("shard", right, 1),
            over("rep", left, 1),
            over("rep", right, 1),
        )
        up, down = run_whole(
            split_rows_kernel, [(4, 2 * SUB, D), (4, FSUB, D)], where, own_mlp, m1, m2, m3
        )
        near, near3, left_x, right_y, up, down = tie(near, near3, left_x, right_y, up, down)
        near1, near2, up_y, down_x, left_far, right_far = tie(
            over("shard", near, 2),
            over("shard", near3, 2),
            over("shard", up, 1),
            over("rep", down, 2),
            over("rep", left_x, 1),
            over("rep", right_y, 1),
        )
        pieces = (left, left_x, left_core, left_far, right, right_y, right_core, right_far)
        up, up_y, down, down_x, pieces = tie(up, up_y, down, down_x, pieces)
        mlp_pieces = (
            up, over("rep", up, 2), up_y, over("rep", up_y, 2),
            down, down_x, over("shard", down, 1), over("shard", down_x, 1),
        )
    else:
        gathered = [
            lax.all_gather(w, "shard", axis=0, tiled=True)
            for w in (w_qkv, w_out, gain_attn, gain_mlp, w_up, w_down)
        ]
        natural = jnp.stack(halves(*gathered[:4])).reshape(2, 4, 2, 2, SUB, WIDE)
        pieces = []
        for dc in (0, 1):
            by_core = pick(natural, core ^ dc)
            for dx in (0, 1):
                both = pick_of(by_core[..., :LEFT], side ^ dx, 2)
                pieces.append(jnp.concatenate([both[:, 0], both[:, 1]], axis=0))
        for dc in (0, 1):
            by_core = pick(natural, core ^ dc)[..., LEFT:]
            for dy in (0, 1):
                both = [pick_of(by_core[:, dy], side ^ dx, 1) for dx in (0, 1)]
                pieces.append(jnp.concatenate(both, axis=0))
        pieces = tuple(pieces)
        up = half_up(gathered[4]).reshape(4, 2, 2, SUB, 2, D).transpose(1, 0, 2, 4, 3, 5)
        up = up.reshape(2, 4, 2, 2 * SUB, D)
        down = pick_of(gathered[5].reshape(4, 2, 2, 2, FSUB, D), core, 2).transpose(1, 0, 2, 3, 4)
        mlp_pieces = tuple(
            pick_of(both[dy], side ^ dx, 1) for both in (up, down) for dy in (0, 1) for dx in (0, 1)
        )
        near, cont = own_parts(tokens, over("shard", to_give(tokens), 1))
        near1, near2, near3 = [over("shard", near, k) for k in (2, 4, 6)]
        g_got = over("shard", to_give(d_out), 1)
    parts = (near, near1, near2, near3, cont)
    g_own = jnp.concatenate(own_parts(d_out, g_got), axis=0)
    parts, g_own = tie(parts, g_own)

    g_core = over("rep", g_own, 1)
    forward = attn_fwd(where, parts, pieces)
    forward, mlp_pieces, g_core = tie(forward, mlp_pieces, g_core)
    w_all, q, k, v, e, ec, attended, inv_sum, middle, nm, normed = forward

    nm_core, nm = tie(over("rep", nm, 1), nm)
    e_own, y_own, e_give, y_give, *mlp_grads = mlp(
        where, (nm, nm_core), (g_own, g_core), mlp_pieces
    )
    e_got, y_give, mlp_grads = tie(over("rep", e_give, 1), y_give, mlp_grads)
    up_keep, up_give, down_keep, down_give = mlp_grads
    y_got = over("rep", y_give, 1)
    if staged:
        up_got, down_got = over("rep", up_give, 2), over("shard", down_give, 1)
    d_mid, d_att, d_right = branch(middle, g_own, e_own, e_got, attended, w_all)

    saved = (q, k, v, e, ec, attended, inv_sum)
    kv2, f2_give, dq = attn_bwd((2,), saved, d_att, w_all)
    y_got, dq = tie(y_got, dq)
    block_rows = (middle + y_own.astype(F32) + y_got.astype(F32)).astype(BF)
    block_give = to_return(block_rows)
    f2_give, dq, block_give = tie(f2_give, dq, block_give)
    f2_got = over("shard", f2_give, 2)
    kv3, kv1, f3_give, f1_give, dq = attn_bwd((3, 1), saved, d_att, w_all, dq)
    f2_got, f3_give, f1_give, dq, block_give = tie(f2_got, f3_give, f1_give, dq, block_give)
    f3_send = total_of(f3_give, f2_got)
    if staged:
        up_got, down_got, dq = tie(up_got, down_got, dq)
        by_pair = (4, 2, 2 * SUB, D)
        folded = run_whole(
            fold_two_kernel, [(4, 2 * SUB, D)] * 4, where,
            up_keep.reshape(by_pair), up_got.reshape(by_pair), down_keep, down_got,
        )
        (up_keep, up_give, down_keep, down_give), dq, f3_send, f1_give, block_give = tie(
            folded, dq, f3_send, f1_give, block_give
        )
        up_got, down_got = over("shard", up_give, 1), over("rep", down_give, 2)
    f1, f3, b_got = over("shard", f1_give, 2), over("shard", f3_send, 6), over("shard", block_give, 1)
    keep, give, f0, f_cont = attn_bwd(
        (0,), saved, d_att, w_all, dq,
        (where, parts, normed, (kv1, kv2, kv3), (f1_give, f2_give, f3_give), d_right),
    )
    f1, f3, b_got, keep, give, f0, f_cont = tie(f1, f3, b_got, keep, give, f0, f_cont)
    if staged:
        up_got, down_got, give = tie(up_got, down_got, give)
        mlp_total, *mlp_gives = run_whole(
            fold_rows_kernel, [(4 * SUB, D)] * 4, where, up_keep, up_got, down_keep, down_got
        )
        chip_got, m2, mlp_gives = tie(
            over("rep", give, 1), over("shard", mlp_gives[1], 2), mlp_gives
        )
        m1_send, m3_send = mlp_gives[0], total_of(mlp_gives[2], m2)
        left, right = (4, 2, SUB, LEFT), (4, 2, SUB, WIDE - LEFT)
        left_keep, left_give, right_keep, right_give = run_whole(
            fold_core_kernel, [left, left, right, right], where, keep, chip_got
        )
        left_give, right_give, m1_send, m3_send, f0 = tie(
            left_give, right_give, m1_send, m3_send, f0
        )
        left_got, right_got, m1, m3, token_keep, token_give = tie(
            over("rep", left_give, 2),
            over("shard", right_give, 1),
            over("shard", m1_send, 2),
            over("shard", m3_send, 6),
            *tail(near, cont, (f0, f1, f3), f_cont, d_mid, w_all),
        )
        mlp_total = total_of(mlp_total, m1, m3)
        left_keep, left_give, right_keep, right_give = run_whole(
            fold_two_kernel,
            [(4, SUB, LEFT)] * 2 + [(4, SUB, WIDE - LEFT)] * 2,
            where, left_keep, left_got, right_keep, right_got,
        )
        left_got, right_got, m_got, mlp_total = tie(
            over("shard", left_give, 1),
            over("rep", right_give, 2),
            over("rep", mlp_total, 2),
            mlp_total,
        )
        total, *gives = run_whole(
            fold_cols_kernel, [(SUB, WIDE)] * 4, where, left_keep, left_got, right_keep, right_got
        )
        by_side = jnp.stack([mlp_total, m_got])
        gives, by_side = tie(gives, by_side)
        z1, z2, z3, m_got, by_side, t_got = tie(
            *[over("shard", gives[step - 1], 2 * step) for step in (1, 2, 3)],
            over("rep", by_side, 1),
            by_side,
            over("shard", token_give, 1),
        )
        total = total_of(total, z1, z2, z3)
        other, core_got, d_wup, d_wdown = tie(
            over("rep", total, 2),
            over("rep", total, 1),
            *run_whole(
                unpack_kernel, [(2 * SUB, FF), (4 * FSUB, D)], where, by_side, m_got, dtype=F32
            ),
        )
        far = over("rep", other, 1)
        d_wqkv, d_wout, d_gain_attn, d_gain_mlp = run_whole(
            finish_kernel, [(2 * SUB, 3 * D), (2 * SUB, D), (1, 2 * SUB), (1, 2 * SUB)],
            where, total, other, core_got, far, dtype=F32,
        )
        d_gain_attn, d_gain_mlp = d_gain_attn.reshape(2 * SUB), d_gain_mlp.reshape(2 * SUB)
    else:
        token_keep, token_give = tail(near, cont, (f0, f1, f3), f_cont, d_mid, w_all)
        t_got = over("shard", token_give, 1)
        low, high = jnp.where(core == 0, keep, give), jnp.where(core == 0, give, keep)

        def by_side_of(keep, give, at):
            first = at == 0
            return jnp.stack([jnp.where(first, keep, give), jnp.where(first, give, keep)])

        up = by_side_of(up_keep, up_give, side).reshape(2, 8, 2, SUB, D)
        up = up.transpose(1, 0, 3, 2, 4).reshape(D, 8, 1, 2 * FSUB)
        down = by_side_of(down_keep, down_give, y_at).transpose(1, 0, 2, 3, 4)
        down = down.reshape(8, 1, 2 * FSUB, D)
        peer_up, peer_down = over("rep", up, 1), over("rep", down, 1)
        first = core == 0
        up, peer_up = jnp.where(first, up, peer_up), jnp.where(first, peer_up, up)
        down, peer_down = jnp.where(first, down, peer_down), jnp.where(first, peer_down, down)
        up = jnp.concatenate([up, peer_up], axis=2).reshape(D, FF)
        down = jnp.concatenate([down, peer_down], axis=1).reshape(FF, D)
        rest = lambda v: (v.astype(F32) + over("rep", v, 2).astype(F32)).astype(BF)
        up, down = rest(up), rest(down)
        scatter = lambda v: lax.psum_scatter(v, "shard", scatter_dimension=0, tiled=True)
        d_wup, d_wdown = scatter(up).astype(F32), scatter(down).astype(F32)
        low = lax.psum(scatter(low), "rep").astype(F32)
        high = lax.psum(scatter(high), "rep").astype(F32)
        d_wqkv = jnp.concatenate([low[:, :HALF], high[:, :D]], axis=1)
        d_wout, d_gain_attn, d_gain_mlp = high[:, D:HALF], low[:, HALF], high[:, HALF]

    return (
        home_rows(block_rows[:PR], block_rows[2 * PR : 3 * PR], b_got),
        home_rows(token_keep[:PR], token_keep[PR:], t_got),
        d_wqkv,
        d_wout,
        d_wup,
        d_wdown,
        d_gain_attn,
        d_gain_mlp,
    )


def solution(mesh):
    weights = P("shard", None)
    rows = P(("rep", "shard"), None)
    return jax.shard_map(
        per_device,
        mesh=mesh,
        in_specs=(rows, weights, weights, weights, weights, P("shard"), P("shard"), rows),
        out_specs=(rows, rows, weights, weights, weights, weights, P("shard"), P("shard")),
        check_vma=False,
    )
```

```python
import jax
import jax.numpy as jnp
from jax import lax
from jax.experimental import pallas as pl
from jax.experimental.pallas import tpu as pltpu
from jax.sharding import PartitionSpec as P

D = 768
HEADS = 12
HDIM = 64
FF = 3072
PR = 128
PLEN = 1024
KEYS = PLEN + 2 * PR
ROWS = 4 * PR
PAIRS = HEADS // 2
WIDTH = 2 * HDIM
HALF = 1536
WIDE = HALF + 128
SUB = 48
LEFT = 896
RIGHT = D + 128
UNIT = 2 * PR
FSUB = 96
FH = FF // 2
norm_eps = 1e-05
neg_fill = -1e30
SCALE = HDIM ** (-0.5)
GELU_C = 0.7978845608028654
GELU_A = 0.044715
BF = jnp.bfloat16
F32 = jnp.float32
VMEM_LIMIT = 60 * 1024 * 1024
BLOCKS = (0, 1, 2, 3, 4, 5, 6, 7)
ORDER = (0, 2, 4, 6, 1, 3, 5, 7)


def dot_nt(a, b):
    return lax.dot_general(a, b, (((1,), (1,)), ((), ())), preferred_element_type=F32)


def dot_tn(a, b):
    return lax.dot_general(a, b, (((0,), (0,)), ((), ())), preferred_element_type=F32)


def dot_nn(a, b):
    return jnp.dot(a, b, preferred_element_type=F32)


def rms_inv(values):
    return lax.rsqrt(jnp.mean(values * values, axis=-1, keepdims=True) + norm_eps)


def params():
    return pltpu.CompilerParams(vmem_limit_bytes=VMEM_LIMIT)


def shape(dims, dtype):
    return jax.ShapeDtypeStruct(dims, dtype)


def fill_normed(x_ref, gain, normed_ref):
    @pl.loop(0, KEYS, step=PR)
    def _(row):
        rows = pl.ds(pl.multiple_of(row, PR), PR)
        part = x_ref[rows, :].astype(F32)
        normed_ref[rows, :] = (part * rms_inv(part) * gain).astype(BF)


def lane_half(head):
    lanes = lax.broadcasted_iota(jnp.int32, (1, WIDTH), 1)
    return (lanes >= HDIM) if head else (lanes < HDIM)


def sum_column(values):
    return jnp.broadcast_to(jnp.sum(values, axis=0, keepdims=True), (128, values.shape[1])).T


def gain_row(column):
    return column.astype(F32).T[0:1, :]


def attn_fwd_kernel(
    where_ref, x0_ref, x1_ref, x2_ref, x3_ref, xc_ref,
    l00_ref, l10_ref, l01_ref, l11_ref, r00_ref, r10_ref, r01_ref, r11_ref,
    w_out_ref, q_ref, k_ref, v_ref, e_ref, ec_ref, o_ref, r_ref, mid_ref, nm_ref, normed_out_ref,
    w_ref, x_ref, normed_ref, bias_ref, att_ref, qs_ref, s_ref, inv_ref, out_ref, sems, out_sems,
):
    step = pl.program_id(0)
    late = [
        pltpu.make_async_copy(w_ref, w_out_ref, out_sems.at[0]),
        pltpu.make_async_copy(normed_ref, normed_out_ref, out_sems.at[1]),
    ]

    @pl.when(step == 0)
    def _():
        side, core = where_ref[1], where_ref[2]
        copies = []
        for at, (dx, dc, piece) in enumerate(
            ((0, 0, l00_ref), (1, 0, l10_ref), (0, 1, l01_ref), (1, 1, l11_ref))
        ):
            for i in range(8):
                start = where_ref[8 + i] * (2 * SUB) + jnp.bitwise_xor(side, dx) * SUB
                copies.append(
                    pltpu.make_async_copy(
                        piece.at[i],
                        w_ref.at[
                            jnp.bitwise_xor(core, dc),
                            pl.ds(pl.multiple_of(start, 16), SUB),
                            pl.ds(0, LEFT),
                        ],
                        sems.at[at * 8 + i],
                    )
                )
        for at, (far, dc, piece) in enumerate(
            ((0, 0, r00_ref), (1, 0, r10_ref), (0, 1, r01_ref), (1, 1, r11_ref))
        ):
            for i in range(8):
                start = where_ref[8 + far * 4 + i % 4] * (2 * SUB)
                start = start + jnp.bitwise_xor(side, i // 4) * SUB
                copies.append(
                    pltpu.make_async_copy(
                        piece.at[i],
                        w_ref.at[
                            jnp.bitwise_xor(core, dc),
                            pl.ds(pl.multiple_of(start, 16), SUB),
                            pl.ds(LEFT, WIDE - LEFT),
                        ],
                        sems.at[32 + at * 8 + i],
                    )
                )
        for at, part in enumerate((x0_ref, x1_ref, x2_ref, x3_ref, xc_ref)):
            copies.append(
                pltpu.make_async_copy(part, x_ref.at[pl.ds(at * UNIT, UNIT), :], sems.at[64 + at])
            )
        for copy in copies:
            copy.start()
        pos = where_ref[0]
        row = lax.broadcasted_iota(jnp.int32, (PR, PR), 0)
        col = lax.broadcasted_iota(jnp.int32, (PR, PR), 1)
        tri = jnp.where(col <= row, 0.0, neg_fill)
        for part in range(2):
            mine = jnp.bitwise_xor(pos, BLOCKS[part])
            for block in range(8):
                at = (pl.ds(part * PR, PR), pl.ds(block * PR, PR))
                if block == part:
                    bias_ref[at] = tri
                else:
                    seen = jnp.bitwise_xor(pos, BLOCKS[block]) < mine
                    bias_ref[at] = jnp.full((PR, PR), jnp.where(seen, 0.0, neg_fill), F32)
        for copy in copies:
            copy.wait()
        late[0].start()
        fill_normed(x_ref, gain_row(w_ref[0, :, HALF:]), normed_ref)
        late[1].start()

    at = pl.ds(pl.multiple_of(step * UNIT, UNIT), UNIT)
    at_k = pl.ds(pl.multiple_of(D + step * UNIT, UNIT), UNIT)
    k_ref[...] = dot_nn(normed_ref[...], w_ref[0, :, at_k]).astype(BF)
    v_ref[...] = dot_nn(normed_ref[...], w_ref[1, :, at]).astype(BF)
    wq = w_ref[0, :, at]
    q_ref[0:UNIT, :] = (dot_nn(normed_ref[0:UNIT, :], wq) * SCALE).astype(BF)
    q_ref[UNIT:, :] = (dot_nn(normed_ref[PLEN:, :], wq) * SCALE).astype(BF)
    row = lax.broadcasted_iota(jnp.int32, (PR, PR), 0)
    col = lax.broadcasted_iota(jnp.int32, (PR, PR), 1)
    tri = jnp.where(col <= row, 0.0, neg_fill)
    low_half = lane_half(0)
    for pair in range(2):
        lanes = slice(pair * WIDTH, (pair + 1) * WIDTH)
        query = q_ref[:, lanes]
        for head in range(2):
            rows = slice(head * ROWS, (head + 1) * ROWS)
            qs_ref[rows, :] = jnp.where(lane_half(head), query, jnp.zeros_like(query))
        s_ref[...] = dot_nt(qs_ref[...], k_ref[0:PLEN, lanes])
        for head in range(2):
            for chunk in range(4):
                mine = slice(chunk * PR, (chunk + 1) * PR)
                rows = slice(head * ROWS + chunk * PR, head * ROWS + (chunk + 1) * PR)
                scores = s_ref[rows, :]
                if chunk < 2:
                    scores = scores + bias_ref[mine, :]
                    top = jnp.max(scores, axis=-1, keepdims=True)
                    terms = jnp.exp(scores - top)
                    total = jnp.sum(terms, axis=-1, keepdims=True)
                else:
                    own = slice(PLEN + (chunk - 2) * PR, PLEN + (chunk - 1) * PR)
                    near = dot_nt(qs_ref[rows, :], k_ref[own, lanes]) + tri
                    top = jnp.maximum(
                        jnp.max(scores, axis=-1, keepdims=True),
                        jnp.max(near, axis=-1, keepdims=True),
                    )
                    terms = jnp.exp(scores - top)
                    near_terms = jnp.exp(near - top)
                    total = jnp.sum(terms, axis=-1, keepdims=True) + jnp.sum(
                        near_terms, axis=-1, keepdims=True
                    )
                    ec_ref[2 * pair + head, (chunk - 2) * PR : (chunk - 1) * PR, :] = (
                        near_terms.astype(BF)
                    )
                e_ref[2 * pair + head, mine, :] = terms.astype(BF)
                inv_ref[rows, :] = jnp.broadcast_to(1.0 / total, (PR, WIDTH))
        terms = e_ref[2 * pair : 2 * pair + 2].reshape(2 * ROWS, PLEN)
        out_ref[...] = dot_nn(terms, v_ref[0:PLEN, lanes])
        for head in range(2):
            for side in range(2):
                own = slice(PLEN + side * PR, PLEN + (side + 1) * PR)
                start = head * ROWS + (2 + side) * PR
                near = ec_ref[2 * pair + head, side * PR : (side + 1) * PR, :]
                out_ref[start : start + PR, :] += dot_nn(near, v_ref[own, lanes])
        inv = jnp.where(low_half, inv_ref[0:ROWS, :], inv_ref[ROWS:, :])
        r_ref[:, lanes] = inv
        o_ref[:, lanes] = (
            jnp.where(low_half, out_ref[0:ROWS, :], out_ref[ROWS:, :]) * inv
        ).astype(BF)
    att_ref[step] = o_ref[...]

    @pl.when(step == pl.num_programs(0) - 1)
    def _():
        wout = w_ref[1, :, D:HALF]
        gain = gain_row(w_ref[1, :, HALF:])
        for chunk in range(4):
            rows = slice(chunk * PR, (chunk + 1) * PR)
            from_row = chunk * PR if chunk < 2 else PLEN + (chunk - 2) * PR
            middle = x_ref[from_row : from_row + PR, :].astype(F32)
            for i in range(3):
                middle = middle + dot_nn(att_ref[i, rows, :], wout[i * UNIT : (i + 1) * UNIT, :])
            mid_ref[rows, :] = middle
            nm_ref[rows, :] = (middle * rms_inv(middle) * gain).astype(BF)
        for copy in late:
            copy.wait()


def attn_fwd(where, parts, pieces):
    pair = lambda i: (0, i)
    whole = lambda i: (0, 0)
    heads = lambda i: (i, 0, 0)
    anywhere = pl.BlockSpec(memory_space=pl.ANY)
    return pl.pallas_call(
        attn_fwd_kernel,
        grid=(3,),
        in_specs=[
            pl.BlockSpec(memory_space=pltpu.SMEM),
            *[anywhere] * 13,
        ],
        out_specs=[
            anywhere,
            pl.BlockSpec((ROWS, UNIT), pair),
            pl.BlockSpec((KEYS, UNIT), pair),
            pl.BlockSpec((KEYS, UNIT), pair),
            pl.BlockSpec((4, ROWS, PLEN), heads),
            pl.BlockSpec((4, UNIT, PR), heads),
            pl.BlockSpec((ROWS, UNIT), pair),
            pl.BlockSpec((ROWS, UNIT), pair),
            pl.BlockSpec((ROWS, D), whole),
            pl.BlockSpec((ROWS, D), whole),
            anywhere,
        ],
        out_shape=[
            shape((2, D, WIDE), BF),
            shape((ROWS, D), BF),
            shape((KEYS, D), BF),
            shape((KEYS, D), BF),
            shape((HEADS, ROWS, PLEN), BF),
            shape((HEADS, 2 * PR, PR), BF),
            shape((ROWS, D), BF),
            shape((ROWS, D), F32),
            shape((ROWS, D), F32),
            shape((ROWS, D), BF),
            shape((KEYS, D), BF),
        ],
        scratch_shapes=[
            pltpu.VMEM((2, D, WIDE), BF),
            pltpu.VMEM((KEYS, D), BF),
            pltpu.VMEM((KEYS, D), BF),
            pltpu.VMEM((2 * PR, PLEN), F32),
            pltpu.VMEM((3, ROWS, UNIT), BF),
            pltpu.VMEM((2 * ROWS, WIDTH), BF),
            pltpu.VMEM((2 * ROWS, PLEN), F32),
            pltpu.VMEM((2 * ROWS, WIDTH), F32),
            pltpu.VMEM((2 * ROWS, WIDTH), F32),
            pltpu.SemaphoreType.DMA((69,)),
            pltpu.SemaphoreType.DMA((2,)),
        ],
        compiler_params=params(),
        cost_estimate=pl.CostEstimate(
            flops=30_000_000_000, bytes_accessed=30_000_000, transcendentals=6_300_000
        ),
    )(where, *parts, *pieces)


def mlp_kernel(
    where_ref, nm0_ref, nm1_ref, g0_ref, g1_ref,
    up00_ref, up10_ref, up01_ref, up11_ref, down00_ref, down10_ref, down01_ref, down11_ref,
    e_ref, y_ref, give_e_ref, give_y_ref, up_keep_ref, up_give_ref, down_keep_ref, down_give_ref,
    wup_ref, wdown_ref, nm_ref, g_ref, acc_e_ref, acc_y_ref, part_ref, active_ref, d_hidden_ref, sems,
):
    step = pl.program_id(0)
    side, y_at = where_ref[1], where_ref[0] % 2

    @pl.when(step == 0)
    def _():
        copies = []
        for dy, ups, downs in (
            (0, (up00_ref, up10_ref), (down00_ref, down10_ref)),
            (1, (up01_ref, up11_ref), (down01_ref, down11_ref)),
        ):
            for dx in range(2):
                for i in range(4):
                    block = where_ref[8 + dy * 4 + i] * 2 + jnp.bitwise_xor(side, dx)
                    rows = pl.ds(pl.multiple_of(block * SUB, 16), SUB)
                    for half in range(2):
                        copies.append(
                            pltpu.make_async_copy(
                                ups[dx].at[i, pl.ds(half * SUB, SUB), :],
                                wup_ref.at[rows, pl.ds(half * D, D)],
                                sems.at[len(copies)],
                            )
                        )
                    copies.append(
                        pltpu.make_async_copy(
                            downs[dx].at[i],
                            wdown_ref.at[pl.ds(pl.multiple_of(block * FSUB, 16), FSUB), :],
                            sems.at[len(copies)],
                        )
                    )
        for copy in copies:
            copy.start()
        nm_ref[0:ROWS, :] = nm0_ref[...]
        nm_ref[ROWS:, :] = nm1_ref[...]
        g_ref[0:ROWS, :] = g0_ref[...]
        g_ref[ROWS:, :] = g1_ref[...]
        for copy in copies:
            copy.wait()

    at = pl.ds(pl.multiple_of(step * D, D), D)
    for start in range(0, 2 * ROWS, 256):
        rows = slice(start, start + 256)
        hidden = dot_nn(nm_ref[rows, :], wup_ref[:, at])
        square = hidden * hidden
        th = jnp.tanh(hidden * (GELU_C + GELU_C * GELU_A * square))
        left = 0.5 + 0.5 * th
        active_ref[rows, :] = (hidden * left).astype(BF)
        slope = left + hidden * (0.5 - 0.5 * th * th) * (GELU_C + 3.0 * GELU_A * GELU_C * square)
        d_hidden_ref[rows, :] = (dot_nt(g_ref[rows, :], wdown_ref[at, :]) * slope).astype(BF)
    part_y = dot_nn(active_ref[...], wdown_ref[at, :])
    part_e = dot_nt(d_hidden_ref[...], wup_ref[:, at])

    @pl.when(step == 0)
    def _():
        acc_y_ref[...] = part_y
        acc_e_ref[...] = part_e

    @pl.when(step == 1)
    def _():
        e_ref[...] = (acc_e_ref[0:ROWS, :] + part_e[0:ROWS]).astype(BF)
        y_ref[...] = (acc_y_ref[0:ROWS, :] + part_y[0:ROWS]).astype(BF)
        give_e_ref[...] = (acc_e_ref[ROWS:, :] + part_e[ROWS:]).astype(BF)
        give_y_ref[...] = (acc_y_ref[ROWS:, :] + part_y[ROWS:]).astype(BF)

    part_ref[...] = dot_tn(nm_ref[...], d_hidden_ref[...]).astype(BF).reshape(16, SUB, D)
    at_half = pl.ds(pl.multiple_of(step * SUB, 16), SUB)
    for s in range(8):
        up_keep_ref[s, at_half, :] = part_ref[2 * s + side]
        up_give_ref[s, at_half, :] = part_ref[2 * s + 1 - side]
    part_ref[...] = dot_tn(active_ref[...], g_ref[...]).astype(BF).reshape(16, SUB, D)
    for z in range(2):
        for x in range(2):
            for h in range(2):
                at_h = pl.ds(h * SUB, SUB)
                row = 8 * z + 2 * x + h
                down_keep_ref[z, x, at_h, :] = part_ref[row + 4 * y_at]
                down_give_ref[z, x, at_h, :] = part_ref[row + 4 - 4 * y_at]


def mlp(where, normed, grads, pieces):
    whole = pl.BlockSpec((ROWS, D), lambda i: (0, 0))
    anywhere = pl.BlockSpec(memory_space=pl.ANY)
    return pl.pallas_call(
        mlp_kernel,
        grid=(2,),
        in_specs=[pl.BlockSpec(memory_space=pltpu.SMEM)] + [whole] * 4 + [anywhere] * 8,
        out_specs=[whole] * 4
        + [pl.BlockSpec((8, 2 * SUB, D), lambda i: (0, 0, 0))] * 2
        + [pl.BlockSpec((2, 2, FSUB, D), lambda i: (i, 0, 0, 0))] * 2,
        out_shape=[shape((ROWS, D), BF)] * 4
        + [shape((8, 2 * SUB, D), BF)] * 2
        + [shape((4, 2, FSUB, D), BF)] * 2,
        scratch_shapes=[
            pltpu.VMEM((D, FH), BF),
            pltpu.VMEM((FH, D), BF),
            pltpu.VMEM((2 * ROWS, D), BF),
            pltpu.VMEM((2 * ROWS, D), BF),
            pltpu.VMEM((2 * ROWS, D), F32),
            pltpu.VMEM((2 * ROWS, D), F32),
            pltpu.VMEM((16, SUB, D), BF),
            pltpu.VMEM((2 * ROWS, D), BF),
            pltpu.VMEM((2 * ROWS, D), BF),
            pltpu.SemaphoreType.DMA((48,)),
        ],
        compiler_params=params(),
        cost_estimate=pl.CostEstimate(
            flops=20_000_000_000, bytes_accessed=20_000_000, transcendentals=1_600_000
        ),
    )(where, *normed, *grads, *pieces)


def branch_kernel(
    mid_ref, g_ref, e0_ref, e1_ref, att_ref, w_ref, gcol_ref, dmid_ref, datt_ref, right_ref,
    low_ref,
):
    gain = gain_row(gcol_ref[0])
    wout = w_ref[0]
    gain_sum = jnp.zeros((1, D), F32)
    for chunk in range(4):
        rows = slice(chunk * PR, (chunk + 1) * PR)
        middle = mid_ref[rows, :]
        inv = rms_inv(middle)
        unit = middle * inv
        grad = e0_ref[rows, :].astype(F32) + e1_ref[rows, :].astype(F32)
        scaled = gain * grad
        mean = jnp.mean(unit * scaled, axis=-1, keepdims=True)
        d_mid = g_ref[rows, :].astype(F32) + inv * (scaled - unit * mean)
        dmid_ref[rows, :] = d_mid
        gain_sum = gain_sum + jnp.sum(grad * unit, axis=0, keepdims=True)
        branch = d_mid.astype(BF)
        low_ref[rows, :] = branch
        datt_ref[rows, :] = dot_nt(branch, wout).astype(BF)
    right_ref[:, D:] = sum_column(gain_sum).astype(BF)
    right_ref[:, 0:D] = dot_tn(att_ref[...], low_ref[...]).astype(BF)


def branch(middle, d_out, own, given, attended, w_all):
    return pl.pallas_call(
        branch_kernel,
        grid=(1,),
        in_specs=[pl.BlockSpec((ROWS, D), lambda i: (0, 0))] * 5
        + [
            pl.BlockSpec((1, D, D), lambda i: (1, 0, 1)),
            pl.BlockSpec((1, D, 128), lambda i: (1, 0, HALF // 128)),
        ],
        out_specs=[
            pl.BlockSpec((ROWS, D), lambda i: (0, 0)),
            pl.BlockSpec((ROWS, D), lambda i: (0, 0)),
            pl.BlockSpec((D, RIGHT), lambda i: (0, 0)),
        ],
        out_shape=[shape((ROWS, D), F32), shape((ROWS, D), BF), shape((D, RIGHT), BF)],
        scratch_shapes=[pltpu.VMEM((ROWS, D), BF)],
        compiler_params=params(),
        cost_estimate=pl.CostEstimate(
            flops=2_000_000_000, bytes_accessed=9_000_000, transcendentals=1000
        ),
    )(middle, d_out, own, given, attended, w_all, w_all)


def attn_bwd_kernel(units, *refs):
    first, last = units == (2,), units[0] == 0
    q_ref, g_ref, o_ref, r_ref, *refs = refs
    keyed = []
    for _ in units:
        keyed.append(refs[:3])
        refs = refs[3:]
    if last:
        ec_ref, kc_ref, vc_ref, *refs = refs
    if not first:
        dq_in_ref, *refs = refs
    wk_ref, wv_ref, *refs = refs
    if last:
        where_ref, wq_ref, normed_ref, gcol_ref, kv1_ref, kv2_ref, kv3_ref, *refs = refs
        right_ref, keep_ref, give_ref, dkv_own_ref, dq_own_ref, *refs = refs
        late_in = (wq_ref, wk_ref, wv_ref, normed_ref, right_ref)
        *late, sems_late = refs[:6]
        refs = refs[6:]
        wq_ref, wk_ref, wv_ref, normed_ref, right_ref = late
        dkv_ref, dq_ref, low_ref, high_ref, sems, *refs = refs
    else:
        dkv_refs, refs = refs[: len(units)], refs[len(units) :]
        f_refs, refs = refs[: len(units)], refs[len(units) :]
        dq_ref, *refs = refs
    qs_ref, gs_ref, ds_ref, *refs = refs
    if last:
        sum_ref, near_ref, near_e_ref, near_qs_ref, near_gs_ref = refs
    step = pl.program_id(0)

    def late_copies():
        sources = (
            late_in[0].at[pl.ds(0, 1), :, pl.ds(0, D)],
            late_in[1].at[pl.ds(0, 1), :, pl.ds(D, D)],
            late_in[2].at[pl.ds(1, 1), :, pl.ds(0, D)],
            *late_in[3:],
        )
        return [
            pltpu.make_async_copy(source, target, sems_late.at[at])
            for at, (source, target) in enumerate(zip(sources, late))
        ]

    if last:

        @pl.when(step == 0)
        def _():
            for at, ref in enumerate((kv1_ref, kv2_ref, kv3_ref)):
                rows = pl.ds((at + 1) * UNIT, UNIT)
                pltpu.make_async_copy(ref, dkv_ref.at[:, rows, :], sems.at[at]).start()
            for copy in late_copies():
                copy.start()

    low_half = lane_half(0)
    for pair in range(2):
        lanes = slice(pair * WIDTH, (pair + 1) * WIDTH)
        lanes_v = slice((2 + pair) * WIDTH, (3 + pair) * WIDTH)
        scaled_grad = g_ref[:, lanes].astype(F32) * r_ref[:, lanes]
        prod = scaled_grad * o_ref[:, lanes].astype(F32)
        low_grad = scaled_grad.astype(BF)
        query = q_ref[:, lanes]
        deltas = []
        for head in range(2):
            half = lane_half(head)
            rows = slice(head * ROWS, (head + 1) * ROWS)
            deltas.append(jnp.sum(jnp.where(half, prod, 0.0), axis=-1, keepdims=True))
            gs_ref[rows, :] = jnp.where(half, low_grad, jnp.zeros_like(low_grad))
            qs_ref[rows, :] = jnp.where(half, query, jnp.zeros_like(query))
        delta = jnp.concatenate(deltas, axis=0)
        d_query = None
        for u, (e_ref, k_ref, v_ref) in enumerate(keyed):
            out_ref = dkv_ref if last else dkv_refs[u]
            terms = e_ref[2 * pair : 2 * pair + 2].reshape(2 * ROWS, UNIT)
            d_soft = dot_nt(gs_ref[...], v_ref[:, lanes])
            ds_ref[...] = terms * (d_soft - delta).astype(BF)
            more = dot_nn(ds_ref[...], k_ref[:, lanes])
            d_query = more if d_query is None else d_query + more
            out_ref[step, 0:UNIT, lanes] = dot_tn(ds_ref[...], qs_ref[...]).astype(BF)
            out_ref[step, 0:UNIT, lanes_v] = dot_tn(terms, gs_ref[...]).astype(BF)
        total = jnp.where(low_half, d_query[0:ROWS], d_query[ROWS:])
        if not first:
            total = total + dq_in_ref[:, lanes]
        if not last:
            dq_ref[:, lanes] = total
            continue
        sum_ref[...] = total
        for side in range(2):
            own = slice(side * PR, (side + 1) * PR)
            mine = slice((2 + side) * PR, (3 + side) * PR)
            near_q = []
            for head in range(2):
                rows = slice(head * ROWS + mine.start, head * ROWS + mine.stop)
                at = slice(head * PR, (head + 1) * PR)
                near = ec_ref[2 * pair + head, own, :]
                d_soft = dot_nt(gs_ref[rows, :], vc_ref[own, lanes])
                near_ref[at, :] = near * (d_soft - deltas[head][mine]).astype(BF)
                near_e_ref[at, :] = near
                near_qs_ref[at, :] = qs_ref[rows, :]
                near_gs_ref[at, :] = gs_ref[rows, :]
                near_q.append(dot_nn(near_ref[at, :], kc_ref[own, lanes]))
            sum_ref[mine, :] += jnp.where(low_half, near_q[0], near_q[1])
            rows = slice(PLEN + side * PR, PLEN + (side + 1) * PR)
            dkv_ref[step, rows, lanes] = dot_tn(near_ref[...], near_qs_ref[...]).astype(BF)
            dkv_ref[step, rows, lanes_v] = dot_tn(near_e_ref[...], near_gs_ref[...]).astype(BF)
        dq_ref[step, :, lanes] = (sum_ref[...] * SCALE).astype(BF)

    def back_to_rows(dkv, rows):
        grad = None
        for i in range(3):
            at = slice(i * UNIT, (i + 1) * UNIT)
            more = dot_nt(dkv[i, rows, 0:UNIT], wk_ref[0, :, at])
            more = more + dot_nt(dkv[i, rows, UNIT:], wv_ref[0, :, at])
            grad = more if grad is None else grad + more
        return grad

    @pl.when(step == pl.num_programs(0) - 1)
    def _():
        if not last:
            for dkv, f_ref in zip(dkv_refs, f_refs):
                f_ref[...] = back_to_rows(dkv, slice(0, UNIT)).astype(BF)
            return
        for at, ref in enumerate((kv1_ref, kv2_ref, kv3_ref)):
            rows = pl.ds((at + 1) * UNIT, UNIT)
            pltpu.make_async_copy(ref, dkv_ref.at[:, rows, :], sems.at[at]).wait()
        for copy in late_copies():
            copy.wait()
        high_ref[:, D:] = right_ref[...]
        own = [
            pltpu.make_async_copy(
                dkv_ref.at[:, pl.ds(start, UNIT), :],
                dkv_own_ref.at[:, pl.ds(at * UNIT, UNIT), :],
                sems.at[at],
            )
            for at, start in enumerate((0, PLEN))
        ]
        own.append(pltpu.make_async_copy(dq_ref, dq_own_ref, sems.at[2]))
        for copy in own:
            copy.start()
        rows_sum = jnp.zeros((D, 1), F32)
        for i in range(3):
            at = slice(i * UNIT, (i + 1) * UNIT)
            d_wq = dot_tn(normed_ref[0:UNIT, :], dq_ref[i, 0:UNIT, :]) + dot_tn(
                normed_ref[PLEN:, :], dq_ref[i, UNIT:, :]
            )
            both = dot_tn(normed_ref[...], dkv_ref[i])
            for grad, w_ref in ((d_wq, wq_ref), (both[:, 0:UNIT], wk_ref), (both[:, UNIT:], wv_ref)):
                product = grad * w_ref[0, :, at].astype(F32)
                rows_sum = rows_sum + jnp.sum(product, axis=-1, keepdims=True)
            low_ref[:, at] = d_wq.astype(BF)
            low_ref[:, D + i * UNIT : D + (i + 1) * UNIT] = both[:, 0:UNIT].astype(BF)
            high_ref[:, at] = both[:, UNIT:].astype(BF)
        low_ref[:, HALF:] = (rows_sum / gcol_ref[0].astype(F32)).astype(BF)
        for copy in own:
            copy.wait()

        for core, low_out, high_out in ((0, keep_ref, give_ref), (1, give_ref, keep_ref)):

            @pl.when(where_ref[2] == core)
            def _():
                copies = [
                    pltpu.make_async_copy(low_ref, low_out, sems.at[3]),
                    pltpu.make_async_copy(high_ref, high_out, sems.at[4]),
                ]
                for copy in copies:
                    copy.start()
                for copy in copies:
                    copy.wait()


def attn_bwd(units, saved, d_att, w_all, dq=None, rest=None):
    first, last = units == (2,), units[0] == 0
    q, k, v, e, ec, o, r = saved
    width = 2 * WIDTH
    lanes = lambda i: (0, i)
    full = lambda *dims: pl.BlockSpec(dims, lambda i: (0,) * len(dims))
    rows = pl.BlockSpec((ROWS, width), lanes)
    anywhere = pl.BlockSpec(memory_space=pl.ANY)
    weight = lambda half, at: pl.BlockSpec((1, D, D), lambda i: (half, 0, at))
    specs, args = [rows] * 4, [q, d_att, o, r]
    for u in units:
        specs += [
            pl.BlockSpec((4, ROWS, UNIT), lambda i, u=u: (i, 0, u)),
            pl.BlockSpec((UNIT, width), lambda i, u=u: (u, i)),
            pl.BlockSpec((UNIT, width), lambda i, u=u: (u, i)),
        ]
        args += [e, k, v]
    if last:
        specs += [
            pl.BlockSpec((4, UNIT, PR), lambda i: (i, 0, 0)),
            pl.BlockSpec((UNIT, width), lambda i: (4, i)),
            pl.BlockSpec((UNIT, width), lambda i: (4, i)),
        ]
        args += [ec, k, v]
    if not first:
        specs.append(rows)
        args.append(dq)
    specs += [anywhere, anywhere] if last else [weight(0, 1), weight(1, 0)]
    args += [w_all, w_all]
    kv = (3, UNIT, 2 * UNIT)
    if last:
        where, normed, kvs, right = rest
        specs += [pl.BlockSpec(memory_space=pltpu.SMEM)] + [anywhere] * 2
        specs += [pl.BlockSpec((1, D, 128), lambda i: (0, 0, HALF // 128))] + [anywhere] * 4
        args += [where, w_all, normed, w_all, *kvs, right]
        outs = [anywhere] * 4
        out_shapes = [shape((D, WIDE), BF)] * 2
        out_shapes += [shape((3, ROWS, 2 * UNIT), BF), shape((3, ROWS, UNIT), BF)]
        scratch = [
            pltpu.VMEM((1, D, D), BF),
            pltpu.VMEM((1, D, D), BF),
            pltpu.VMEM((1, D, D), BF),
            pltpu.VMEM((KEYS, D), BF),
            pltpu.VMEM((D, RIGHT), BF),
            pltpu.SemaphoreType.DMA((5,)),
            pltpu.VMEM((3, KEYS, 2 * UNIT), BF),
            pltpu.VMEM((3, ROWS, UNIT), BF),
            pltpu.VMEM((D, WIDE), BF),
            pltpu.VMEM((D, WIDE), BF),
            pltpu.SemaphoreType.DMA((5,)),
        ]
    else:
        outs = [full(*kv)] * len(units) + [full(UNIT, D)] * len(units) + [rows]
        out_shapes = [shape(kv, BF)] * len(units) + [shape((UNIT, D), BF)] * len(units)
        out_shapes.append(shape((ROWS, D), F32))
        scratch = []
    return pl.pallas_call(
        lambda *refs: attn_bwd_kernel(units, *refs),
        grid=(3,),
        in_specs=specs,
        out_specs=outs,
        out_shape=out_shapes,
        scratch_shapes=scratch
        + [
            pltpu.VMEM((2 * ROWS, WIDTH), BF),
            pltpu.VMEM((2 * ROWS, WIDTH), BF),
            pltpu.VMEM((2 * ROWS, UNIT), BF),
        ]
        + ([pltpu.VMEM((ROWS, WIDTH), F32)] + [pltpu.VMEM((UNIT, WIDTH), BF)] * 4 if last else []),
        compiler_params=params(),
        cost_estimate=pl.CostEstimate(
            flops=10_000_000_000 * (len(units) + last), bytes_accessed=10_000_000, transcendentals=1000
        ),
    )(*args)


def tail_kernel(
    near_ref, cont_ref, dkv_ref, dq_ref, wq_ref, wk_ref, wv_ref, f1_ref, f3_ref, dmid_ref, gcol_ref,
    keep_ref, give_ref,
):
    gain = gain_row(gcol_ref[0])
    for half, x_ref in enumerate((near_ref, cont_ref)):
        rows = slice(half * UNIT, (half + 1) * UNIT)
        grad = None
        for i in range(3):
            at = slice(i * UNIT, (i + 1) * UNIT)
            more = dot_nt(dkv_ref[i, rows, 0:UNIT], wk_ref[0, :, at])
            more = more + dot_nt(dkv_ref[i, rows, UNIT:], wv_ref[0, :, at])
            more = more + dot_nt(dq_ref[i, rows, :], wq_ref[0, :, at])
            grad = more if grad is None else grad + more
        if half == 0:
            grad = grad + f1_ref[...].astype(F32) + f3_ref[...].astype(F32)
        part = x_ref[...].astype(F32)
        inv = rms_inv(part)
        unit = part * inv
        scaled = gain * grad
        mean = jnp.mean(unit * scaled, axis=-1, keepdims=True)
        d_rows = dmid_ref[rows, :] + inv * (scaled - unit * mean)
        at = slice(half * PR, (half + 1) * PR)
        keep_ref[at, :] = d_rows[0:PR]
        give_ref[at, :] = d_rows[PR:].astype(BF)


def tail(near, cont, own, f_parts, d_mid, w_all):
    full = lambda *dims: pl.BlockSpec(dims, lambda i: (0,) * len(dims))
    weight = lambda half, at: pl.BlockSpec((1, D, D), lambda i: (half, 0, at))
    half = full(UNIT, D)
    return pl.pallas_call(
        tail_kernel,
        grid=(1,),
        in_specs=[half, half, full(3, ROWS, 2 * UNIT), full(3, ROWS, UNIT)]
        + [weight(0, 0), weight(0, 1), weight(1, 0), half, half, full(ROWS, D)]
        + [pl.BlockSpec((1, D, 128), lambda i: (0, 0, HALF // 128))],
        out_specs=[half, half],
        out_shape=[shape((UNIT, D), F32), shape((UNIT, D), BF)],
        compiler_params=params(),
        cost_estimate=pl.CostEstimate(flops=20_000_000, bytes_accessed=7_000_000, transcendentals=1000),
    )(near, cont, *own, w_all, w_all, w_all, *f_parts, d_mid, w_all)


def total_of(*parts):
    total = parts[0].astype(F32)
    for part in parts[1:]:
        total = total + part.astype(F32)
    return total.astype(BF)


def run_whole(kernel, outs, *args, dtype=BF):
    return pl.pallas_call(
        kernel,
        in_specs=[pl.BlockSpec(memory_space=pltpu.SMEM)]
        + [pl.BlockSpec(memory_space=pltpu.VMEM)] * (len(args) - 1),
        out_specs=[pl.BlockSpec(memory_space=pltpu.VMEM)] * len(outs),
        out_shape=[shape(dims, dtype) for dims in outs],
        compiler_params=params(),
        cost_estimate=pl.CostEstimate(flops=1_000_000, bytes_accessed=7_000_000, transcendentals=0),
    )(*args)


def fold_two_kernel(where_ref, a0_ref, a1_ref, b0_ref, b1_ref, ak_ref, ag_ref, bk_ref, bg_ref):
    y_at, side = where_ref[0] % 2, where_ref[1]
    ak_ref[0] = total_of(a0_ref[0, y_at], a1_ref[0, y_at])
    ag_ref[0] = total_of(a0_ref[0, 1 - y_at], a1_ref[0, 1 - y_at])
    bk_ref[0] = total_of(b0_ref[0, side], b1_ref[0, side])
    bg_ref[0] = total_of(b0_ref[0, 1 - side], b1_ref[0, 1 - side])


def fold_more_kernel(
    where_ref, a0_ref, a1_ref, b0_ref, b1_ref, c0_ref, c1_ref, ak_ref, ag_ref, bk_ref, bg_ref, c_ref
):
    fold_two_kernel(
        where_ref, a0_ref, a1_ref, b0_ref, b1_ref, ak_ref, ag_ref, bk_ref, bg_ref
    )
    c_ref[...] = total_of(c0_ref[...], c1_ref[...])


def run_by_z(kernel, outs, *args):
    def spec(dims):
        block = (dims[0] // 4, *dims[1:])
        return pl.BlockSpec(block, lambda z: (z,) + (0,) * (len(dims) - 1))

    return pl.pallas_call(
        kernel,
        grid=(4,),
        in_specs=[pl.BlockSpec(memory_space=pltpu.SMEM)] + [spec(arg.shape) for arg in args[1:]],
        out_specs=[spec(dims) for dims in outs],
        out_shape=[shape(dims, BF) for dims in outs],
        compiler_params=params(),
        cost_estimate=pl.CostEstimate(flops=1_000_000, bytes_accessed=7_000_000, transcendentals=0),
    )(*args)


def fold_halves_kernel(where_ref, a0_ref, a1_ref, b0_ref, b1_ref, *outs):
    for z in range(4):
        at = slice(z, z + 1)
        fold_two_kernel(
            where_ref, *[ref.at[at] for ref in (a0_ref, a1_ref, b0_ref, b1_ref, *outs)]
        )


def fold_rows_kernel(where_ref, a0_ref, a1_ref, b0_ref, b1_ref, *outs):
    z_at = where_ref[0] // 2
    rows = a0_ref.shape[1]
    for step, out_ref in enumerate(outs):
        z = jnp.bitwise_xor(z_at, step)
        out_ref[0:rows, :] = total_of(a0_ref[z], a1_ref[z])
        out_ref[rows:, :] = total_of(b0_ref[z], b1_ref[z])


def fold_cols_kernel(where_ref, a0_ref, a1_ref, b0_ref, b1_ref, *outs):
    z_at = where_ref[0] // 2
    cols = a0_ref.shape[2]
    for step, out_ref in enumerate(outs):
        z = jnp.bitwise_xor(z_at, step)
        out_ref[:, 0:cols] = total_of(a0_ref[z], a1_ref[z])
        out_ref[:, cols:] = total_of(b0_ref[z], b1_ref[z])


def fold_core_kernel(where_ref, own_ref, got_ref, ak_ref, ag_ref, bk_ref, bg_ref):
    y_at, side = where_ref[0] % 2, where_ref[1]
    left, right = slice(0, LEFT), slice(LEFT, WIDE)

    def block(y, x, cols):
        rows = pl.ds(pl.multiple_of((2 * y + x) * SUB, 16), SUB)
        return total_of(own_ref[rows, cols], got_ref[rows, cols])

    for at in range(2):
        ak_ref[0, at] = block(at, side, left)
        ag_ref[0, at] = block(at, 1 - side, left)
        bk_ref[0, at] = block(y_at, at, right)
        bg_ref[0, at] = block(1 - y_at, at, right)


def take_kernel(where_ref, qkv_ref, out_ref, gain_a_ref, gain_m_ref, piece_ref):
    rows = pl.ds(pl.multiple_of(where_ref[1] * SUB, 16), SUB)
    for core, gain_ref in ((0, gain_a_ref), (1, gain_m_ref)):

        @pl.when(where_ref[2] == core)
        def _():
            if core == 0:
                piece_ref[:, 0:HALF] = qkv_ref[rows, 0:HALF]
            else:
                piece_ref[:, 0:D] = qkv_ref[rows, HALF:]
                piece_ref[:, D:HALF] = out_ref[rows, :]
            wide = jnp.broadcast_to(gain_ref[...].astype(F32), (128, 2 * SUB)).T
            piece_ref[:, HALF:] = jnp.where(where_ref[1] == 0, wide[0:SUB], wide[SUB:]).astype(BF)


def split_cols_kernel(where_ref, a0_ref, a1_ref, a2_ref, a3_ref, left_ref, right_ref):
    for at, ref in enumerate((a0_ref, a1_ref, a2_ref, a3_ref)):
        left_ref[at] = ref[:, 0:LEFT]
        right_ref[at] = ref[:, LEFT:]


def join_kernel(where_ref, a0_ref, a1_ref, b0_ref, b1_ref, left_ref, right_ref):
    for out_ref, parts in ((left_ref, (a0_ref, a1_ref)), (right_ref, (b0_ref, b1_ref))):
        out_ref[0:4] = parts[0][...]
        out_ref[4:8] = parts[1][...]


def split_rows_kernel(where_ref, m0_ref, m1_ref, m2_ref, m3_ref, up_ref, down_ref):
    for at, ref in enumerate((m0_ref, m1_ref, m2_ref, m3_ref)):
        up_ref[at] = ref[0 : 2 * SUB, :]
        down_ref[at] = ref[2 * SUB :, :]


def unpack_kernel(where_ref, here_ref, far_ref, up_ref, down_ref):
    side, core = where_ref[1], where_ref[2]
    first = core == 0
    for x in range(2):
        at = jnp.bitwise_xor(side, x)
        rows = slice(x * SUB, (x + 1) * SUB)
        here, far = here_ref[at].astype(F32), far_ref[at].astype(F32)
        low, high = jnp.where(first, here, far), jnp.where(first, far, here)
        down_ref[x * FSUB : (x + 1) * FSUB, :] = low[2 * SUB :]
        down_ref[(2 + x) * FSUB : (3 + x) * FSUB, :] = high[2 * SUB :]
        for half in range(2):
            own = slice(half * SUB, (half + 1) * SUB)
            for i in range(4):
                cols = slice(i * 2 * FSUB, (i + 1) * 2 * FSUB)
                start = (half * 4 + i) * 4 * FSUB
                up_ref[rows, start : start + 4 * FSUB] = jnp.concatenate(
                    [low[own, cols], high[own, cols]], axis=1
                )


def finish_kernel(
    where_ref, own_ref, side_ref, core_ref, far_ref, qkv_ref, out_ref, gain_a_ref, gain_m_ref
):
    first, near = where_ref[2] == 0, where_ref[1] == 0
    columns = []
    for x in range(2):
        mine = jnp.where(near == (x == 0), own_ref[...], side_ref[...]).astype(F32)
        theirs = jnp.where(near == (x == 0), core_ref[...], far_ref[...]).astype(F32)
        low, high = jnp.where(first, mine, theirs), jnp.where(first, theirs, mine)
        rows = slice(x * SUB, (x + 1) * SUB)
        qkv_ref[rows, 0:HALF] = low[:, 0:HALF]
        qkv_ref[rows, HALF:] = high[:, 0:D]
        out_ref[rows, :] = high[:, D:HALF]
        columns.append((low[:, HALF:], high[:, HALF:]))
    for at, gain_ref in enumerate((gain_a_ref, gain_m_ref)):
        both = jnp.concatenate([columns[0][at], columns[1][at]], axis=0)
        gain_ref[...] = both.T[0:1, :]


def over(axis, value, bits):
    return lax.ppermute(value, axis, [(i, i ^ bits) for i in range(lax.axis_size(axis))])


def cut(values, start, rows=PR):
    return lax.dynamic_slice_in_dim(values, start, rows, 0)


def pick(values, at):
    return lax.dynamic_index_in_dim(values, at, 0, keepdims=False)


def pick_of(values, at, axis):
    return lax.dynamic_index_in_dim(values, at, axis, keepdims=False)


def tie(*values):
    return lax.optimization_barrier(values)


def per_device(tokens, w_qkv, w_out, w_up, w_down, gain_attn, gain_mlp, d_out):
    staged = lax.axis_size("shard") == 8
    shard = lax.axis_index("shard")
    rep = lax.axis_index("rep")
    side, core = rep // 2, rep % 2
    pos = shard % 8
    y_at, z_at = pos % 2, pos // 2
    table = [pos ^ d for d in ORDER] if staged else [jnp.int32(2 * (d % 4) + d // 4) for d in range(8)]
    where = jnp.stack([pos, side, core] + [jnp.int32(0)] * 5 + table).astype(jnp.int32)

    def to_give(values):
        return jnp.concatenate([cut(values, (1 - y_at) * PR), cut(values, (3 - y_at) * PR)], axis=0)

    def own_parts(values, got):
        mine_p, mine_c = cut(values, y_at * PR), cut(values, (2 + y_at) * PR)
        return (
            jnp.concatenate([mine_p, got[:PR]], axis=0), jnp.concatenate([mine_c, got[PR:]], axis=0)
        )

    def to_return(values):
        return jnp.concatenate([values[PR : 2 * PR], values[3 * PR :]], axis=0)

    def home_rows(keep_p, keep_c, got):
        got = got.astype(keep_p.dtype)
        first = y_at == 0
        return jnp.concatenate(
            [
                jnp.where(first, keep_p, got[:PR]),
                jnp.where(first, got[:PR], keep_p),
                jnp.where(first, keep_c, got[PR:]),
                jnp.where(first, got[PR:], keep_c),
            ],
            axis=0,
        )

    def wide(gain):
        return jnp.broadcast_to(gain[:, None], (gain.shape[0], 128))

    def halves(qkv, out, gain_a, gain_m):
        return (
            jnp.concatenate([qkv[:, :HALF], wide(gain_a)], axis=1),
            jnp.concatenate([qkv[:, HALF:], out, wide(gain_m)], axis=1),
        )

    def half_up(up):
        return pick_of(up.reshape(up.shape[0], 8, 2, 2 * FSUB), core, 2).reshape(up.shape[0], FH)

    def own_up(up):
        mine = half_up(cut(up, side * SUB, SUB))
        return jnp.concatenate([mine[:, :D], mine[:, D:]], axis=0)

    if staged:
        (own_piece,) = run_whole(
            take_kernel, [(SUB, WIDE)], where, w_qkv, w_out,
            gain_attn.reshape(1, 2 * SUB), gain_mlp.reshape(1, 2 * SUB),
        )
        own_mlp = jnp.concatenate(
            [own_up(w_up), cut(w_down, core * 2 * FSUB + side * FSUB, FSUB)], axis=0
        )
        t_got, z1, z2, z3 = tie(
            over("shard", to_give(tokens), 1),
            *[over("shard", own_piece, k) for k in (2, 4, 6)],
        )
        near, cont = own_parts(tokens, t_got)
        left, right = run_whole(
            split_cols_kernel, [(4, SUB, LEFT), (4, SUB, WIDE - LEFT)], where, own_piece, z1, z2, z3
        )
        own_mlp, near, left, right = tie(own_mlp, near, left, right)
        m1, m3, left_y, right_x, g_got = tie(
            over("shard", own_mlp, 2),
            over("shard", own_mlp, 6),
            over("shard", left, 1),
            over("rep", right, 2),
            over("shard", to_give(d_out), 1),
        )
        left, right = run_whole(
            join_kernel, [(8, SUB, LEFT), (8, SUB, WIDE - LEFT)], where, left, left_y, right, right_x
        )
        m3, near, left, right = tie(m3, near, left, right)
        m2, near3, left_x, right_y, left_core, right_core = tie(
            over("shard", m3, 2),
            over("shard", near, 6),
            over("rep", left, 2),
            over("shard", right, 1),
            over("rep", left, 1),
            over("rep", right, 1),
        )
        up, down = run_whole(
            split_rows_kernel, [(4, 2 * SUB, D), (4, FSUB, D)], where, own_mlp, m1, m2, m3
        )
        near, near3, left_x, right_y, up, down = tie(near, near3, left_x, right_y, up, down)
        near1, near2, up_y, down_x, left_far, right_far = tie(
            over("shard", near, 2),
            over("shard", near3, 2),
            over("shard", up, 1),
            over("rep", down, 2),
            over("rep", left_x, 1),
            over("rep", right_y, 1),
        )
        pieces = (left, left_x, left_core, left_far, right, right_y, right_core, right_far)
        up, up_y, down, down_x, pieces = tie(up, up_y, down, down_x, pieces)
        mlp_pieces = (
            up, over("rep", up, 2), up_y, over("rep", up_y, 2),
            down, down_x, over("shard", down, 1), over("shard", down_x, 1),
        )
    else:
        gathered = [
            lax.all_gather(w, "shard", axis=0, tiled=True)
            for w in (w_qkv, w_out, gain_attn, gain_mlp, w_up, w_down)
        ]
        natural = jnp.stack(halves(*gathered[:4])).reshape(2, 4, 2, 2, SUB, WIDE)
        pieces = []
        for dc in (0, 1):
            by_core = pick(natural, core ^ dc)
            for dx in (0, 1):
                both = pick_of(by_core[..., :LEFT], side ^ dx, 2)
                pieces.append(jnp.concatenate([both[:, 0], both[:, 1]], axis=0))
        for dc in (0, 1):
            by_core = pick(natural, core ^ dc)[..., LEFT:]
            for dy in (0, 1):
                both = [pick_of(by_core[:, dy], side ^ dx, 1) for dx in (0, 1)]
                pieces.append(jnp.concatenate(both, axis=0))
        pieces = tuple(pieces)
        up = half_up(gathered[4]).reshape(4, 2, 2, SUB, 2, D).transpose(1, 0, 2, 4, 3, 5)
        up = up.reshape(2, 4, 2, 2 * SUB, D)
        down = pick_of(gathered[5].reshape(4, 2, 2, 2, FSUB, D), core, 2).transpose(1, 0, 2, 3, 4)
        mlp_pieces = tuple(
            pick_of(both[dy], side ^ dx, 1) for both in (up, down) for dy in (0, 1) for dx in (0, 1)
        )
        near, cont = own_parts(tokens, over("shard", to_give(tokens), 1))
        near1, near2, near3 = [over("shard", near, k) for k in (2, 4, 6)]
        g_got = over("shard", to_give(d_out), 1)
    parts = (near, near1, near2, near3, cont)
    g_own = jnp.concatenate(own_parts(d_out, g_got), axis=0)
    parts, g_own = tie(parts, g_own)

    g_core = over("rep", g_own, 1)
    forward = attn_fwd(where, parts, pieces)
    forward, mlp_pieces, g_core = tie(forward, mlp_pieces, g_core)
    w_all, q, k, v, e, ec, attended, inv_sum, middle, nm, normed = forward

    nm_core, nm = tie(over("rep", nm, 1), nm)
    e_own, y_own, e_give, y_give, *mlp_grads = mlp(
        where, (nm, nm_core), (g_own, g_core), mlp_pieces
    )
    e_got, y_give, mlp_grads = tie(over("rep", e_give, 1), y_give, mlp_grads)
    up_keep, up_give, down_keep, down_give = mlp_grads
    y_got = over("rep", y_give, 1)
    if staged:
        up_got, down_got = over("rep", up_give, 2), over("shard", down_give, 1)
    d_mid, d_att, d_right = branch(middle, g_own, e_own, e_got, attended, w_all)

    saved = (q, k, v, e, ec, attended, inv_sum)
    kv2, f2_give, dq = attn_bwd((2,), saved, d_att, w_all)
    y_got, dq = tie(y_got, dq)
    block_rows = (middle + y_own.astype(F32) + y_got.astype(F32)).astype(BF)
    block_give = to_return(block_rows)
    f2_give, dq, block_give = tie(f2_give, dq, block_give)
    f2_got = over("shard", f2_give, 2)
    kv3, kv1, f3_give, f1_give, dq = attn_bwd((3, 1), saved, d_att, w_all, dq)
    f2_got, f3_give, f1_give, dq, block_give = tie(f2_got, f3_give, f1_give, dq, block_give)
    if staged:
        up_got, down_got, dq = tie(up_got, down_got, dq)
        by_pair = (4, 2, 2 * SUB, D)
        f3_send = total_of(f3_give, f2_got)
        folded = run_by_z(
            fold_two_kernel, [(4, 2 * SUB, D)] * 4, where,
            up_keep.reshape(by_pair), up_got.reshape(by_pair), down_keep, down_got,
        )
        (up_keep, up_give, down_keep, down_give), dq, f3_send, f1_give, block_give = tie(
            folded, dq, f3_send, f1_give, block_give
        )
        up_got, down_got = over("shard", up_give, 1), over("rep", down_give, 2)
    else:
        f3_send = total_of(f3_give, f2_got)
    f1, f3, b_got = over("shard", f1_give, 2), over("shard", f3_send, 6), over("shard", block_give, 1)
    keep, give, *own = attn_bwd(
        (0,), saved, d_att, w_all, dq, (where, normed, (kv1, kv2, kv3), d_right)
    )
    f1, f3, b_got, keep, give, own = tie(f1, f3, b_got, keep, give, own)
    if staged:
        up_got, down_got, give = tie(up_got, down_got, give)
        mlp_total, *mlp_gives = run_whole(
            fold_rows_kernel, [(4 * SUB, D)] * 4, where, up_keep, up_got, down_keep, down_got
        )
        chip_got, mlp_gives = tie(over("rep", give, 1), mlp_gives)
        m2 = over("shard", mlp_gives[1], 2)
        left, right = (4, 2, SUB, LEFT), (4, 2, SUB, WIDE - LEFT)
        left_keep, left_give, right_keep, right_give = run_by_z(
            fold_core_kernel, [left, left, right, right], where, keep, chip_got
        )
        left_give, right_give, m2, mlp_gives, own = tie(left_give, right_give, m2, mlp_gives, own)
        m1_send, m3_send = mlp_gives[0], total_of(mlp_gives[2], m2)
        left_got, right_got, m1, m3, token_keep, token_give = tie(
            over("rep", left_give, 2),
            over("shard", right_give, 1),
            over("shard", m1_send, 2),
            over("shard", m3_send, 6),
            *tail(near, cont, own, (f1, f3), d_mid, w_all),
        )
        mlp_total = total_of(mlp_total, m1, m3)
        left_keep, left_give, right_keep, right_give = run_whole(
            fold_halves_kernel,
            [(4, SUB, LEFT)] * 2 + [(4, SUB, WIDE - LEFT)] * 2,
            where, left_keep, left_got, right_keep, right_got,
        )
        left_got, right_got, mlp_total = tie(
            over("shard", left_give, 1), over("rep", right_give, 2), mlp_total
        )
        total, *gives = run_whole(
            fold_cols_kernel, [(SUB, WIDE)] * 4, where, left_keep, left_got, right_keep, right_got
        )
        z1, z2, z3, m_got, mlp_total, t_got = tie(
            *[over("shard", gives[step - 1], 2 * step) for step in (1, 2, 3)],
            over("rep", mlp_total, 2),
            mlp_total,
            over("shard", token_give, 1),
        )
        by_side = jnp.stack([mlp_total, m_got])
        total = total_of(total, z1, z2, z3)
        other, core_got, m_got, by_side = tie(
            over("rep", total, 2), over("rep", total, 1), over("rep", by_side, 1), by_side
        )
        far = over("rep", other, 1)
        d_wup, d_wdown = run_whole(
            unpack_kernel, [(2 * SUB, FF), (4 * FSUB, D)], where, by_side, m_got, dtype=F32
        )
        d_wqkv, d_wout, d_gain_attn, d_gain_mlp = run_whole(
            finish_kernel, [(2 * SUB, 3 * D), (2 * SUB, D), (1, 2 * SUB), (1, 2 * SUB)],
            where, total, other, core_got, far, dtype=F32,
        )
        d_gain_attn, d_gain_mlp = d_gain_attn.reshape(2 * SUB), d_gain_mlp.reshape(2 * SUB)
    else:
        token_keep, token_give = tail(near, cont, own, (f1, f3), d_mid, w_all)
        t_got = over("shard", token_give, 1)
        low, high = jnp.where(core == 0, keep, give), jnp.where(core == 0, give, keep)

        def by_side_of(keep, give, at):
            first = at == 0
            return jnp.stack([jnp.where(first, keep, give), jnp.where(first, give, keep)])

        up = by_side_of(up_keep, up_give, side).reshape(2, 8, 2, SUB, D)
        up = up.transpose(1, 0, 3, 2, 4).reshape(D, 8, 1, 2 * FSUB)
        down = by_side_of(down_keep, down_give, y_at).transpose(1, 0, 2, 3, 4)
        down = down.reshape(8, 1, 2 * FSUB, D)
        peer_up, peer_down = over("rep", up, 1), over("rep", down, 1)
        first = core == 0
        up, peer_up = jnp.where(first, up, peer_up), jnp.where(first, peer_up, up)
        down, peer_down = jnp.where(first, down, peer_down), jnp.where(first, peer_down, down)
        up = jnp.concatenate([up, peer_up], axis=2).reshape(D, FF)
        down = jnp.concatenate([down, peer_down], axis=1).reshape(FF, D)
        rest = lambda v: (v.astype(F32) + over("rep", v, 2).astype(F32)).astype(BF)
        up, down = rest(up), rest(down)
        scatter = lambda v: lax.psum_scatter(v, "shard", scatter_dimension=0, tiled=True)
        d_wup, d_wdown = scatter(up).astype(F32), scatter(down).astype(F32)
        low = lax.psum(scatter(low), "rep").astype(F32)
        high = lax.psum(scatter(high), "rep").astype(F32)
        d_wqkv = jnp.concatenate([low[:, :HALF], high[:, :D]], axis=1)
        d_wout, d_gain_attn, d_gain_mlp = high[:, D:HALF], low[:, HALF], high[:, HALF]

    return (
        home_rows(block_rows[:PR], block_rows[2 * PR : 3 * PR], b_got),
        home_rows(token_keep[:PR], token_keep[PR:], t_got),
        d_wqkv,
        d_wout,
        d_wup,
        d_wdown,
        d_gain_attn,
        d_gain_mlp,
    )


def solution(mesh):
    weights = P("shard", None)
    rows = P(("rep", "shard"), None)
    return jax.shard_map(
        per_device,
        mesh=mesh,
        in_specs=(rows, weights, weights, weights, weights, P("shard"), P("shard"), rows),
        out_specs=(rows, rows, weights, weights, weights, weights, P("shard"), P("shard")),
        check_vma=False,
    )
```

```python
import jax
import jax.numpy as jnp
from jax import lax
from jax.experimental import pallas as pl
from jax.experimental.pallas import tpu as pltpu
from jax.sharding import PartitionSpec as P

D = 768
HEADS = 12
HDIM = 64
FF = 3072
PR = 128
PLEN = 1024
KEYS = PLEN + 2 * PR
ROWS = 4 * PR
PAIRS = HEADS // 2
WIDTH = 2 * HDIM
HALF = 1536
WIDE = HALF + 128
SUB = 48
LEFT = 896
RIGHT = D + 128
UNIT = 2 * PR
FSUB = 96
FH = FF // 2
norm_eps = 1e-05
neg_fill = -1e30
SCALE = HDIM ** (-0.5)
GELU_C = 0.7978845608028654
GELU_A = 0.044715
BF = jnp.bfloat16
F32 = jnp.float32
VMEM_LIMIT = 60 * 1024 * 1024
BLOCKS = (0, 1, 2, 3, 4, 5, 6, 7)
ORDER = (0, 2, 4, 6, 1, 3, 5, 7)


def dot_nt(a, b):
    return lax.dot_general(a, b, (((1,), (1,)), ((), ())), preferred_element_type=F32)


def dot_tn(a, b):
    return lax.dot_general(a, b, (((0,), (0,)), ((), ())), preferred_element_type=F32)


def dot_nn(a, b):
    return jnp.dot(a, b, preferred_element_type=F32)


def rms_inv(values):
    return lax.rsqrt(jnp.mean(values * values, axis=-1, keepdims=True) + norm_eps)


def params():
    return pltpu.CompilerParams(vmem_limit_bytes=VMEM_LIMIT)


def shape(dims, dtype):
    return jax.ShapeDtypeStruct(dims, dtype)


def fill_normed(x_ref, gain, normed_ref):
    @pl.loop(0, KEYS, step=PR)
    def _(row):
        rows = pl.ds(pl.multiple_of(row, PR), PR)
        part = x_ref[rows, :].astype(F32)
        normed_ref[rows, :] = (part * rms_inv(part) * gain).astype(BF)


def lane_half(head):
    lanes = lax.broadcasted_iota(jnp.int32, (1, WIDTH), 1)
    return (lanes >= HDIM) if head else (lanes < HDIM)


def sum_column(values):
    return jnp.broadcast_to(jnp.sum(values, axis=0, keepdims=True), (128, values.shape[1])).T


def gain_row(column):
    return column.astype(F32).T[0:1, :]


def attn_fwd_kernel(
    where_ref, x0_ref, x1_ref, x2_ref, x3_ref, xc_ref,
    l00_ref, l10_ref, l01_ref, l11_ref, r00_ref, r10_ref, r01_ref, r11_ref,
    w_out_ref, q_ref, k_ref, v_ref, e_ref, ec_ref, o_ref, r_ref, mid_ref, nm_ref, normed_out_ref,
    w_ref, x_ref, normed_ref, bias_ref, att_ref, qs_ref, s_ref, inv_ref, out_ref, sems, out_sems,
):
    step = pl.program_id(0)
    late = [
        pltpu.make_async_copy(w_ref, w_out_ref, out_sems.at[0]),
        pltpu.make_async_copy(normed_ref, normed_out_ref, out_sems.at[1]),
    ]

    @pl.when(step == 0)
    def _():
        side, core = where_ref[1], where_ref[2]
        copies = []
        for at, (dx, dc, piece) in enumerate(
            ((0, 0, l00_ref), (1, 0, l10_ref), (0, 1, l01_ref), (1, 1, l11_ref))
        ):
            for i in range(8):
                start = where_ref[8 + i] * (2 * SUB) + jnp.bitwise_xor(side, dx) * SUB
                copies.append(
                    pltpu.make_async_copy(
                        piece.at[i],
                        w_ref.at[
                            jnp.bitwise_xor(core, dc),
                            pl.ds(pl.multiple_of(start, 16), SUB),
                            pl.ds(0, LEFT),
                        ],
                        sems.at[at * 8 + i],
                    )
                )
        for at, (far, dc, piece) in enumerate(
            ((0, 0, r00_ref), (1, 0, r10_ref), (0, 1, r01_ref), (1, 1, r11_ref))
        ):
            for i in range(8):
                start = where_ref[8 + far * 4 + i % 4] * (2 * SUB)
                start = start + jnp.bitwise_xor(side, i // 4) * SUB
                copies.append(
                    pltpu.make_async_copy(
                        piece.at[i],
                        w_ref.at[
                            jnp.bitwise_xor(core, dc),
                            pl.ds(pl.multiple_of(start, 16), SUB),
                            pl.ds(LEFT, WIDE - LEFT),
                        ],
                        sems.at[32 + at * 8 + i],
                    )
                )
        for at, part in enumerate((x0_ref, x1_ref, x2_ref, x3_ref, xc_ref)):
            copies.append(
                pltpu.make_async_copy(part, x_ref.at[pl.ds(at * UNIT, UNIT), :], sems.at[64 + at])
            )
        for copy in copies:
            copy.start()
        pos = where_ref[0]
        row = lax.broadcasted_iota(jnp.int32, (PR, PR), 0)
        col = lax.broadcasted_iota(jnp.int32, (PR, PR), 1)
        tri = jnp.where(col <= row, 0.0, neg_fill)
        for part in range(2):
            mine = jnp.bitwise_xor(pos, BLOCKS[part])
            for block in range(8):
                at = (pl.ds(part * PR, PR), pl.ds(block * PR, PR))
                if block == part:
                    bias_ref[at] = tri
                else:
                    seen = jnp.bitwise_xor(pos, BLOCKS[block]) < mine
                    bias_ref[at] = jnp.full((PR, PR), jnp.where(seen, 0.0, neg_fill), F32)
        for copy in copies:
            copy.wait()
        late[0].start()
        fill_normed(x_ref, gain_row(w_ref[0, :, HALF:]), normed_ref)
        late[1].start()

    at = pl.ds(pl.multiple_of(step * UNIT, UNIT), UNIT)
    at_k = pl.ds(pl.multiple_of(D + step * UNIT, UNIT), UNIT)
    k_ref[...] = dot_nn(normed_ref[...], w_ref[0, :, at_k]).astype(BF)
    v_ref[...] = dot_nn(normed_ref[...], w_ref[1, :, at]).astype(BF)
    wq = w_ref[0, :, at]
    q_ref[0:UNIT, :] = (dot_nn(normed_ref[0:UNIT, :], wq) * SCALE).astype(BF)
    q_ref[UNIT:, :] = (dot_nn(normed_ref[PLEN:, :], wq) * SCALE).astype(BF)
    row = lax.broadcasted_iota(jnp.int32, (PR, PR), 0)
    col = lax.broadcasted_iota(jnp.int32, (PR, PR), 1)
    tri = jnp.where(col <= row, 0.0, neg_fill)
    low_half = lane_half(0)
    for pair in range(2):
        lanes = slice(pair * WIDTH, (pair + 1) * WIDTH)
        query = q_ref[:, lanes]
        for head in range(2):
            rows = slice(head * ROWS, (head + 1) * ROWS)
            qs_ref[rows, :] = jnp.where(lane_half(head), query, jnp.zeros_like(query))
        s_ref[...] = dot_nt(qs_ref[...], k_ref[0:PLEN, lanes])
        for head in range(2):
            for chunk in range(4):
                mine = slice(chunk * PR, (chunk + 1) * PR)
                rows = slice(head * ROWS + chunk * PR, head * ROWS + (chunk + 1) * PR)
                scores = s_ref[rows, :]
                if chunk < 2:
                    scores = scores + bias_ref[mine, :]
                    top = jnp.max(scores, axis=-1, keepdims=True)
                    terms = jnp.exp(scores - top)
                    total = jnp.sum(terms, axis=-1, keepdims=True)
                else:
                    own = slice(PLEN + (chunk - 2) * PR, PLEN + (chunk - 1) * PR)
                    near = dot_nt(qs_ref[rows, :], k_ref[own, lanes]) + tri
                    top = jnp.maximum(
                        jnp.max(scores, axis=-1, keepdims=True),
                        jnp.max(near, axis=-1, keepdims=True),
                    )
                    terms = jnp.exp(scores - top)
                    near_terms = jnp.exp(near - top)
                    total = jnp.sum(terms, axis=-1, keepdims=True) + jnp.sum(
                        near_terms, axis=-1, keepdims=True
                    )
                    ec_ref[2 * pair + head, (chunk - 2) * PR : (chunk - 1) * PR, :] = (
                        near_terms.astype(BF)
                    )
                e_ref[2 * pair + head, mine, :] = terms.astype(BF)
                inv_ref[rows, :] = jnp.broadcast_to(1.0 / total, (PR, WIDTH))
        terms = e_ref[2 * pair : 2 * pair + 2].reshape(2 * ROWS, PLEN)
        out_ref[...] = dot_nn(terms, v_ref[0:PLEN, lanes])
        for head in range(2):
            for side in range(2):
                own = slice(PLEN + side * PR, PLEN + (side + 1) * PR)
                start = head * ROWS + (2 + side) * PR
                near = ec_ref[2 * pair + head, side * PR : (side + 1) * PR, :]
                out_ref[start : start + PR, :] += dot_nn(near, v_ref[own, lanes])
        inv = jnp.where(low_half, inv_ref[0:ROWS, :], inv_ref[ROWS:, :])
        r_ref[:, lanes] = inv
        o_ref[:, lanes] = (
            jnp.where(low_half, out_ref[0:ROWS, :], out_ref[ROWS:, :]) * inv
        ).astype(BF)
    att_ref[step] = o_ref[...]

    @pl.when(step == pl.num_programs(0) - 1)
    def _():
        wout = w_ref[1, :, D:HALF]
        gain = gain_row(w_ref[1, :, HALF:])
        for chunk in range(4):
            rows = slice(chunk * PR, (chunk + 1) * PR)
            from_row = chunk * PR if chunk < 2 else PLEN + (chunk - 2) * PR
            middle = x_ref[from_row : from_row + PR, :].astype(F32)
            for i in range(3):
                middle = middle + dot_nn(att_ref[i, rows, :], wout[i * UNIT : (i + 1) * UNIT, :])
            mid_ref[rows, :] = middle
            nm_ref[rows, :] = (middle * rms_inv(middle) * gain).astype(BF)
        for copy in late:
            copy.wait()


def attn_fwd(where, parts, pieces):
    pair = lambda i: (0, i)
    whole = lambda i: (0, 0)
    heads = lambda i: (i, 0, 0)
    anywhere = pl.BlockSpec(memory_space=pl.ANY)
    return pl.pallas_call(
        attn_fwd_kernel,
        grid=(3,),
        in_specs=[
            pl.BlockSpec(memory_space=pltpu.SMEM),
            *[anywhere] * 13,
        ],
        out_specs=[
            anywhere,
            pl.BlockSpec((ROWS, UNIT), pair),
            pl.BlockSpec((KEYS, UNIT), pair),
            pl.BlockSpec((KEYS, UNIT), pair),
            pl.BlockSpec((4, ROWS, PLEN), heads),
            pl.BlockSpec((4, UNIT, PR), heads),
            pl.BlockSpec((ROWS, UNIT), pair),
            pl.BlockSpec((ROWS, UNIT), pair),
            pl.BlockSpec((ROWS, D), whole),
            pl.BlockSpec((ROWS, D), whole),
            anywhere,
        ],
        out_shape=[
            shape((2, D, WIDE), BF),
            shape((ROWS, D), BF),
            shape((KEYS, D), BF),
            shape((KEYS, D), BF),
            shape((HEADS, ROWS, PLEN), BF),
            shape((HEADS, 2 * PR, PR), BF),
            shape((ROWS, D), BF),
            shape((ROWS, D), F32),
            shape((ROWS, D), F32),
            shape((ROWS, D), BF),
            shape((KEYS, D), BF),
        ],
        scratch_shapes=[
            pltpu.VMEM((2, D, WIDE), BF),
            pltpu.VMEM((KEYS, D), BF),
            pltpu.VMEM((KEYS, D), BF),
            pltpu.VMEM((2 * PR, PLEN), F32),
            pltpu.VMEM((3, ROWS, UNIT), BF),
            pltpu.VMEM((2 * ROWS, WIDTH), BF),
            pltpu.VMEM((2 * ROWS, PLEN), F32),
            pltpu.VMEM((2 * ROWS, WIDTH), F32),
            pltpu.VMEM((2 * ROWS, WIDTH), F32),
            pltpu.SemaphoreType.DMA((69,)),
            pltpu.SemaphoreType.DMA((2,)),
        ],
        compiler_params=params(),
        cost_estimate=pl.CostEstimate(
            flops=30_000_000_000, bytes_accessed=30_000_000, transcendentals=6_300_000
        ),
    )(where, *parts, *pieces)


def mlp_kernel(
    where_ref, nm0_ref, nm1_ref, g0_ref, g1_ref,
    up00_ref, up10_ref, up01_ref, up11_ref, down00_ref, down10_ref, down01_ref, down11_ref,
    e_ref, y_ref, give_e_ref, give_y_ref, up_keep_ref, up_give_ref, down_keep_ref, down_give_ref,
    wup_ref, wdown_ref, nm_ref, g_ref, acc_e_ref, acc_y_ref, part_ref, active_ref, d_hidden_ref, sems,
):
    step = pl.program_id(0)
    side, y_at = where_ref[1], where_ref[0] % 2

    @pl.when(step == 0)
    def _():
        copies = []
        for dy, ups, downs in (
            (0, (up00_ref, up10_ref), (down00_ref, down10_ref)),
            (1, (up01_ref, up11_ref), (down01_ref, down11_ref)),
        ):
            for dx in range(2):
                for i in range(4):
                    block = where_ref[8 + dy * 4 + i] * 2 + jnp.bitwise_xor(side, dx)
                    rows = pl.ds(pl.multiple_of(block * SUB, 16), SUB)
                    for half in range(2):
                        copies.append(
                            pltpu.make_async_copy(
                                ups[dx].at[i, pl.ds(half * SUB, SUB), :],
                                wup_ref.at[rows, pl.ds(half * D, D)],
                                sems.at[len(copies)],
                            )
                        )
                    copies.append(
                        pltpu.make_async_copy(
                            downs[dx].at[i],
                            wdown_ref.at[pl.ds(pl.multiple_of(block * FSUB, 16), FSUB), :],
                            sems.at[len(copies)],
                        )
                    )
        for copy in copies:
            copy.start()
        nm_ref[0:ROWS, :] = nm0_ref[...]
        nm_ref[ROWS:, :] = nm1_ref[...]
        g_ref[0:ROWS, :] = g0_ref[...]
        g_ref[ROWS:, :] = g1_ref[...]
        for copy in copies:
            copy.wait()

    at = pl.ds(pl.multiple_of(step * D, D), D)
    for start in range(0, 2 * ROWS, 256):
        rows = slice(start, start + 256)
        hidden = dot_nn(nm_ref[rows, :], wup_ref[:, at])
        square = hidden * hidden
        th = jnp.tanh(hidden * (GELU_C + GELU_C * GELU_A * square))
        left = 0.5 + 0.5 * th
        active_ref[rows, :] = (hidden * left).astype(BF)
        slope = left + hidden * (0.5 - 0.5 * th * th) * (GELU_C + 3.0 * GELU_A * GELU_C * square)
        d_hidden_ref[rows, :] = (dot_nt(g_ref[rows, :], wdown_ref[at, :]) * slope).astype(BF)
    part_y = dot_nn(active_ref[...], wdown_ref[at, :])
    part_e = dot_nt(d_hidden_ref[...], wup_ref[:, at])

    @pl.when(step == 0)
    def _():
        acc_y_ref[...] = part_y
        acc_e_ref[...] = part_e

    @pl.when(step == 1)
    def _():
        e_ref[...] = (acc_e_ref[0:ROWS, :] + part_e[0:ROWS]).astype(BF)
        y_ref[...] = (acc_y_ref[0:ROWS, :] + part_y[0:ROWS]).astype(BF)
        give_e_ref[...] = (acc_e_ref[ROWS:, :] + part_e[ROWS:]).astype(BF)
        give_y_ref[...] = (acc_y_ref[ROWS:, :] + part_y[ROWS:]).astype(BF)

    part_ref[...] = dot_tn(nm_ref[...], d_hidden_ref[...]).astype(BF).reshape(16, SUB, D)
    at_half = pl.ds(pl.multiple_of(step * SUB, 16), SUB)
    for s in range(8):
        up_keep_ref[s, at_half, :] = part_ref[2 * s + side]
        up_give_ref[s, at_half, :] = part_ref[2 * s + 1 - side]
    part_ref[...] = dot_tn(active_ref[...], g_ref[...]).astype(BF).reshape(16, SUB, D)
    for z in range(2):
        for x in range(2):
            for h in range(2):
                at_h = pl.ds(h * SUB, SUB)
                row = 8 * z + 2 * x + h
                down_keep_ref[z, x, at_h, :] = part_ref[row + 4 * y_at]
                down_give_ref[z, x, at_h, :] = part_ref[row + 4 - 4 * y_at]


def mlp(where, normed, grads, pieces):
    whole = pl.BlockSpec((ROWS, D), lambda i: (0, 0))
    anywhere = pl.BlockSpec(memory_space=pl.ANY)
    return pl.pallas_call(
        mlp_kernel,
        grid=(2,),
        in_specs=[pl.BlockSpec(memory_space=pltpu.SMEM)] + [whole] * 4 + [anywhere] * 8,
        out_specs=[whole] * 4
        + [pl.BlockSpec((8, 2 * SUB, D), lambda i: (0, 0, 0))] * 2
        + [pl.BlockSpec((2, 2, FSUB, D), lambda i: (i, 0, 0, 0))] * 2,
        out_shape=[shape((ROWS, D), BF)] * 4
        + [shape((8, 2 * SUB, D), BF)] * 2
        + [shape((4, 2, FSUB, D), BF)] * 2,
        scratch_shapes=[
            pltpu.VMEM((D, FH), BF),
            pltpu.VMEM((FH, D), BF),
            pltpu.VMEM((2 * ROWS, D), BF),
            pltpu.VMEM((2 * ROWS, D), BF),
            pltpu.VMEM((2 * ROWS, D), F32),
            pltpu.VMEM((2 * ROWS, D), F32),
            pltpu.VMEM((16, SUB, D), BF),
            pltpu.VMEM((2 * ROWS, D), BF),
            pltpu.VMEM((2 * ROWS, D), BF),
            pltpu.SemaphoreType.DMA((48,)),
        ],
        compiler_params=params(),
        cost_estimate=pl.CostEstimate(
            flops=20_000_000_000, bytes_accessed=20_000_000, transcendentals=1_600_000
        ),
    )(where, *normed, *grads, *pieces)


def branch_kernel(
    mid_ref, g_ref, e0_ref, e1_ref, att_ref, w_ref, gcol_ref, dmid_ref, datt_ref, right_ref,
    low_ref,
):
    gain = gain_row(gcol_ref[0])
    wout = w_ref[0]
    gain_sum = jnp.zeros((1, D), F32)
    for chunk in range(4):
        rows = slice(chunk * PR, (chunk + 1) * PR)
        middle = mid_ref[rows, :]
        inv = rms_inv(middle)
        unit = middle * inv
        grad = e0_ref[rows, :].astype(F32) + e1_ref[rows, :].astype(F32)
        scaled = gain * grad
        mean = jnp.mean(unit * scaled, axis=-1, keepdims=True)
        d_mid = g_ref[rows, :].astype(F32) + inv * (scaled - unit * mean)
        dmid_ref[rows, :] = d_mid
        gain_sum = gain_sum + jnp.sum(grad * unit, axis=0, keepdims=True)
        branch = d_mid.astype(BF)
        low_ref[rows, :] = branch
        datt_ref[rows, :] = dot_nt(branch, wout).astype(BF)
    right_ref[:, D:] = sum_column(gain_sum).astype(BF)
    right_ref[:, 0:D] = dot_tn(att_ref[...], low_ref[...]).astype(BF)


def branch(middle, d_out, own, given, attended, w_all):
    return pl.pallas_call(
        branch_kernel,
        grid=(1,),
        in_specs=[pl.BlockSpec((ROWS, D), lambda i: (0, 0))] * 5
        + [
            pl.BlockSpec((1, D, D), lambda i: (1, 0, 1)),
            pl.BlockSpec((1, D, 128), lambda i: (1, 0, HALF // 128)),
        ],
        out_specs=[
            pl.BlockSpec((ROWS, D), lambda i: (0, 0)),
            pl.BlockSpec((ROWS, D), lambda i: (0, 0)),
            pl.BlockSpec((D, RIGHT), lambda i: (0, 0)),
        ],
        out_shape=[shape((ROWS, D), F32), shape((ROWS, D), BF), shape((D, RIGHT), BF)],
        scratch_shapes=[pltpu.VMEM((ROWS, D), BF)],
        compiler_params=params(),
        cost_estimate=pl.CostEstimate(
            flops=2_000_000_000, bytes_accessed=9_000_000, transcendentals=1000
        ),
    )(middle, d_out, own, given, attended, w_all, w_all)


def attn_bwd_kernel(units, *refs):
    first, last = units == (2,), units[0] == 0
    q_ref, g_ref, o_ref, r_ref, *refs = refs
    keyed = []
    for _ in units:
        keyed.append(refs[:3])
        refs = refs[3:]
    if last:
        ec_ref, kc_ref, vc_ref, *refs = refs
    if not first:
        dq_in_ref, *refs = refs
    wk_ref, wv_ref, *refs = refs
    if last:
        where_ref, wq_ref, normed_ref, gcol_ref, kv1_ref, kv2_ref, kv3_ref, *refs = refs
        right_ref, keep_ref, give_ref, dkv_own_ref, dq_own_ref, *refs = refs
        late_in = (wq_ref, wk_ref, wv_ref, normed_ref, right_ref)
        *late, sems_late = refs[:6]
        refs = refs[6:]
        wq_ref, wk_ref, wv_ref, normed_ref, right_ref = late
        dkv_ref, dq_ref, low_ref, high_ref, sems, *refs = refs
    else:
        dkv_refs, refs = refs[: len(units)], refs[len(units) :]
        f_refs, refs = refs[: len(units)], refs[len(units) :]
        dq_ref, *refs = refs
    qs_ref, gs_ref, ds_ref, *refs = refs
    if last:
        sum_ref, near_ref, near_e_ref, near_qs_ref, near_gs_ref = refs
    step = pl.program_id(0)

    def late_copies():
        sources = (
            late_in[0].at[pl.ds(0, 1), :, pl.ds(0, D)],
            late_in[1].at[pl.ds(0, 1), :, pl.ds(D, D)],
            late_in[2].at[pl.ds(1, 1), :, pl.ds(0, D)],
            *late_in[3:],
        )
        return [
            pltpu.make_async_copy(source, target, sems_late.at[at])
            for at, (source, target) in enumerate(zip(sources, late))
        ]

    if last:

        @pl.when(step == 0)
        def _():
            for at, ref in enumerate((kv1_ref, kv2_ref, kv3_ref)):
                rows = pl.ds((at + 1) * UNIT, UNIT)
                pltpu.make_async_copy(ref, dkv_ref.at[:, rows, :], sems.at[at]).start()
            for copy in late_copies():
                copy.start()

    low_half = lane_half(0)
    for pair in range(2):
        lanes = slice(pair * WIDTH, (pair + 1) * WIDTH)
        lanes_v = slice((2 + pair) * WIDTH, (3 + pair) * WIDTH)
        scaled_grad = g_ref[:, lanes].astype(F32) * r_ref[:, lanes]
        prod = scaled_grad * o_ref[:, lanes].astype(F32)
        low_grad = scaled_grad.astype(BF)
        query = q_ref[:, lanes]
        deltas = []
        for head in range(2):
            half = lane_half(head)
            rows = slice(head * ROWS, (head + 1) * ROWS)
            deltas.append(jnp.sum(jnp.where(half, prod, 0.0), axis=-1, keepdims=True))
            gs_ref[rows, :] = jnp.where(half, low_grad, jnp.zeros_like(low_grad))
            qs_ref[rows, :] = jnp.where(half, query, jnp.zeros_like(query))
        delta = jnp.concatenate(deltas, axis=0)
        d_query = None
        for u, (e_ref, k_ref, v_ref) in enumerate(keyed):
            out_ref = dkv_ref if last else dkv_refs[u]
            terms = e_ref[2 * pair : 2 * pair + 2].reshape(2 * ROWS, UNIT)
            d_soft = dot_nt(gs_ref[...], v_ref[:, lanes])
            ds_ref[...] = terms * (d_soft - delta).astype(BF)
            more = dot_nn(ds_ref[...], k_ref[:, lanes])
            d_query = more if d_query is None else d_query + more
            out_ref[step, 0:UNIT, lanes] = dot_tn(ds_ref[...], qs_ref[...]).astype(BF)
            out_ref[step, 0:UNIT, lanes_v] = dot_tn(terms, gs_ref[...]).astype(BF)
        total = jnp.where(low_half, d_query[0:ROWS], d_query[ROWS:])
        if not first:
            total = total + dq_in_ref[:, lanes]
        if not last:
            dq_ref[:, lanes] = total
            continue
        sum_ref[...] = total
        for side in range(2):
            own = slice(side * PR, (side + 1) * PR)
            mine = slice((2 + side) * PR, (3 + side) * PR)
            near_q = []
            for head in range(2):
                rows = slice(head * ROWS + mine.start, head * ROWS + mine.stop)
                at = slice(head * PR, (head + 1) * PR)
                near = ec_ref[2 * pair + head, own, :]
                d_soft = dot_nt(gs_ref[rows, :], vc_ref[own, lanes])
                near_ref[at, :] = near * (d_soft - deltas[head][mine]).astype(BF)
                near_e_ref[at, :] = near
                near_qs_ref[at, :] = qs_ref[rows, :]
                near_gs_ref[at, :] = gs_ref[rows, :]
                near_q.append(dot_nn(near_ref[at, :], kc_ref[own, lanes]))
            sum_ref[mine, :] += jnp.where(low_half, near_q[0], near_q[1])
            rows = slice(PLEN + side * PR, PLEN + (side + 1) * PR)
            dkv_ref[step, rows, lanes] = dot_tn(near_ref[...], near_qs_ref[...]).astype(BF)
            dkv_ref[step, rows, lanes_v] = dot_tn(near_e_ref[...], near_gs_ref[...]).astype(BF)
        dq_ref[step, :, lanes] = (sum_ref[...] * SCALE).astype(BF)

    def back_to_rows(dkv, rows):
        grad = None
        for i in range(3):
            at = slice(i * UNIT, (i + 1) * UNIT)
            more = dot_nt(dkv[i, rows, 0:UNIT], wk_ref[0, :, at])
            more = more + dot_nt(dkv[i, rows, UNIT:], wv_ref[0, :, at])
            grad = more if grad is None else grad + more
        return grad

    @pl.when(step == pl.num_programs(0) - 1)
    def _():
        if not last:
            for dkv, f_ref in zip(dkv_refs, f_refs):
                f_ref[...] = back_to_rows(dkv, slice(0, UNIT)).astype(BF)
            return
        for at, ref in enumerate((kv1_ref, kv2_ref, kv3_ref)):
            rows = pl.ds((at + 1) * UNIT, UNIT)
            pltpu.make_async_copy(ref, dkv_ref.at[:, rows, :], sems.at[at]).wait()
        for copy in late_copies():
            copy.wait()
        high_ref[:, D:] = right_ref[...]
        own = [
            pltpu.make_async_copy(
                dkv_ref.at[:, pl.ds(start, UNIT), :],
                dkv_own_ref.at[:, pl.ds(at * UNIT, UNIT), :],
                sems.at[at],
            )
            for at, start in enumerate((0, PLEN))
        ]
        own.append(pltpu.make_async_copy(dq_ref, dq_own_ref, sems.at[2]))
        for copy in own:
            copy.start()
        rows_sum = jnp.zeros((D, 1), F32)
        for i in range(3):
            at = slice(i * UNIT, (i + 1) * UNIT)
            d_wq = dot_tn(normed_ref[0:UNIT, :], dq_ref[i, 0:UNIT, :]) + dot_tn(
                normed_ref[PLEN:, :], dq_ref[i, UNIT:, :]
            )
            both = dot_tn(normed_ref[...], dkv_ref[i])
            for grad, w_ref in ((d_wq, wq_ref), (both[:, 0:UNIT], wk_ref), (both[:, UNIT:], wv_ref)):
                product = grad * w_ref[0, :, at].astype(F32)
                rows_sum = rows_sum + jnp.sum(product, axis=-1, keepdims=True)
            low_ref[:, at] = d_wq.astype(BF)
            low_ref[:, D + i * UNIT : D + (i + 1) * UNIT] = both[:, 0:UNIT].astype(BF)
            high_ref[:, at] = both[:, UNIT:].astype(BF)
        low_ref[:, HALF:] = (rows_sum / gcol_ref[0].astype(F32)).astype(BF)
        for copy in own:
            copy.wait()

        for core, low_out, high_out in ((0, keep_ref, give_ref), (1, give_ref, keep_ref)):

            @pl.when(where_ref[2] == core)
            def _():
                copies = [
                    pltpu.make_async_copy(low_ref, low_out, sems.at[3]),
                    pltpu.make_async_copy(high_ref, high_out, sems.at[4]),
                ]
                for copy in copies:
                    copy.start()
                for copy in copies:
                    copy.wait()


def attn_bwd(units, saved, d_att, w_all, dq=None, rest=None):
    first, last = units == (2,), units[0] == 0
    q, k, v, e, ec, o, r = saved
    width = 2 * WIDTH
    lanes = lambda i: (0, i)
    full = lambda *dims: pl.BlockSpec(dims, lambda i: (0,) * len(dims))
    rows = pl.BlockSpec((ROWS, width), lanes)
    anywhere = pl.BlockSpec(memory_space=pl.ANY)
    weight = lambda half, at: pl.BlockSpec((1, D, D), lambda i: (half, 0, at))
    specs, args = [rows] * 4, [q, d_att, o, r]
    for u in units:
        specs += [
            pl.BlockSpec((4, ROWS, UNIT), lambda i, u=u: (i, 0, u)),
            pl.BlockSpec((UNIT, width), lambda i, u=u: (u, i)),
            pl.BlockSpec((UNIT, width), lambda i, u=u: (u, i)),
        ]
        args += [e, k, v]
    if last:
        specs += [
            pl.BlockSpec((4, UNIT, PR), lambda i: (i, 0, 0)),
            pl.BlockSpec((UNIT, width), lambda i: (4, i)),
            pl.BlockSpec((UNIT, width), lambda i: (4, i)),
        ]
        args += [ec, k, v]
    if not first:
        specs.append(rows)
        args.append(dq)
    specs += [anywhere, anywhere] if last else [weight(0, 1), weight(1, 0)]
    args += [w_all, w_all]
    kv = (3, UNIT, 2 * UNIT)
    if last:
        where, normed, kvs, right = rest
        specs += [pl.BlockSpec(memory_space=pltpu.SMEM)] + [anywhere] * 2
        specs += [pl.BlockSpec((1, D, 128), lambda i: (0, 0, HALF // 128))] + [anywhere] * 4
        args += [where, w_all, normed, w_all, *kvs, right]
        outs = [anywhere] * 4
        out_shapes = [shape((D, WIDE), BF)] * 2
        out_shapes += [shape((3, ROWS, 2 * UNIT), BF), shape((3, ROWS, UNIT), BF)]
        scratch = [
            pltpu.VMEM((1, D, D), BF),
            pltpu.VMEM((1, D, D), BF),
            pltpu.VMEM((1, D, D), BF),
            pltpu.VMEM((KEYS, D), BF),
            pltpu.VMEM((D, RIGHT), BF),
            pltpu.SemaphoreType.DMA((5,)),
            pltpu.VMEM((3, KEYS, 2 * UNIT), BF),
            pltpu.VMEM((3, ROWS, UNIT), BF),
            pltpu.VMEM((D, WIDE), BF),
            pltpu.VMEM((D, WIDE), BF),
            pltpu.SemaphoreType.DMA((5,)),
        ]
    else:
        outs = [full(*kv)] * len(units) + [full(UNIT, D)] * len(units) + [rows]
        out_shapes = [shape(kv, BF)] * len(units) + [shape((UNIT, D), BF)] * len(units)
        out_shapes.append(shape((ROWS, D), F32))
        scratch = []
    return pl.pallas_call(
        lambda *refs: attn_bwd_kernel(units, *refs),
        grid=(3,),
        in_specs=specs,
        out_specs=outs,
        out_shape=out_shapes,
        scratch_shapes=scratch
        + [
            pltpu.VMEM((2 * ROWS, WIDTH), BF),
            pltpu.VMEM((2 * ROWS, WIDTH), BF),
            pltpu.VMEM((2 * ROWS, UNIT), BF),
        ]
        + ([pltpu.VMEM((ROWS, WIDTH), F32)] + [pltpu.VMEM((UNIT, WIDTH), BF)] * 4 if last else []),
        compiler_params=params(),
        cost_estimate=pl.CostEstimate(
            flops=10_000_000_000 * (len(units) + last), bytes_accessed=10_000_000, transcendentals=1000
        ),
    )(*args)


def tail_kernel(
    near_ref, cont_ref, dkv_ref, dq_ref, wq_ref, wk_ref, wv_ref, f1_ref, f3_ref, dmid_ref, gcol_ref,
    keep_ref, give_ref,
):
    gain = gain_row(gcol_ref[0])
    for half, x_ref in enumerate((near_ref, cont_ref)):
        rows = slice(half * UNIT, (half + 1) * UNIT)
        grad = None
        for i in range(3):
            at = slice(i * UNIT, (i + 1) * UNIT)
            more = dot_nt(dkv_ref[i, rows, 0:UNIT], wk_ref[0, :, at])
            more = more + dot_nt(dkv_ref[i, rows, UNIT:], wv_ref[0, :, at])
            more = more + dot_nt(dq_ref[i, rows, :], wq_ref[0, :, at])
            grad = more if grad is None else grad + more
        if half == 0:
            grad = grad + f1_ref[...].astype(F32) + f3_ref[...].astype(F32)
        part = x_ref[...].astype(F32)
        inv = rms_inv(part)
        unit = part * inv
        scaled = gain * grad
        mean = jnp.mean(unit * scaled, axis=-1, keepdims=True)
        d_rows = dmid_ref[rows, :] + inv * (scaled - unit * mean)
        at = slice(half * PR, (half + 1) * PR)
        keep_ref[at, :] = d_rows[0:PR]
        give_ref[at, :] = d_rows[PR:].astype(BF)


def tail(near, cont, own, f_parts, d_mid, w_all):
    full = lambda *dims: pl.BlockSpec(dims, lambda i: (0,) * len(dims))
    weight = lambda half, at: pl.BlockSpec((1, D, D), lambda i: (half, 0, at))
    half = full(UNIT, D)
    return pl.pallas_call(
        tail_kernel,
        grid=(1,),
        in_specs=[half, half, full(3, ROWS, 2 * UNIT), full(3, ROWS, UNIT)]
        + [weight(0, 0), weight(0, 1), weight(1, 0), half, half, full(ROWS, D)]
        + [pl.BlockSpec((1, D, 128), lambda i: (0, 0, HALF // 128))],
        out_specs=[half, half],
        out_shape=[shape((UNIT, D), F32), shape((UNIT, D), BF)],
        compiler_params=params(),
        cost_estimate=pl.CostEstimate(flops=20_000_000, bytes_accessed=7_000_000, transcendentals=1000),
    )(near, cont, *own, w_all, w_all, w_all, *f_parts, d_mid, w_all)


def total_of(*parts):
    total = parts[0].astype(F32)
    for part in parts[1:]:
        total = total + part.astype(F32)
    return total.astype(BF)


def run_whole(kernel, outs, *args, dtype=BF):
    return pl.pallas_call(
        kernel,
        in_specs=[pl.BlockSpec(memory_space=pltpu.SMEM)]
        + [pl.BlockSpec(memory_space=pltpu.VMEM)] * (len(args) - 1),
        out_specs=[pl.BlockSpec(memory_space=pltpu.VMEM)] * len(outs),
        out_shape=[shape(dims, dtype) for dims in outs],
        compiler_params=params(),
        cost_estimate=pl.CostEstimate(flops=1_000_000, bytes_accessed=7_000_000, transcendentals=0),
    )(*args)


def fold_two_kernel(where_ref, a0_ref, a1_ref, b0_ref, b1_ref, ak_ref, ag_ref, bk_ref, bg_ref):
    y_at, side = where_ref[0] % 2, where_ref[1]
    ak_ref[0] = total_of(a0_ref[0, y_at], a1_ref[0, y_at])
    ag_ref[0] = total_of(a0_ref[0, 1 - y_at], a1_ref[0, 1 - y_at])
    bk_ref[0] = total_of(b0_ref[0, side], b1_ref[0, side])
    bg_ref[0] = total_of(b0_ref[0, 1 - side], b1_ref[0, 1 - side])


def fold_more_kernel(
    where_ref, a0_ref, a1_ref, b0_ref, b1_ref, c0_ref, c1_ref, ak_ref, ag_ref, bk_ref, bg_ref, c_ref
):
    fold_two_kernel(
        where_ref, a0_ref, a1_ref, b0_ref, b1_ref, ak_ref, ag_ref, bk_ref, bg_ref
    )
    c_ref[...] = total_of(c0_ref[...], c1_ref[...])


def run_by_z(kernel, outs, *args):
    def spec(dims):
        block = (dims[0] // 4, *dims[1:])
        return pl.BlockSpec(block, lambda z: (z,) + (0,) * (len(dims) - 1))

    return pl.pallas_call(
        kernel,
        grid=(4,),
        in_specs=[pl.BlockSpec(memory_space=pltpu.SMEM)] + [spec(arg.shape) for arg in args[1:]],
        out_specs=[spec(dims) for dims in outs],
        out_shape=[shape(dims, BF) for dims in outs],
        compiler_params=params(),
        cost_estimate=pl.CostEstimate(flops=1_000_000, bytes_accessed=7_000_000, transcendentals=0),
    )(*args)


def fold_halves_kernel(where_ref, a0_ref, a1_ref, b0_ref, b1_ref, *outs):
    for z in range(4):
        at = slice(z, z + 1)
        fold_two_kernel(
            where_ref, *[ref.at[at] for ref in (a0_ref, a1_ref, b0_ref, b1_ref, *outs)]
        )


def fold_rows_kernel(where_ref, a0_ref, a1_ref, b0_ref, b1_ref, *outs):
    z_at = where_ref[0] // 2
    rows = a0_ref.shape[1]
    for step, out_ref in enumerate(outs):
        z = jnp.bitwise_xor(z_at, step)
        out_ref[0:rows, :] = total_of(a0_ref[z], a1_ref[z])
        out_ref[rows:, :] = total_of(b0_ref[z], b1_ref[z])


def fold_cols_kernel(where_ref, a0_ref, a1_ref, b0_ref, b1_ref, *outs):
    z_at = where_ref[0] // 2
    cols = a0_ref.shape[2]
    for step, out_ref in enumerate(outs):
        z = jnp.bitwise_xor(z_at, step)
        out_ref[:, 0:cols] = total_of(a0_ref[z], a1_ref[z])
        out_ref[:, cols:] = total_of(b0_ref[z], b1_ref[z])


def fold_core_kernel(where_ref, own_ref, got_ref, ak_ref, ag_ref, bk_ref, bg_ref):
    y_at, side = where_ref[0] % 2, where_ref[1]
    left, right = slice(0, LEFT), slice(LEFT, WIDE)

    def block(y, x, cols):
        rows = pl.ds(pl.multiple_of((2 * y + x) * SUB, 16), SUB)
        return total_of(own_ref[rows, cols], got_ref[rows, cols])

    for at in range(2):
        ak_ref[0, at] = block(at, side, left)
        ag_ref[0, at] = block(at, 1 - side, left)
        bk_ref[0, at] = block(y_at, at, right)
        bg_ref[0, at] = block(1 - y_at, at, right)


def take_kernel(where_ref, qkv_ref, out_ref, gain_a_ref, gain_m_ref, piece_ref):
    rows = pl.ds(pl.multiple_of(where_ref[1] * SUB, 16), SUB)
    for core, gain_ref in ((0, gain_a_ref), (1, gain_m_ref)):

        @pl.when(where_ref[2] == core)
        def _():
            if core == 0:
                piece_ref[:, 0:HALF] = qkv_ref[rows, 0:HALF]
            else:
                piece_ref[:, 0:D] = qkv_ref[rows, HALF:]
                piece_ref[:, D:HALF] = out_ref[rows, :]
            wide = jnp.broadcast_to(gain_ref[...].astype(F32), (128, 2 * SUB)).T
            piece_ref[:, HALF:] = jnp.where(where_ref[1] == 0, wide[0:SUB], wide[SUB:]).astype(BF)


def split_cols_kernel(where_ref, a0_ref, a1_ref, a2_ref, a3_ref, left_ref, right_ref):
    for at, ref in enumerate((a0_ref, a1_ref, a2_ref, a3_ref)):
        left_ref[at] = ref[:, 0:LEFT]
        right_ref[at] = ref[:, LEFT:]


def join_kernel(where_ref, a0_ref, a1_ref, b0_ref, b1_ref, left_ref, right_ref):
    for out_ref, parts in ((left_ref, (a0_ref, a1_ref)), (right_ref, (b0_ref, b1_ref))):
        out_ref[0:4] = parts[0][...]
        out_ref[4:8] = parts[1][...]


def split_rows_kernel(where_ref, m0_ref, m1_ref, m2_ref, m3_ref, up_ref, down_ref):
    for at, ref in enumerate((m0_ref, m1_ref, m2_ref, m3_ref)):
        up_ref[at] = ref[0 : 2 * SUB, :]
        down_ref[at] = ref[2 * SUB :, :]


def unpack_kernel(where_ref, here_ref, far_ref, up_ref, down_ref):
    side, core = where_ref[1], where_ref[2]
    first = core == 0
    for x in range(2):
        at = jnp.bitwise_xor(side, x)
        rows = slice(x * SUB, (x + 1) * SUB)
        here, far = here_ref[at].astype(F32), far_ref[at].astype(F32)
        low, high = jnp.where(first, here, far), jnp.where(first, far, here)
        down_ref[x * FSUB : (x + 1) * FSUB, :] = low[2 * SUB :]
        down_ref[(2 + x) * FSUB : (3 + x) * FSUB, :] = high[2 * SUB :]
        for half in range(2):
            own = slice(half * SUB, (half + 1) * SUB)
            for i in range(4):
                cols = slice(i * 2 * FSUB, (i + 1) * 2 * FSUB)
                start = (half * 4 + i) * 4 * FSUB
                up_ref[rows, start : start + 4 * FSUB] = jnp.concatenate(
                    [low[own, cols], high[own, cols]], axis=1
                )


def finish_kernel(
    where_ref, own_ref, side_ref, core_ref, far_ref, qkv_ref, out_ref, gain_a_ref, gain_m_ref
):
    first, near = where_ref[2] == 0, where_ref[1] == 0
    columns = []
    for x in range(2):
        mine = jnp.where(near == (x == 0), own_ref[...], side_ref[...]).astype(F32)
        theirs = jnp.where(near == (x == 0), core_ref[...], far_ref[...]).astype(F32)
        low, high = jnp.where(first, mine, theirs), jnp.where(first, theirs, mine)
        rows = slice(x * SUB, (x + 1) * SUB)
        qkv_ref[rows, 0:HALF] = low[:, 0:HALF]
        qkv_ref[rows, HALF:] = high[:, 0:D]
        out_ref[rows, :] = high[:, D:HALF]
        columns.append((low[:, HALF:], high[:, HALF:]))
    for at, gain_ref in enumerate((gain_a_ref, gain_m_ref)):
        both = jnp.concatenate([columns[0][at], columns[1][at]], axis=0)
        gain_ref[...] = both.T[0:1, :]


def over(axis, value, bits):
    return lax.ppermute(value, axis, [(i, i ^ bits) for i in range(lax.axis_size(axis))])


def cut(values, start, rows=PR):
    return lax.dynamic_slice_in_dim(values, start, rows, 0)


def pick(values, at):
    return lax.dynamic_index_in_dim(values, at, 0, keepdims=False)


def pick_of(values, at, axis):
    return lax.dynamic_index_in_dim(values, at, axis, keepdims=False)


def tie(*values):
    return lax.optimization_barrier(values)


def per_device(tokens, w_qkv, w_out, w_up, w_down, gain_attn, gain_mlp, d_out):
    staged = lax.axis_size("shard") == 8
    shard = lax.axis_index("shard")
    rep = lax.axis_index("rep")
    side, core = rep // 2, rep % 2
    pos = shard % 8
    y_at, z_at = pos % 2, pos // 2
    table = [pos ^ d for d in ORDER] if staged else [jnp.int32(2 * (d % 4) + d // 4) for d in range(8)]
    where = jnp.stack([pos, side, core] + [jnp.int32(0)] * 5 + table).astype(jnp.int32)

    def to_give(values):
        return jnp.concatenate([cut(values, (1 - y_at) * PR), cut(values, (3 - y_at) * PR)], axis=0)

    def own_parts(values, got):
        mine_p, mine_c = cut(values, y_at * PR), cut(values, (2 + y_at) * PR)
        return (
            jnp.concatenate([mine_p, got[:PR]], axis=0), jnp.concatenate([mine_c, got[PR:]], axis=0)
        )

    def to_return(values):
        return jnp.concatenate([values[PR : 2 * PR], values[3 * PR :]], axis=0)

    def home_rows(keep_p, keep_c, got):
        got = got.astype(keep_p.dtype)
        first = y_at == 0
        return jnp.concatenate(
            [
                jnp.where(first, keep_p, got[:PR]),
                jnp.where(first, got[:PR], keep_p),
                jnp.where(first, keep_c, got[PR:]),
                jnp.where(first, got[PR:], keep_c),
            ],
            axis=0,
        )

    def wide(gain):
        return jnp.broadcast_to(gain[:, None], (gain.shape[0], 128))

    def halves(qkv, out, gain_a, gain_m):
        return (
            jnp.concatenate([qkv[:, :HALF], wide(gain_a)], axis=1),
            jnp.concatenate([qkv[:, HALF:], out, wide(gain_m)], axis=1),
        )

    def half_up(up):
        return pick_of(up.reshape(up.shape[0], 8, 2, 2 * FSUB), core, 2).reshape(up.shape[0], FH)

    def own_up(up):
        mine = half_up(cut(up, side * SUB, SUB))
        return jnp.concatenate([mine[:, :D], mine[:, D:]], axis=0)

    if staged:
        (own_piece,) = run_whole(
            take_kernel, [(SUB, WIDE)], where, w_qkv, w_out,
            gain_attn.reshape(1, 2 * SUB), gain_mlp.reshape(1, 2 * SUB),
        )
        own_mlp = jnp.concatenate(
            [own_up(w_up), cut(w_down, core * 2 * FSUB + side * FSUB, FSUB)], axis=0
        )
        t_got, z1, z2, z3 = tie(
            over("shard", to_give(tokens), 1),
            *[over("shard", own_piece, k) for k in (2, 4, 6)],
        )
        near, cont = own_parts(tokens, t_got)
        left, right = run_whole(
            split_cols_kernel, [(4, SUB, LEFT), (4, SUB, WIDE - LEFT)], where, own_piece, z1, z2, z3
        )
        own_mlp, near, left, right = tie(own_mlp, near, left, right)
        m1, m3, left_y, right_x, g_got = tie(
            over("shard", own_mlp, 2),
            over("shard", own_mlp, 6),
            over("shard", left, 1),
            over("rep", right, 2),
            over("shard", to_give(d_out), 1),
        )
        left, right = run_whole(
            join_kernel, [(8, SUB, LEFT), (8, SUB, WIDE - LEFT)], where, left, left_y, right, right_x
        )
        m3, near, left, right = tie(m3, near, left, right)
        m2, near3, left_x, right_y, left_core, right_core = tie(
            over("shard", m3, 2),
            over("shard", near, 6),
            over("rep", left, 2),
            over("shard", right, 1),
            over("rep", left, 1),
            over("rep", right, 1),
        )
        up, down = run_whole(
            split_rows_kernel, [(4, 2 * SUB, D), (4, FSUB, D)], where, own_mlp, m1, m2, m3
        )
        near, near3, left_x, right_y, up, down = tie(near, near3, left_x, right_y, up, down)
        near1, near2, up_y, down_x, left_far, right_far = tie(
            over("shard", near, 2),
            over("shard", near3, 2),
            over("shard", up, 1),
            over("rep", down, 2),
            over("rep", left_x, 1),
            over("rep", right_y, 1),
        )
        pieces = (left, left_x, left_core, left_far, right, right_y, right_core, right_far)
        up, up_y, down, down_x, pieces = tie(up, up_y, down, down_x, pieces)
        mlp_pieces = (
            up, over("rep", up, 2), up_y, over("rep", up_y, 2),
            down, down_x, over("shard", down, 1), over("shard", down_x, 1),
        )
    else:
        gathered = [
            lax.all_gather(w, "shard", axis=0, tiled=True)
            for w in (w_qkv, w_out, gain_attn, gain_mlp, w_up, w_down)
        ]
        natural = jnp.stack(halves(*gathered[:4])).reshape(2, 4, 2, 2, SUB, WIDE)
        pieces = []
        for dc in (0, 1):
            by_core = pick(natural, core ^ dc)
            for dx in (0, 1):
                both = pick_of(by_core[..., :LEFT], side ^ dx, 2)
                pieces.append(jnp.concatenate([both[:, 0], both[:, 1]], axis=0))
        for dc in (0, 1):
            by_core = pick(natural, core ^ dc)[..., LEFT:]
            for dy in (0, 1):
                both = [pick_of(by_core[:, dy], side ^ dx, 1) for dx in (0, 1)]
                pieces.append(jnp.concatenate(both, axis=0))
        pieces = tuple(pieces)
        up = half_up(gathered[4]).reshape(4, 2, 2, SUB, 2, D).transpose(1, 0, 2, 4, 3, 5)
        up = up.reshape(2, 4, 2, 2 * SUB, D)
        down = pick_of(gathered[5].reshape(4, 2, 2, 2, FSUB, D), core, 2).transpose(1, 0, 2, 3, 4)
        mlp_pieces = tuple(
            pick_of(both[dy], side ^ dx, 1) for both in (up, down) for dy in (0, 1) for dx in (0, 1)
        )
        near, cont = own_parts(tokens, over("shard", to_give(tokens), 1))
        near1, near2, near3 = [over("shard", near, k) for k in (2, 4, 6)]
        g_got = over("shard", to_give(d_out), 1)
    parts = (near, near1, near2, near3, cont)
    g_own = jnp.concatenate(own_parts(d_out, g_got), axis=0)
    parts, g_own = tie(parts, g_own)

    g_core = over("rep", g_own, 1)
    forward = attn_fwd(where, parts, pieces)
    forward, mlp_pieces, g_core = tie(forward, mlp_pieces, g_core)
    w_all, q, k, v, e, ec, attended, inv_sum, middle, nm, normed = forward

    nm_core, nm = tie(over("rep", nm, 1), nm)
    e_own, y_own, e_give, y_give, *mlp_grads = mlp(
        where, (nm, nm_core), (g_own, g_core), mlp_pieces
    )
    e_got, y_give, mlp_grads = tie(over("rep", e_give, 1), y_give, mlp_grads)
    up_keep, up_give, down_keep, down_give = mlp_grads
    y_got = over("rep", y_give, 1)
    if staged:
        up_got, down_got = over("rep", up_give, 2), over("shard", down_give, 1)
    d_mid, d_att, d_right = branch(middle, g_own, e_own, e_got, attended, w_all)

    saved = (q, k, v, e, ec, attended, inv_sum)
    kv2, f2_give, dq = attn_bwd((2,), saved, d_att, w_all)
    f2_give, dq = tie(f2_give, dq)
    f2_got = over("shard", f2_give, 2)
    kv3, kv1, f3_give, f1_give, dq = attn_bwd((3, 1), saved, d_att, w_all, dq)
    f2_got, f3_give, f1_give, dq, y_got = tie(f2_got, f3_give, f1_give, dq, y_got)
    if staged:
        up_got, down_got, dq = tie(up_got, down_got, dq)
        by_pair = (4, 2, 2 * SUB, D)
        f3_send = total_of(f3_give, f2_got)
        folded = run_by_z(
            fold_two_kernel, [(4, 2 * SUB, D)] * 4, where,
            up_keep.reshape(by_pair), up_got.reshape(by_pair), down_keep, down_got,
        )
        (up_keep, up_give, down_keep, down_give), dq, f3_send, f1_give = tie(
            folded, dq, f3_send, f1_give
        )
        up_got, down_got = over("shard", up_give, 1), over("rep", down_give, 2)
    else:
        f3_send = total_of(f3_give, f2_got)
    f1, f3 = over("shard", f1_give, 2), over("shard", f3_send, 6)
    keep, give, *own = attn_bwd(
        (0,), saved, d_att, w_all, dq, (where, normed, (kv1, kv2, kv3), d_right)
    )
    f1, f3, keep, give, own = tie(f1, f3, keep, give, own)

    def block_of(got):
        return (middle + y_own.astype(F32) + got.astype(F32)).astype(BF)

    if staged:
        up_got, down_got, give = tie(up_got, down_got, give)
        mlp_total, *mlp_gives = run_whole(
            fold_rows_kernel, [(4 * SUB, D)] * 4, where, up_keep, up_got, down_keep, down_got
        )
        chip_got, mlp_gives = tie(over("rep", give, 1), mlp_gives)
        m2 = over("shard", mlp_gives[1], 2)
        left, right = (4, 2, SUB, LEFT), (4, 2, SUB, WIDE - LEFT)
        left_keep, left_give, right_keep, right_give = run_by_z(
            fold_core_kernel, [left, left, right, right], where, keep, chip_got
        )
        left_give, right_give, m2, mlp_gives, own, y_got = tie(
            left_give, right_give, m2, mlp_gives, own, y_got
        )
        block_rows = block_of(y_got)
        m1_send, m3_send = mlp_gives[0], total_of(mlp_gives[2], m2)
        left_got, right_got, m1, m3, block_rows, block_give, token_keep, token_give = tie(
            over("rep", left_give, 2),
            over("shard", right_give, 1),
            over("shard", m1_send, 2),
            over("shard", m3_send, 6),
            block_rows,
            to_return(block_rows),
            *tail(near, cont, own, (f1, f3), d_mid, w_all),
        )
        mlp_total = total_of(mlp_total, m1, m3)
        left_keep, left_give, right_keep, right_give = run_whole(
            fold_halves_kernel,
            [(4, SUB, LEFT)] * 2 + [(4, SUB, WIDE - LEFT)] * 2,
            where, left_keep, left_got, right_keep, right_got,
        )
        left_got, right_got, mlp_total = tie(
            over("shard", left_give, 1), over("rep", right_give, 2), mlp_total
        )
        total, *gives = run_whole(
            fold_cols_kernel, [(SUB, WIDE)] * 4, where, left_keep, left_got, right_keep, right_got
        )
        z1, z2, z3, m_got, mlp_total, t_got = tie(
            *[over("shard", gives[step - 1], 2 * step) for step in (1, 2, 3)],
            over("rep", mlp_total, 2),
            mlp_total,
            over("shard", token_give, 1),
        )
        by_side = jnp.stack([mlp_total, m_got])
        total = total_of(total, z1, z2, z3)
        b_got = over("shard", block_give, 1)
        other, core_got, m_got, by_side = tie(
            over("rep", total, 2), over("rep", total, 1), over("rep", by_side, 1), by_side
        )
        far = over("rep", other, 1)
        d_wup, d_wdown = run_whole(
            unpack_kernel, [(2 * SUB, FF), (4 * FSUB, D)], where, by_side, m_got, dtype=F32
        )
        d_wqkv, d_wout, d_gain_attn, d_gain_mlp = run_whole(
            finish_kernel, [(2 * SUB, 3 * D), (2 * SUB, D), (1, 2 * SUB), (1, 2 * SUB)],
            where, total, other, core_got, far, dtype=F32,
        )
        d_gain_attn, d_gain_mlp = d_gain_attn.reshape(2 * SUB), d_gain_mlp.reshape(2 * SUB)
    else:
        block_rows = block_of(y_got)
        b_got = over("shard", to_return(block_rows), 1)
        token_keep, token_give = tail(near, cont, own, (f1, f3), d_mid, w_all)
        t_got = over("shard", token_give, 1)
        low, high = jnp.where(core == 0, keep, give), jnp.where(core == 0, give, keep)

        def by_side_of(keep, give, at):
            first = at == 0
            return jnp.stack([jnp.where(first, keep, give), jnp.where(first, give, keep)])

        up = by_side_of(up_keep, up_give, side).reshape(2, 8, 2, SUB, D)
        up = up.transpose(1, 0, 3, 2, 4).reshape(D, 8, 1, 2 * FSUB)
        down = by_side_of(down_keep, down_give, y_at).transpose(1, 0, 2, 3, 4)
        down = down.reshape(8, 1, 2 * FSUB, D)
        peer_up, peer_down = over("rep", up, 1), over("rep", down, 1)
        first = core == 0
        up, peer_up = jnp.where(first, up, peer_up), jnp.where(first, peer_up, up)
        down, peer_down = jnp.where(first, down, peer_down), jnp.where(first, peer_down, down)
        up = jnp.concatenate([up, peer_up], axis=2).reshape(D, FF)
        down = jnp.concatenate([down, peer_down], axis=1).reshape(FF, D)
        rest = lambda v: (v.astype(F32) + over("rep", v, 2).astype(F32)).astype(BF)
        up, down = rest(up), rest(down)
        scatter = lambda v: lax.psum_scatter(v, "shard", scatter_dimension=0, tiled=True)
        d_wup, d_wdown = scatter(up).astype(F32), scatter(down).astype(F32)
        low = lax.psum(scatter(low), "rep").astype(F32)
        high = lax.psum(scatter(high), "rep").astype(F32)
        d_wqkv = jnp.concatenate([low[:, :HALF], high[:, :D]], axis=1)
        d_wout, d_gain_attn, d_gain_mlp = high[:, D:HALF], low[:, HALF], high[:, HALF]

    return (
        home_rows(block_rows[:PR], block_rows[2 * PR : 3 * PR], b_got),
        home_rows(token_keep[:PR], token_keep[PR:], t_got),
        d_wqkv,
        d_wout,
        d_wup,
        d_wdown,
        d_gain_attn,
        d_gain_mlp,
    )


def solution(mesh):
    weights = P("shard", None)
    rows = P(("rep", "shard"), None)
    return jax.shard_map(
        per_device,
        mesh=mesh,
        in_specs=(rows, weights, weights, weights, weights, P("shard"), P("shard"), rows),
        out_specs=(rows, rows, weights, weights, weights, weights, P("shard"), P("shard")),
        check_vma=False,
    )
```
